32 devices in a mesh: dp: 8 (over z, y), seq: 4 (over x, core).
Axes of the slice: x: 2, y: 2, z: 4, core: 2. Of those that a mesh axis runs over, the one named last changes fastest.
Arguments:
- token_ids: int32 [8192], replicated, may hold values from 0 to 50687
- targets: int32 [8192], P('dp'), may hold values from 0 to 50687
- loss_mask: int32 [8192], P('dp'), may hold values from 0 to 1
- square_weights: float32 [2, 5, 768, 768], P(None, None, ('dp', 'seq')), may hold values from -0.21875 to 0.21875
- expand_weights: float32 [2, 768, 3072], P(None, ('dp', 'seq')), may hold values from -0.21875 to 0.21875
- shrink_weights: float32 [2, 3072, 768], P(None, ('dp', 'seq')), may hold values from -0.109375 to 0.109375
- vector_params: float32 [26, 768], P(None, ('dp', 'seq')), as said below
- embed_table: float32 [768, 50688], P(('dp', 'seq')), may hold values from -6 to 6
- head_table: float32 [768, 50688], P('dp', 'seq')
- square_first: float32 [2, 5, 768, 768], P(None, None, ('dp', 'seq')), may hold values from -3.5762787e-07 to 3.5762787e-07
- expand_first: float32 [2, 768, 3072], P(None, ('dp', 'seq')), may hold values from -3.5762787e-07 to 3.5762787e-07
- shrink_first: float32 [2, 3072, 768], P(None, ('dp', 'seq')), may hold values from -3.5762787e-07 to 3.5762787e-07
- vector_first: float32 [26, 768], P(None, ('dp', 'seq')), may hold values from -1.4305115e-06 to 1.4305115e-06
- embed_first: float32 [768, 50688], P(('dp', 'seq')), may hold values from -1.8626451e-08 to 1.8626451e-08
- head_first: float32 [768, 50688], P('dp', 'seq'), may hold values from -3.5762787e-07 to 3.5762787e-07
- square_second: float32 [2, 5, 768, 768], P(None, None, ('dp', 'seq')), may hold values from 1.6369956e-16 to 2.619193e-15
- expand_second: float32 [2, 768, 3072], P(None, ('dp', 'seq')), may hold values from 1.6369956e-16 to 2.619193e-15
- shrink_second: float32 [2, 3072, 768], P(None, ('dp', 'seq')), may hold values from 1.6369956e-16 to 2.619193e-15
- vector_second: float32 [26, 768], P(None, ('dp', 'seq')), may hold values from 2.619193e-15 to 4.1907087e-14
- embed_second: float32 [768, 50688], P(('dp', 'seq')), may hold values from 8.184978e-18 to 1.3095964e-16
- head_second: float32 [768, 50688], P('dp', 'seq'), may hold values from 1.6369956e-16 to 2.619193e-15
Outputs:
- loss_sum: float32 [], replicated
- grad_norm: float32 [], replicated
- square_out: float32 [2, 5, 768, 768], P(None, None, ('dp', 'seq'))
- expand_out: float32 [2, 768, 3072], P(None, ('dp', 'seq'))
- shrink_out: float32 [2, 3072, 768], P(None, ('dp', 'seq'))
- vector_out: float32 [26, 768], P(None, ('dp', 'seq'))
- embed_out: float32 [768, 50688], P(('dp', 'seq'))
- head_out: float32 [768, 50688], P('dp', 'seq')
- square_first_out: float32 [2, 5, 768, 768], P(None, None, ('dp', 'seq'))
- expand_first_out: float32 [2, 768, 3072], P(None, ('dp', 'seq'))
- shrink_first_out: float32 [2, 3072, 768], P(None, ('dp', 'seq'))
- vector_first_out: float32 [26, 768], P(None, ('dp', 'seq'))
- embed_first_out: float32 [768, 50688], P(('dp', 'seq'))
- head_first_out: float32 [768, 50688], P('dp', 'seq')
- square_second_out: float32 [2, 5, 768, 768], P(None, None, ('dp', 'seq'))
- expand_second_out: float32 [2, 768, 3072], P(None, ('dp', 'seq'))
- shrink_second_out: float32 [2, 3072, 768], P(None, ('dp', 'seq'))
- vector_second_out: float32 [26, 768], P(None, ('dp', 'seq'))
- embed_second_out: float32 [768, 50688], P(('dp', 'seq'))
- head_second_out: float32 [768, 50688], P('dp', 'seq')
The draws below stay inside these ranges and needn't reach their ends.
Inputs may be any that keep to these rules, and one draw needn't show every extreme that they name: `vector_params`: time decays lie between log(0.25 / 1024) and log(1 / 24); mixing shares between 0.1 and 0.9.
All inputs are finite; a program needn't handle non-finite values.
Results may differ from the reference program's by a relative error of at most 0.018.
Values may be sent and summed in bfloat16 or wider, within the bound.
A program may use at most 448 MiB of HBM per device.

```python
import math
import jax
import jax.numpy as jnp
import numpy as np
from jax import lax

D = 768
FF = 3072
V = 50688
LAYERS = 2
STEP = 10
LEN = 1024
SEQS = 8
TOKENS = 8192
VROWS = 26
PARAMS = 93212160


def draw_loss_mask(key, part):
    key = jax.random.fold_in(key, 47)
    seq_rank = jnp.arange(SEQS, dtype=jnp.int32)[:, None]
    position = jnp.arange(LEN, dtype=jnp.int32)[None, :]
    threshold = 95 * (SEQS - 1 + 2 * seq_rank) * (LEN - 1 + 2 * position) // (9 * (SEQS - 1) * (LEN - 1))
    rolled = jax.random.randint(key, (SEQS, LEN), 0, 100)
    return (rolled < threshold).astype(jnp.int32).reshape(SEQS * LEN)


def draw_vector_params(key, part):
    key = jax.random.fold_in(key, 31)
    subkeys = jax.random.split(key, 7)
    row_count = 11 * LAYERS + 4
    grid_shape = (row_count, D)
    column_place = jnp.arange(D, dtype=jnp.float32)[None, :] / (D - 1)
    gains = (0.6 + 1.2 * column_place) * (1.0 + 0.1 * jax.random.normal(subkeys[0], grid_shape))
    biases = 0.3 * jax.random.normal(subkeys[1], grid_shape)
    shares = jax.random.uniform(subkeys[2], grid_shape, minval=0.1, maxval=0.9)
    bonuses = jax.random.uniform(subkeys[3], grid_shape, minval=-1.0, maxval=1.0)
    slow_log = jax.random.uniform(subkeys[4], grid_shape, minval=math.log(0.5 / LEN), maxval=math.log(2.0 / LEN))
    fast_log = jax.random.uniform(subkeys[5], grid_shape, minval=math.log(0.5 / LEN), maxval=math.log(1.0 / 24))
    pick_fast = jax.random.uniform(subkeys[6], grid_shape) < 0.5
    decays = jnp.where(pick_fast, fast_log, slow_log)
    row_id = jnp.arange(row_count)[:, None]
    row_kind = jnp.where(row_id < 11 * LAYERS, row_id % 11, (row_id - 11 * LAYERS) % 2)
    is_gain = (row_kind == 0) | (row_kind == 7)
    is_bias = (row_kind == 1) | (row_kind == 8)
    picked = jnp.where(row_kind == 6, bonuses, shares)
    picked = jnp.where(row_kind == 5, decays, picked)
    picked = jnp.where(is_bias, biases, picked)
    return jnp.where(is_gain, gains, picked).astype(jnp.float32)


def draw_head_table(key, part):
    key = jax.random.fold_in(key, 53)
    entry_place = jnp.arange(V, dtype=jnp.float32)[None, :] / (V - 1)
    basic = jax.random.normal(key, (D, V))
    rising = 1.0 + 2.0 * entry_place
    return (basic * rising / (1.3 * math.sqrt(D))).astype(jnp.float32)


def with_ends(drawn, own_key, smallest, top_value):
    longest = drawn.shape.index(max(drawn.shape))
    spots = []
    for shift in (0, 1):
        where = [jax.random.randint(jax.random.fold_in(own_key, axis), (), 0, length) for axis, length in enumerate(drawn.shape)]
        where[longest] = (where[longest] + shift) % drawn.shape[longest]
        spots.append(tuple(where))
    return drawn.at[spots[0]].set(smallest).at[spots[1]].set(top_value)


def level_of(rng, dims, pieces, least, high):
    loudness = 1.0
    for dim, parts in pieces:
        heights = jax.random.uniform(jax.random.fold_in(jax.random.fold_in(rng, 6), dim), (parts,), jnp.float32, least / len(pieces), high / len(pieces))
        loudness = loudness * jnp.repeat(jnp.exp(heights), dims[dim] // parts).reshape((-1,) + (1,) * (len(dims) - 1 - dim))
    return loudness


def rank_bounds(amount, slope):
    loads = [(1 << 20) // math.isqrt(grade ** slope) + 1 for grade in range(1, amount + 1)]
    width = 1 + sum(loads) // (1 << 30)
    return np.cumsum(np.array([max(1, weight // width) for weight in loads]))


def ranked(rng, dims, count, skew):
    listing = rank_bounds(count, skew)
    pick = jax.random.randint(jax.random.fold_in(rng, 1), dims, 0, int(listing[count - 1]))
    grade = jnp.searchsorted(jnp.asarray(listing, jnp.int32), pick, side="right")
    return jax.random.permutation(jax.random.fold_in(rng, 2), count)[grade].astype(jnp.int32)


def scatter_about(stream_key, dims, scale, bound, cuts=(), kind=jnp.bfloat16):
    level = level_of(stream_key, dims, cuts, -0.22, 0.18) if cuts else 1.0
    entries = jax.random.normal(stream_key, dims, jnp.float32) * scale * level
    return jnp.minimum(jnp.maximum(entries, -bound), bound).astype(kind)


def setup_inputs(seed: int = 0) -> dict:
    streams_of = jax.random.split(jax.random.key(seed), 22)
    token_ids = with_ends(ranked(streams_of[0], (TOKENS,), V, 2), jax.random.fold_in(streams_of[0], 3), 0, V - 1).astype(jnp.int32)
    targets = with_ends(ranked(streams_of[1], (TOKENS,), V, 2), jax.random.fold_in(streams_of[1], 3), 0, V - 1).astype(jnp.int32)
    loss_mask = draw_loss_mask(jax.random.fold_in(streams_of[21], 71), 0)
    square_weights = scatter_about(streams_of[3], (LAYERS, 5, D, D), D ** -0.5, 0.21875, ((2, 32),), jnp.float32)
    expand_weights = scatter_about(streams_of[4], (LAYERS, D, FF), D ** -0.5, 0.21875, ((1, 32),), jnp.float32)
    shrink_weights = scatter_about(streams_of[5], (LAYERS, FF, D), FF ** -0.5, 0.109375, ((1, 32),), jnp.float32)
    vector_params = draw_vector_params(jax.random.fold_in(streams_of[21], 71), 0)
    embed_table = scatter_about(streams_of[7], (D, V), 1.0, 6.0, ((0, 32),), jnp.float32)
    head_table = draw_head_table(jax.random.fold_in(streams_of[21], 71), 0)
    square_first = scatter_about(streams_of[9], (LAYERS, 5, D, D), (0.11 * (0.25 / (TOKENS * PARAMS)) ** 0.5), 3.5762786865234375e-07, ((2, 32),), jnp.float32)
    expand_first = scatter_about(streams_of[10], (LAYERS, D, FF), (0.11 * (0.25 / (TOKENS * PARAMS)) ** 0.5), 3.5762786865234375e-07, ((1, 32),), jnp.float32)
    shrink_first = scatter_about(streams_of[11], (LAYERS, FF, D), (0.11 * (0.25 / (TOKENS * PARAMS)) ** 0.5), 3.5762786865234375e-07, ((1, 32),), jnp.float32)
    vector_first = scatter_about(streams_of[12], (VROWS, D), (0.44 * (0.25 / (TOKENS * PARAMS)) ** 0.5), 1.430511474609375e-06, ((1, 32),), jnp.float32)
    embed_first = scatter_about(streams_of[13], (D, V), (0.006 * (0.25 / (TOKENS * PARAMS)) ** 0.5), 1.862645149230957e-08, ((0, 32),), jnp.float32)
    head_first = scatter_about(streams_of[14], (D, V), (0.11 * (0.25 / (TOKENS * PARAMS)) ** 0.5), 3.5762786865234375e-07, ((0, 8), (1, 4)), jnp.float32)
    square_second = jnp.clip(jnp.exp(math.log(2.6191929501591426e-15) - 2.7725887 * jax.random.uniform(streams_of[15], (LAYERS, 5, D, D), jnp.float32) ** level_of(streams_of[15], (LAYERS, 5, D, D), ((2, 32),), -0.2, 0.2)), 1.636995593849464e-16, 2.6191929501591426e-15)
    expand_second = jnp.clip(jnp.exp(math.log(2.6191929501591426e-15) - 2.7725887 * jax.random.uniform(streams_of[16], (LAYERS, D, FF), jnp.float32) ** level_of(streams_of[16], (LAYERS, D, FF), ((1, 32),), -0.2, 0.2)), 1.636995593849464e-16, 2.6191929501591426e-15)
    shrink_second = jnp.clip(jnp.exp(math.log(2.6191929501591426e-15) - 2.7725887 * jax.random.uniform(streams_of[17], (LAYERS, FF, D), jnp.float32) ** level_of(streams_of[17], (LAYERS, FF, D), ((1, 32),), -0.2, 0.2)), 1.636995593849464e-16, 2.6191929501591426e-15)
    vector_second = jnp.clip(jnp.exp(math.log(4.190708720254628e-14) - 2.7725887 * jax.random.uniform(streams_of[18], (VROWS, D), jnp.float32) ** level_of(streams_of[18], (VROWS, D), ((1, 32),), -0.2, 0.2)), 2.6191929501591426e-15, 4.190708720254628e-14)
    embed_second = jnp.clip(jnp.exp(math.log(1.3095964486097917e-16) - 2.7725887 * jax.random.uniform(streams_of[19], (D, V), jnp.float32) ** level_of(streams_of[19], (D, V), ((0, 32),), -0.2, 0.2)), 8.184977803811198e-18, 1.3095964486097917e-16)
    head_second = jnp.clip(jnp.exp(math.log(2.6191929501591426e-15) - 2.7725887 * jax.random.uniform(streams_of[20], (D, V), jnp.float32) ** level_of(streams_of[20], (D, V), ((0, 8), (1, 4)), -0.2, 0.2)), 1.636995593849464e-16, 2.6191929501591426e-15)
    return dict(token_ids=token_ids, targets=targets, loss_mask=loss_mask, square_weights=square_weights, expand_weights=expand_weights, shrink_weights=shrink_weights, vector_params=vector_params, embed_table=embed_table, head_table=head_table, square_first=square_first, expand_first=expand_first, shrink_first=shrink_first, vector_first=vector_first, embed_first=embed_first, head_first=head_first, square_second=square_second, expand_second=expand_second, shrink_second=shrink_second, vector_second=vector_second, embed_second=embed_second, head_second=head_second)


@jax.custom_vjp
def low(v):
    return lax.optimization_barrier(v.astype(jnp.bfloat16)).astype(jnp.float32)

@jax.custom_vjp
def low_back(v):
    return v

def low_keep(v):
    return (low(v), None)

def low_pass(kept, grad):
    return (grad,)

def back_keep(v):
    return (v, None)

def back_low(kept, grad):
    return (low(grad),)
low.defvjp(low_keep, low_pass)
low_back.defvjp(back_keep, back_low)
EXACT_MATMUL = lax.Precision.HIGHEST
BETA_ONE = 0.9
BETA_TWO = 0.999
ADAM_EPS = 1e-08
WEIGHT_DECAY = 0.01
LEARN_RATES = (0.03, 0.03, 0.015, 0.5, 2.0, 0.05)
DECAY_FLAGS = (True, True, True, False, True, True)
param_stride = 11

def layer_norm(values, gain, bias):
    centre = values - lax.optimization_barrier(jnp.mean(values, axis=-1, keepdims=True))
    spread = lax.optimization_barrier(jnp.mean(centre * centre, axis=-1, keepdims=True))
    return centre * lax.rsqrt(spread + 1e-05) * gain + bias

def shift_rows(incoming_rows):
    return jnp.concatenate([jnp.zeros_like(incoming_rows[:, :1]), incoming_rows[:, :-1]], axis=1)

def blend_rows(incoming_rows, earlier, share):
    return incoming_rows * share + earlier * (1.0 - share)

def project(incoming_rows, weight_matrix):
    return jnp.einsum('hza,av->hzv', incoming_rows, weight_matrix, precision=EXACT_MATMUL)

def scaled_carryover(arriving_lookups, arriving_contents, logarithmic_fading_speed, present_reward):
    keep_rate = jnp.exp(-jnp.exp(logarithmic_fading_speed))
    diagonal_amplifier = jnp.exp(present_reward)

    @jax.checkpoint
    def advance(state, step_item):
        numerator, denominator = state
        key_now, value_now = step_item
        growth = jnp.exp(key_now)
        own_term = diagonal_amplifier * growth
        result = (numerator + own_term * value_now) / (denominator + own_term)
        return ((keep_rate * numerator + growth * value_now, keep_rate * denominator + growth), result)
    zero_state = jnp.zeros(arriving_lookups[:, 0].shape, jnp.float32)
    moved = (jnp.swapaxes(arriving_lookups, 0, 1), jnp.swapaxes(arriving_contents, 0, 1))
    spare_placeholder, results = lax.scan(advance, (zero_state, zero_state), moved)
    return jnp.swapaxes(results, 0, 1)

def layer_step(stream, params, square, expand, shrink):
    normed = layer_norm(stream, params[0], params[1])
    earlier = shift_rows(normed)
    mixed_key = low(blend_rows(normed, earlier, params[2]))
    mixed_value = low(blend_rows(normed, earlier, params[3]))
    mixed_gate = low(blend_rows(normed, earlier, params[4]))
    arriving_lookups = low_back(project(mixed_key, square[0]))
    arriving_contents = low_back(project(mixed_value, square[1]))
    gates_in = low_back(project(mixed_gate, square[2]))
    mixed_out = scaled_carryover(arriving_lookups, arriving_contents, params[5], params[6])
    gated = low(jax.nn.sigmoid(gates_in) * mixed_out)
    middle = stream + low_back(project(gated, square[3]))
    normed_two = layer_norm(middle, params[7], params[8])
    earlier_two = shift_rows(normed_two)
    chan_key = low(blend_rows(normed_two, earlier_two, params[9]))
    chan_gate = low(blend_rows(normed_two, earlier_two, params[10]))
    pre_act = low_back(project(chan_key, expand))
    activated = low(jnp.square(jnp.maximum(pre_act, 0.0)))
    chan_value = low_back(project(activated, shrink))
    gate_pre = low_back(project(chan_gate, square[4]))
    return middle + jax.nn.sigmoid(gate_pre) * chan_value

def objective(square, expand, shrink, params, table, head, token_ids, targets, loss_mask):
    square = low(square)
    expand = low(expand)
    shrink = low(shrink)
    params = low(params)
    table = low(table)
    head = low(head)
    base_row = param_stride * LAYERS
    embedded = low_back(jnp.take(table, token_ids, axis=1).T).reshape(SEQS, LEN, D)
    stream = layer_norm(embedded, params[base_row], params[base_row + 1])
    for layer_id in range(LAYERS):
        rows_here = params[layer_id * param_stride:(layer_id + 1) * param_stride]
        stream = layer_step(stream, rows_here, square[layer_id], expand[layer_id], shrink[layer_id])
    normed = layer_norm(stream, params[base_row + 2], params[base_row + 3])

    @jax.checkpoint
    def sequence_loss(step_item):
        rows_now, wanted, counted = step_item
        logits = low_back(jnp.dot(low(rows_now), head, precision=EXACT_MATMUL))
        row_top = lax.optimization_barrier(jnp.max(logits, axis=1, keepdims=True))
        log_total = row_top[:, 0] + jnp.log(lax.optimization_barrier(jnp.sum(jnp.exp(logits - row_top), axis=1)))
        picked = jnp.take_along_axis(logits, wanted[:, None], axis=1)[:, 0]
        return jnp.sum(counted.astype(jnp.float32) * (log_total - picked))
    per_sequence = lax.map(sequence_loss, (normed, targets.reshape(SEQS, LEN), loss_mask.reshape(SEQS, LEN)))
    whole_sum = jnp.sum(per_sequence)
    return (whole_sum / TOKENS, whole_sum)

def adam_update(weights, gradient, first, second, step_rate, decay_on):
    first_new = BETA_ONE * first + (1.0 - BETA_ONE) * gradient
    second_new = BETA_TWO * second + (1.0 - BETA_TWO) * gradient * gradient
    first_hat = first_new / (1.0 - BETA_ONE ** STEP)
    second_hat = second_new / (1.0 - BETA_TWO ** STEP)
    moved = first_hat / (jnp.sqrt(second_hat) + ADAM_EPS)
    if decay_on:
        moved = moved + WEIGHT_DECAY * weights
    return (weights - step_rate * moved, first_new, second_new)

def reference(token_ids, targets, loss_mask, square_weights, expand_weights, shrink_weights, vector_params, embed_table, head_table, square_first, expand_first, shrink_first, vector_first, embed_first, head_first, square_second, expand_second, shrink_second, vector_second, embed_second, head_second):
    weights = (square_weights, expand_weights, shrink_weights, vector_params, embed_table, head_table)
    firsts = (square_first, expand_first, shrink_first, vector_first, embed_first, head_first)
    seconds = (square_second, expand_second, shrink_second, vector_second, embed_second, head_second)

    def loss_of(square, expand, shrink, params, table, head):
        return objective(square, expand, shrink, params, table, head, token_ids, targets, loss_mask)
    spare_placeholder, pull, loss_sum = jax.vjp(loss_of, *weights, has_aux=True)
    gradients = pull(jnp.ones((), jnp.float32))
    square_sum = jnp.zeros((), jnp.float32)
    for gradient in gradients:
        square_sum = square_sum + jnp.sum(gradient * gradient)
    grad_norm = jnp.sqrt(square_sum)
    scale = jnp.minimum(1.0, 0.5 / math.sqrt(TOKENS) / (grad_norm + 1e-06))
    updated = [adam_update(weights[slot], gradients[slot] * scale, firsts[slot], seconds[slot], LEARN_RATES[slot], DECAY_FLAGS[slot]) for slot in range(6)]
    return (loss_sum, grad_norm, updated[0][0], updated[1][0], updated[2][0], updated[3][0], updated[4][0], updated[5][0], updated[0][1], updated[1][1], updated[2][1], updated[3][1], updated[4][1], updated[5][1], updated[0][2], updated[1][2], updated[2][2], updated[3][2], updated[4][2], updated[5][2])
```

```python
import math

import jax
import jax.numpy as jnp
from jax import lax
from jax.experimental import pallas as pl
from jax.experimental.pallas import tpu as pltpu
from jax.sharding import PartitionSpec as P

STEP = 10
ON_MESH = pl.DeviceIdType.MESH


def place():
    dp, seq = lax.axis_index("dp"), lax.axis_index("seq")
    return dp, seq, dp // 2, lax.rem(dp, 2), seq // 2, lax.rem(seq, 2)


def greet(partners, extra):
    barrier = pltpu.get_barrier_semaphore()
    for partner in partners:
        pl.semaphore_signal(barrier, inc=1, device_id=partner, device_id_type=ON_MESH)
    for exists, partner in extra:
        @pl.when(exists)
        def _():
            pl.semaphore_signal(barrier, inc=1, device_id=partner, device_id_type=ON_MESH)
    peers = len(partners)
    for exists, partner in extra:
        peers = peers + exists.astype(jnp.int32)
    pl.semaphore_wait(barrier, peers)


class Sems:
    def __init__(self, send, recv, local):
        self.send, self.recv, self.local = send, recv, local
        self.ns = self.nr = self.nl = 0

    def pair(self):
        self.ns += 1
        return self.send.at[self.ns - 1], self.recv.at[self.ns - 1]

    def own(self):
        self.nl += 1
        return self.local.at[self.nl - 1]


def gather_blocks(tensors, portions, collective_id):
    count = len(tensors)
    dims = [t.shape for t in tensors]
    hops = 3
    pieces_total = sum(len(p) for p in portions)
    n_send = count + count + pieces_total * (1 + 2 * hops + 7)

    def kernel(*refs):
        ins, outs = refs[:count], refs[count : 2 * count]
        wide = refs[2 * count : 3 * count]
        half = refs[3 * count : 4 * count]
        send, recv, local = refs[4 * count :]
        dp, seq, z, y, x, c = place()
        core = (dp, seq + 1 - 2 * c)
        xway = (dp, seq + 2 - 4 * x)
        yway = (dp + 1 - 2 * y, seq)
        up, down = (dp + 2, seq), (dp - 2, seq)
        has_up, has_down = z < hops, z > 0
        greet([core, xway, yway], [(has_up, up), (has_down, down)])
        sems = Sems(send, recv, local)

        def cols(t, side):
            width = dims[t][2] // 2
            return pl.ds(pl.multiple_of(side * width, 128), width)

        first = []
        for t in range(count):
            rows = pl.ds(pl.multiple_of(c * dims[t][1], 8), dims[t][1])
            mine = pltpu.make_async_copy(ins[t].at[:, :, cols(t, c)], wide[t].at[:, rows, :], sems.own())
            ss, rs = sems.pair()
            other = pltpu.make_async_remote_copy(
                src_ref=ins[t].at[:, :, cols(t, 1 - c)], dst_ref=wide[t].at[:, rows, :],
                send_sem=ss, recv_sem=rs, device_id=core, device_id_type=ON_MESH)
            other.start()
            mine.start()
            first.append((mine, other))
        core_sems = [sems.pair() for t in range(count)]
        stay = []
        for t in range(count):
            first[t][0].wait()
            first[t][1].wait()
            half[t][...] = wide[t][...].astype(jnp.bfloat16)
            own = pltpu.make_async_copy(half[t], outs[t].at[:, z, y, x, :, cols(t, c)], sems.own())
            own.start()
            stay.append(own)

        def block(piece, zz, yy, xx):
            t, m0, m1, r0, r1 = piece
            return outs[t].at[m0:m1, zz, yy, xx, r0:r1, cols(t, c)]

        def to_core(p, zz, yy, xx, source=None):
            for piece in portions[p]:
                t = piece[0]
                region = block(piece, zz, yy, xx)
                pltpu.make_async_remote_copy(
                    src_ref=region if source is None else source(piece), dst_ref=region,
                    send_sem=core_sems[t][0], recv_sem=core_sems[t][1], device_id=core, device_id_type=ON_MESH).start()

        def message(p, where, device, source=None):
            copies = []
            for piece in portions[p]:
                ss, rs = sems.pair()
                region = block(piece, *where)
                copies.append(pltpu.make_async_remote_copy(
                    src_ref=region if source is None else source(piece), dst_ref=region,
                    send_sem=ss, recv_sem=rs, device_id=device, device_id_type=ON_MESH))
            return copies

        def start(copies):
            for copy in copies:
                copy.start()

        def arrive(copies):
            for copy in copies:
                copy.wait_recv()

        def sent(copies):
            for copy in copies:
                copy.wait_send()

        def from_half(piece):
            t, m0, m1, r0, r1 = piece
            return half[t].at[m0:m1, r0:r1, :]

        both = slice(0, 2)
        a_way, b_way = (yway, xway), (xway, yway)
        a_msgs = []
        for p in range(2):
            msg = message(p, (z, y, x), a_way[p], from_half)
            start(msg)
            a_msgs.append(msg)
        for own in stay:
            own.wait()
        for p in range(2):
            to_core(p, z, y, x, from_half)

        def pair_of(p, zz):
            return (zz, both, x) if p == 0 else (zz, y, both)

        def other_of(p, zz):
            return (zz, 1 - y, x) if p == 0 else (zz, y, 1 - x)

        def far_of(p, zz):
            return (zz, both, 1 - x) if p == 0 else (zz, 1 - y, both)

        zmsg = [[[message(p, pair_of(p, z - k), up) for k in range(hops)],
                 [message(p, pair_of(p, z + k), down) for k in range(hops)]] for p in range(2)]
        b_msgs = []
        for p in range(2):
            own = message(p, pair_of(p, z), b_way[p])
            ups = [message(p, pair_of(p, z - 1 - k), b_way[p]) for k in range(hops)]
            downs = [message(p, pair_of(p, z + 1 + k), b_way[p]) for k in range(hops)]
            b_msgs.append((own, ups, downs))

        for p in range(2):
            arrive(a_msgs[p])

            @pl.when(has_up)
            def _():
                start(zmsg[p][0][0])

            @pl.when(has_down)
            def _():
                start(zmsg[p][1][0])
            start(b_msgs[p][0])
            to_core(p, *other_of(p, z))

        def far_own(p):
            arrive(b_msgs[p][0])
            to_core(p, *far_of(p, z))

        def far_hop(p, k):
            @pl.when(z - 1 - k >= 0)
            def _():
                arrive(b_msgs[p][1][k])
                to_core(p, *far_of(p, z - 1 - k))

            @pl.when(z + 1 + k <= hops)
            def _():
                arrive(b_msgs[p][2][k])
                to_core(p, *far_of(p, z + 1 + k))

        for k in range(hops):
            for p in range(2):
                @pl.when(z - 1 - k >= 0)
                def _():
                    arrive(zmsg[p][0][k])
                    if k + 1 < hops:
                        @pl.when(has_up)
                        def _():
                            start(zmsg[p][0][k + 1])
                    start(b_msgs[p][1][k])
                    to_core(p, *pair_of(p, z - 1 - k))

                @pl.when(z + 1 + k <= hops)
                def _():
                    arrive(zmsg[p][1][k])
                    if k + 1 < hops:
                        @pl.when(has_down)
                        def _():
                            start(zmsg[p][1][k + 1])
                    start(b_msgs[p][2][k])
                    to_core(p, *pair_of(p, z + 1 + k))
            for p in range(2):
                if k == 0:
                    far_own(p)
                else:
                    far_hop(p, k - 1)
        for p in range(2):
            far_hop(p, hops - 1)

        for p in range(2):
            sent(a_msgs[p])
            sent(b_msgs[p][0])
            for k in range(hops):
                @pl.when((z - k >= 0) & has_up)
                def _():
                    sent(zmsg[p][0][k])

                @pl.when((z + k <= hops) & has_down)
                def _():
                    sent(zmsg[p][1][k])

                @pl.when(z - 1 - k >= 0)
                def _():
                    sent(b_msgs[p][1][k])

                @pl.when(z + 1 + k <= hops)
                def _():
                    sent(b_msgs[p][2][k])
        for t in range(count):
            whole = pltpu.make_async_remote_copy(
                src_ref=outs[t].at[:, :, :, :, :, cols(t, c)], dst_ref=outs[t].at[:, :, :, :, :, cols(t, 1 - c)],
                send_sem=core_sems[t][0], recv_sem=core_sems[t][1], device_id=core, device_id_type=ON_MESH)
            whole.wait_send()
            whole.wait_recv()

    outs = pl.pallas_call(
        kernel,
        out_shape=[jax.ShapeDtypeStruct((m, hops + 1, 2, 2, 2 * r, w), jnp.bfloat16) for m, r, w in dims],
        in_specs=[pl.BlockSpec(memory_space=pl.ANY)] * count,
        out_specs=[pl.BlockSpec(memory_space=pl.ANY)] * count,
        scratch_shapes=[pltpu.VMEM((m, 2 * r, w // 2), jnp.float32) for m, r, w in dims]
        + [pltpu.VMEM((m, 2 * r, w // 2), jnp.bfloat16) for m, r, w in dims]
        + [pltpu.SemaphoreType.DMA((n_send,)), pltpu.SemaphoreType.DMA((n_send,)), pltpu.SemaphoreType.DMA((2 * count,))],
        compiler_params=pltpu.CompilerParams(collective_id=collective_id, has_side_effects=True, vmem_limit_bytes=40 << 20),
    )(*tensors)
    return [o.reshape(m, (hops + 1) * 8 * r, w) for o, (m, r, w) in zip(outs, dims)]


def scatter_blocks(tensors, portions, rows_own, collective_id):
    count = len(tensors)
    hops = 3
    dims = [(t.shape[0], r, t.shape[2]) for t, r in zip(tensors, rows_own)]
    views = [t.reshape(m, hops + 1, 2, 2, 2 * r, w) for t, (m, r, w) in zip(tensors, dims)]
    pieces_total = sum(len(p) for p in portions)
    n_send = pieces_total * (2 + 4 + 2 * hops + 1) + count
    n_local = pieces_total * 2 + count
    flat = [(p, piece) for p in range(2) for piece in portions[p]]
    flat_dims = [(piece[2] - piece[1], piece[4] - piece[3], dims[piece[0]][2] // 2) for _, piece in flat]

    def kernel(*refs):
        ins, outs = refs[:count], refs[count : 2 * count]
        k0 = 2 * count
        acc = refs[k0 : k0 + count]
        crecv = refs[k0 + count : k0 + 2 * count]
        fin = refs[k0 + 2 * count : k0 + 3 * count]
        k0 += 3 * count
        n = len(flat)
        b_all, u_all, d_all, a_all = (refs[k0 + i * n : k0 + (i + 1) * n] for i in range(4))
        send, recv, local = refs[k0 + 4 * n :]
        index = {}
        for i, (p, piece) in enumerate(flat):
            index.setdefault(p, []).append((i, piece))
        dp, seq, z, y, x, c = place()
        core = (dp, seq + 1 - 2 * c)
        xway = (dp, seq + 2 - 4 * x)
        yway = (dp + 1 - 2 * y, seq)
        up, down = (dp + 2, seq), (dp - 2, seq)
        has_up, has_down = z < hops, z > 0
        greet([core, xway, yway], [(has_up, up), (has_down, down)])
        sems = Sems(send, recv, local)
        a_way, b_way = (yway, xway), (xway, yway)

        def cols(t, side):
            width = dims[t][2] // 2
            return pl.ds(pl.multiple_of(side * width, 128), width)

        def remote(src, dst, device):
            ss, rs = sems.pair()
            return pltpu.make_async_remote_copy(src_ref=src, dst_ref=dst, send_sem=ss, recv_sem=rs,
                                                device_id=device, device_id_type=ON_MESH)

        def place_of(p, zz, a, b):
            return (zz, a, b) if p == 0 else (zz, b, a)

        own_a, own_b = (y, x), (x, y)

        def add(dst, src, lead):
            def turn(i, _):
                where, rest = [], i
                for size in reversed(lead):
                    where.append(lax.rem(rest, size))
                    rest = rest // size
                where = tuple(reversed(where))
                dst[where] = (dst[where].astype(jnp.float32) + src[where].astype(jnp.float32)).astype(dst.dtype)
                return 0
            total = 1
            for size in lead:
                total *= size
            lax.fori_loop(0, total, turn, 0)

        everyz, both = slice(0, hops + 1), slice(0, 2)
        chunks = {}
        for far in (1, 0):
            for p in range(2):
                b = own_b[p] if far == 0 else 1 - own_b[p]
                made = []
                for i, piece in index[p]:
                    t, m0, m1, r0, r1 = piece
                    where = (slice(m0, m1),) + place_of(p, everyz, both, b) + (slice(r0, r1),)
                    there = remote(ins[t].at[where + (cols(t, 1 - c),)], crecv[t].at[where], core)
                    here = pltpu.make_async_copy(ins[t].at[where + (cols(t, c),)], acc[t].at[where], sems.own())
                    there.start()
                    here.start()
                    made.append((there, here, piece, where))
                chunks[far, p] = made

        def core_add(far, p):
            for there, here, piece, where in chunks[far, p]:
                t, m0, m1, r0, r1 = piece
                there.wait_recv()
                here.wait()
                add(acc[t].at[where], crecv[t].at[where], (m1 - m0, hops + 1, 2))

        zorder = (3, 0, 2, 1)
        b_msgs = {}
        for p in range(2):
            core_add(1, p)
            for zz in zorder:
                msgs = []
                for i, (t, m0, m1, r0, r1) in index[p]:
                    src = acc[t].at[(slice(m0, m1),) + place_of(p, zz, both, 1 - own_b[p]) + (slice(r0, r1),)]
                    msgs.append(remote(src, b_all[i].at[:, zz], b_way[p]))
                for msg in msgs:
                    msg.start()
                b_msgs[p, zz] = msgs
        for p in range(2):
            core_add(0, p)

        def b_add(p, zz):
            for msg in b_msgs[p, zz]:
                msg.wait_recv()
            for i, (t, m0, m1, r0, r1) in index[p]:
                dst = acc[t].at[(slice(m0, m1),) + place_of(p, zz, both, own_b[p]) + (slice(r0, r1),)]
                add(dst, b_all[i].at[:, zz], (m1 - m0, 2))

        def mine(p, i, piece, zz):
            t, m0, m1, r0, r1 = piece
            return acc[t].at[(slice(m0, m1),) + place_of(p, zz, both, own_b[p]) + (slice(r0, r1),)]

        up_msgs, down_msgs = {}, {}
        for p in range(2):
            for zz in range(hops + 1):
                up_msgs[p, zz] = [remote(mine(p, i, piece, zz), u_all[i].at[:, zz], up) for i, piece in index[p]] if zz > 0 else None
                down_msgs[p, zz] = [remote(mine(p, i, piece, zz), d_all[i].at[:, zz], down) for i, piece in index[p]] if zz < hops else None

        def z_add(p, zz, msgs, land):
            for msg in msgs[p, zz]:
                msg.wait_recv()
            for i, piece in index[p]:
                add(mine(p, i, piece, zz), land[i].at[:, zz], (piece[2] - piece[1], 2))

        def up_send(p, zz):
            @pl.when(z < zz)
            def _():
                @pl.when(z > 0)
                def _():
                    z_add(p, zz, up_msgs, u_all)
                for msg in up_msgs[p, zz]:
                    msg.start()

        def down_send(p, zz):
            @pl.when(z > zz)
            def _():
                @pl.when(z < hops)
                def _():
                    z_add(p, zz, down_msgs, d_all)
                for msg in down_msgs[p, zz]:
                    msg.start()

        for p in range(2):
            b_add(p, 3)
            up_send(p, 3)
            b_add(p, 0)
            down_send(p, 0)
        for p in range(2):
            b_add(p, 2)
            up_send(p, 2)
            b_add(p, 1)
            down_send(p, 1)
        for p in range(2):
            up_send(p, 1)
            down_send(p, 2)
        a_msgs = {}
        for p in range(2):
            for zz in range(hops + 1):
                @pl.when(z == zz)
                def _():
                    if zz > 0:
                        z_add(p, zz, up_msgs, u_all)
                    if zz < hops:
                        z_add(p, zz, down_msgs, d_all)
            msgs = []
            for i, (t, m0, m1, r0, r1) in index[p]:
                src = acc[t].at[(slice(m0, m1),) + place_of(p, z, 1 - own_a[p], own_b[p]) + (slice(r0, r1),)]
                msgs.append(remote(src, a_all[i], a_way[p]))
            for msg in msgs:
                msg.start()
            a_msgs[p] = msgs
        for p in range(2):
            for msg in a_msgs[p]:
                msg.wait_recv()
            for i, (t, m0, m1, r0, r1) in index[p]:
                for m in range(m0, m1):
                    part = acc[t][(m,) + place_of(p, z, own_a[p], own_b[p]) + (slice(r0, r1),)]
                    fin[t][m, r0:r1, :] = part.astype(jnp.float32) + a_all[i][m - m0].astype(jnp.float32)
        last = []
        for t in range(count):
            r = dims[t][1]
            other = remote(fin[t].at[:, pl.ds(pl.multiple_of((1 - c) * r, 8), r), :], outs[t].at[:, :, cols(t, c)], core)
            keep = pltpu.make_async_copy(fin[t].at[:, pl.ds(pl.multiple_of(c * r, 8), r), :], outs[t].at[:, :, cols(t, c)], sems.own())
            other.start()
            keep.start()
            last.append((other, keep))
        for made in chunks.values():
            for there, here, piece, where in made:
                there.wait_send()
        for msgs in list(b_msgs.values()) + list(a_msgs.values()):
            for msg in msgs:
                msg.wait_send()
        for p in range(2):
            for zz in range(hops + 1):
                if zz > 0:
                    @pl.when(z < zz)
                    def _():
                        for msg in up_msgs[p, zz]:
                            msg.wait_send()
                if zz < hops:
                    @pl.when(z > zz)
                    def _():
                        for msg in down_msgs[p, zz]:
                            msg.wait_send()
        for other, keep in last:
            keep.wait()
            other.wait()

    bf = jnp.bfloat16
    outs = pl.pallas_call(
        kernel,
        out_shape=[jax.ShapeDtypeStruct((m, r, w), jnp.float32) for m, r, w in dims],
        in_specs=[pl.BlockSpec(memory_space=pl.ANY)] * count,
        out_specs=[pl.BlockSpec(memory_space=pl.ANY)] * count,
        scratch_shapes=[pltpu.VMEM((m, hops + 1, 2, 2, 2 * r, w // 2), bf) for m, r, w in dims]
        + [pltpu.VMEM((m, hops + 1, 2, 2, 2 * r, w // 2), bf) for m, r, w in dims]
        + [pltpu.VMEM((m, 2 * r, w // 2), jnp.float32) for m, r, w in dims]
        + [pltpu.VMEM((m, hops + 1, 2, r, w), bf) for m, r, w in flat_dims] * 3
        + [pltpu.VMEM((m, r, w), bf) for m, r, w in flat_dims]
        + [pltpu.SemaphoreType.DMA((n_send,)), pltpu.SemaphoreType.DMA((n_send,)), pltpu.SemaphoreType.DMA((n_local,))],
        compiler_params=pltpu.CompilerParams(collective_id=collective_id, has_side_effects=True, vmem_limit_bytes=50 << 20),
    )(*views)
    return list(lax.optimization_barrier(outs))


def sum_everywhere(value, collective_id):
    sizes = (("dp", lax.axis_size("dp")), ("seq", lax.axis_size("seq")))
    steps = [(axis, 1 << bit) for axis, size in reversed(sizes) for bit in range(size.bit_length() - 1)]

    def kernel(in_ref, out_ref, land, send, recv):
        dp, seq = lax.axis_index("dp"), lax.axis_index("seq")
        partners = []
        for axis, step in steps:
            mine = dp if axis == "dp" else seq
            other = mine + step - 2 * step * lax.rem(mine // step, 2)
            partners.append((other, seq) if axis == "dp" else (dp, other))
        greet(partners, [])
        out_ref[...] = in_ref[...]
        for k, partner in enumerate(partners):
            land[0, k] = out_ref[...]
            copy = pltpu.make_async_remote_copy(
                src_ref=land.at[0, k],
                dst_ref=land.at[1, k],
                send_sem=send.at[k],
                recv_sem=recv.at[k],
                device_id=partner,
                device_id_type=ON_MESH,
            )
            copy.start()
            copy.wait()
            out_ref[...] = out_ref[...] + land[1, k]

    n = len(steps)
    out = pl.pallas_call(
        kernel,
        out_shape=jax.ShapeDtypeStruct((8, 128), jnp.float32),
        in_specs=[pl.BlockSpec(memory_space=pltpu.VMEM)],
        out_specs=pl.BlockSpec(memory_space=pltpu.VMEM),
        scratch_shapes=[
            pltpu.VMEM((2, n, 8, 128), jnp.float32),
            pltpu.SemaphoreType.DMA((n,)),
            pltpu.SemaphoreType.DMA((n,)),
        ],
        compiler_params=pltpu.CompilerParams(collective_id=collective_id, has_side_effects=True),
    )(jnp.broadcast_to(value, (8, 128)))
    return out[0, 0]


BOTH = ("dp", "seq")


def on_box():
    return lax.axis_size("dp") == 8 and lax.axis_size("seq") == 4


def gather_rows(tensors, portions, collective_id):
    if on_box():
        return gather_blocks(tensors, portions, collective_id)
    return [lax.all_gather(t.astype(jnp.bfloat16), BOTH, axis=1, tiled=True) for t in tensors]


def scatter_rows(tensors, portions, collective_id):
    if on_box():
        devices = lax.axis_size("dp") * lax.axis_size("seq")
        rows = [t.shape[1] // devices for t in tensors]
        return scatter_blocks(tensors, portions, rows, collective_id)
    return [
        lax.psum_scatter(t, BOTH, scatter_dimension=1, tiled=True).astype(jnp.float32) for t in tensors
    ]


def weight_portions(square, expand, shrink, vectors):
    first = [(1, 0, 1, 0, 2 * expand), (0, 0, 3, 0, 2 * square)]
    second = [(2, 0, 1, 0, 2 * shrink), (0, 3, 5, 0, 2 * square)]
    if vectors:
        second.append((3, 0, 1, 0, 2 * vectors))
    return [first, second]


def row_portions(rows):
    return [[(0, 0, 1, 0, rows)], [(0, 0, 1, rows, 2 * rows)]]


def as_rows(vectors):
    lanes = -(-vectors.shape[0] // 256) * 256
    return jnp.pad(vectors.T, ((0, 0), (0, lanes - vectors.shape[0])))[None]

EXACT_MATMUL = lax.Precision.HIGHEST
BETA_ONE = 0.9
BETA_TWO = 0.999
ADAM_EPS = 1e-08
WEIGHT_DECAY = 0.01
LEARN_RATES = (0.03, 0.03, 0.015, 0.5, 2.0, 0.05)
DECAY_FLAGS = (True, True, True, False, True, True)
param_stride = 11
logit_block = 512
scan_block = 256


def from_behind(value, axis, steps):
    count = lax.axis_size(axis)
    leading, last = (max(0, -steps), min(count, count - steps))
    return lax.ppermute(value, axis, [(source, source + steps) for source in range(leading, last)])


def carried_in(value, axis, join, neutral, backward):
    count, mine = (lax.axis_size(axis), lax.axis_index(axis))
    pieces = lax.all_gather(jnp.stack(value), axis)
    if backward:
        pieces = pieces[::-1]
        mine = count - 1 - mine
    running = neutral
    for position in range(count - 1):
        longer = join(running, tuple(pieces[position]))
        running = tuple(
            jnp.where(position < mine, new, old) for new, old in zip(longer, running)
        )
    return running


def layer_norm(values, gain, bias):
    centre = values - jnp.mean(values, axis=-1, keepdims=True)
    spread = jnp.mean(centre * centre, axis=-1, keepdims=True)
    return centre * lax.rsqrt(spread + 1e-05) * gain + bias


def matmul(left, right):
    return jnp.dot(left, right, preferred_element_type=jnp.float32)


def matmul_tn(left, right):
    return lax.dot_general(
        left, right, (((0,), (0,)), ((), ())), preferred_element_type=jnp.float32
    )


def matmul_nt(left, right):
    return lax.dot_general(
        left, right, (((1,), (1,)), ((), ())), preferred_element_type=jnp.float32
    )


def blend_all(normed, incoming, shares):
    earlier = jnp.concatenate([incoming, normed[:-1]], axis=0)
    return tuple(
        (
            normed * shares[member] + earlier * (1.0 - shares[member])
            for member in range(shares.shape[0])
        )
    )


def take_previous(normed):
    return from_behind(normed[-1:], "seq", 1)


def give_back(grad_first):
    return from_behind(grad_first, "seq", -1)


def block_ends(arriving_lookups, arriving_contents, logarithmic_fading_speed):
    decay_rate = jnp.exp(logarithmic_fading_speed)
    length = arriving_lookups.shape[0]
    ages = (length - 1.0 - jnp.arange(length, dtype=jnp.float32))[:, None]
    weight = jnp.exp(arriving_lookups - decay_rate * ages)
    return (jnp.sum(weight * arriving_contents, axis=0), jnp.sum(weight, axis=0))


def block_factor(logarithmic_fading_speed, length):
    return jnp.exp(-jnp.exp(logarithmic_fading_speed) * length)


def chain_combine(earlier, later):
    return (
        earlier[0] * later[2] + later[0],
        earlier[1] * later[2] + later[1],
        earlier[2] * later[2],
    )


def token_mixer_block(
    arriving_lookups,
    arriving_contents,
    logarithmic_fading_speed,
    present_reward,
    initial_numerator,
    initial_denominator,
):
    decay_rate = jnp.exp(logarithmic_fading_speed)
    length, channels = arriving_lookups.shape
    block_size = min(scan_block, length)
    block_count = length // block_size
    offsets = jnp.arange(block_size, dtype=jnp.float32)[:, None]
    lower_mask = (offsets > offsets.T).astype(jnp.float32)
    diagonal_amplifier = jnp.exp(present_reward)
    back_decay = jnp.exp(-decay_rate * (offsets - 1.0))
    carry_decay = jnp.exp(-decay_rate * offsets)
    tail_decay = jnp.exp(-decay_rate * (block_size - 1.0))
    full_decay = jnp.exp(-decay_rate * block_size)

    def sub_block(state, step_item):
        numerator, denominator = state
        key_block, value_block = step_item
        lifted = jnp.exp(key_block + decay_rate * offsets)
        prefix_sums = jnp.dot(
            lower_mask,
            jnp.concatenate([lifted * value_block, lifted], axis=1),
            precision=EXACT_MATMUL,
        )
        own_term = diagonal_amplifier * jnp.exp(key_block)
        top_part = (
            back_decay * prefix_sums[:, :channels]
            + carry_decay * numerator
            + own_term * value_block
        )
        low_part = back_decay * prefix_sums[:, channels:] + carry_decay * denominator + own_term
        next_num = tail_decay * jnp.sum(lifted * value_block, axis=0) + full_decay * numerator
        next_den = tail_decay * jnp.sum(lifted, axis=0) + full_decay * denominator
        return ((next_num, next_den), (top_part / low_part, low_part))

    shaped = (
        arriving_lookups.reshape(block_count, block_size, channels),
        arriving_contents.reshape(block_count, block_size, channels),
    )
    (end_num, end_den), (block_outs, denoms) = lax.scan(
        sub_block, (initial_numerator, initial_denominator), shaped
    )
    return (
        (block_outs.reshape(length, channels), end_num, end_den),
        denoms.reshape(length, channels),
    )


def layer_forward(stream, gathered):
    square, expand, shrink, params = gathered
    normed = layer_norm(stream, params[0], params[1])
    incoming_one = take_previous(normed)
    blended = blend_all(normed, incoming_one, params[2:5])
    mixed_key = blended[0].astype(jnp.bfloat16)
    mixed_value = blended[1].astype(jnp.bfloat16)
    mixed_gate = blended[2].astype(jnp.bfloat16)
    arriving_lookups = matmul(mixed_key, square[0])
    arriving_contents = matmul(mixed_value, square[1])
    gates_in = matmul(mixed_gate, square[2])
    length = arriving_lookups.shape[0]
    end_sums = block_ends(arriving_lookups, arriving_contents, params[5])
    zero_state = jnp.zeros_like(end_sums[0])
    one_state = jnp.ones_like(end_sums[0])
    factor = block_factor(params[5], length)
    initial_numerator, initial_denominator, spare_factor = carried_in(
        (end_sums[0], end_sums[1], factor),
        "seq",
        chain_combine,
        (zero_state, zero_state, one_state),
        False,
    )
    (mixed_out, spare_placeholder, spare_placeholder), spare_placeholder = token_mixer_block(
        arriving_lookups,
        arriving_contents,
        params[5],
        params[6],
        initial_numerator,
        initial_denominator,
    )
    gated = (jax.nn.sigmoid(gates_in) * mixed_out).astype(jnp.bfloat16)
    middle = stream + matmul(gated, square[3])
    normed_two = layer_norm(middle, params[7], params[8])
    incoming_two = take_previous(normed_two)
    blended_two = blend_all(normed_two, incoming_two, params[9:11])
    chan_key = blended_two[0].astype(jnp.bfloat16)
    chan_gate = blended_two[1].astype(jnp.bfloat16)
    pre_act = matmul(chan_key, expand)
    activated = jnp.square(jnp.maximum(pre_act, 0.0)).astype(jnp.bfloat16)
    chan_value = matmul(activated, shrink)
    gate_pre = matmul(chan_gate, square[4])
    result = middle + jax.nn.sigmoid(gate_pre) * chan_value
    saved = (
        stream,
        incoming_one,
        mixed_key,
        mixed_value,
        mixed_gate,
        arriving_lookups,
        arriving_contents,
        gates_in,
        initial_numerator,
        initial_denominator,
        gated,
        middle,
        incoming_two,
        chan_key,
        chan_gate,
        pre_act,
        activated,
        chan_value,
        gate_pre,
    )
    return (result, saved)


def norm_back(stream, incoming, params, first_row, share_rows, grads):
    normed, norm_pull = jax.vjp(layer_norm, stream, params[first_row], params[first_row + 1])
    shares = params[share_rows[0] : share_rows[1]]
    spare_placeholder, blend_pull = jax.vjp(blend_all, normed, incoming, shares)
    d_normed, d_incoming, d_shares = blend_pull(grads)
    from_next = give_back(d_incoming)
    d_normed = d_normed.at[-1].add(from_next[0])
    d_stream, d_gain, d_bias = norm_pull(d_normed)
    return (d_stream, jnp.stack([d_gain, d_bias]), d_shares)


def layer_backward(gradient, saved, gathered):
    square, expand, shrink, params = gathered
    (
        stream,
        incoming_one,
        mixed_key,
        mixed_value,
        mixed_gate,
        arriving_lookups,
        arriving_contents,
        gates_in,
        initial_numerator,
        initial_denominator,
        gated,
        middle,
        incoming_two,
        chan_key,
        chan_gate,
        pre_act,
        activated,
        chan_value,
        gate_pre,
    ) = saved
    gate_sig = jax.nn.sigmoid(gate_pre)
    d_value = (gradient * gate_sig).astype(jnp.bfloat16)
    d_gate_pre = (gradient * chan_value * gate_sig * (1.0 - gate_sig)).astype(jnp.bfloat16)
    g_shrink = matmul_tn(activated, d_value)
    d_active = matmul_nt(d_value, shrink)
    d_pre = (d_active * 2.0 * jnp.maximum(pre_act, 0.0)).astype(jnp.bfloat16)
    g_expand = matmul_tn(chan_key, d_pre)
    g_chan_gate = matmul_tn(chan_gate, d_gate_pre)
    d_chan_key = matmul_nt(d_pre, expand)
    d_chan_gate = matmul_nt(d_gate_pre, square[4])
    d_middle, second_norm_gradient, second_share_gradient = norm_back(
        middle, incoming_two, params, 7, (9, 11), (d_chan_key, d_chan_gate)
    )
    d_middle = d_middle + gradient
    d_output = d_middle.astype(jnp.bfloat16)
    g_output = matmul_tn(gated, d_output)
    d_gated = matmul_nt(d_output, square[3])
    (mixed_out, spare_placeholder, spare_placeholder), token_mixer_backward, denoms = jax.vjp(
        token_mixer_block,
        arriving_lookups,
        arriving_contents,
        params[5],
        params[6],
        initial_numerator,
        initial_denominator,
        has_aux=True,
    )
    gate_sig_one = jax.nn.sigmoid(gates_in)
    mixed_gradient = d_gated * gate_sig_one
    d_gates_in = (d_gated * mixed_out * gate_sig_one * (1.0 - gate_sig_one)).astype(jnp.bfloat16)
    length = arriving_lookups.shape[0]
    decay_rate = jnp.exp(params[5])
    carried = (
        jnp.exp(-decay_rate * jnp.arange(length, dtype=jnp.float32)[:, None])
        * mixed_gradient
        / denoms
    )
    zero_state = jnp.zeros_like(decay_rate)
    one_state = jnp.ones_like(decay_rate)
    factor = block_factor(params[5], length)
    following_numerator, following_denominator, spare_factor = carried_in(
        (jnp.sum(carried, axis=0), -jnp.sum(carried * mixed_out, axis=0), factor),
        "seq",
        chain_combine,
        (zero_state, zero_state, one_state),
        True,
    )
    (
        lookup_sensitivity,
        content_sensitivity,
        fading_sensitivity,
        reward_sensitivity,
        spare_placeholder,
        spare_placeholder,
    ) = token_mixer_backward((mixed_gradient, following_numerator, following_denominator))
    lookup_sensitivity = lookup_sensitivity.astype(jnp.bfloat16)
    content_sensitivity = content_sensitivity.astype(jnp.bfloat16)
    g_key = matmul_tn(mixed_key, lookup_sensitivity)
    g_value = matmul_tn(mixed_value, content_sensitivity)
    g_gate = matmul_tn(mixed_gate, d_gates_in)
    d_mixed_key = matmul_nt(lookup_sensitivity, square[0])
    d_mixed_value = matmul_nt(content_sensitivity, square[1])
    d_mixed_gate = matmul_nt(d_gates_in, square[2])
    d_stream, first_norm_gradient, first_share_gradient = norm_back(
        stream, incoming_one, params, 0, (2, 5), (d_mixed_key, d_mixed_value, d_mixed_gate)
    )
    d_stream = d_stream + d_middle
    g_square = jnp.stack([g_key, g_value, g_gate, g_output, g_chan_gate])
    g_params = jnp.concatenate(
        [
            first_norm_gradient,
            first_share_gradient,
            fading_sensitivity[None],
            reward_sensitivity[None],
            second_norm_gradient,
            second_share_gradient,
        ],
        axis=0,
    )
    return (d_stream, (g_square, g_expand, g_shrink, g_params))


def adam_update(weights, gradient, first, second, step_rate, decay_on):
    first_new = BETA_ONE * first + (1.0 - BETA_ONE) * gradient
    second_new = BETA_TWO * second + (1.0 - BETA_TWO) * gradient * gradient
    first_hat = first_new / (1.0 - BETA_ONE**STEP)
    second_hat = second_new / (1.0 - BETA_TWO**STEP)
    moved = first_hat / (jnp.sqrt(second_hat) + ADAM_EPS)
    if decay_on:
        moved = moved + WEIGHT_DECAY * weights
    return (weights - step_rate * moved, first_new, second_new)


def per_device(
    token_ids,
    targets,
    loss_mask,
    square_weights,
    expand_weights,
    shrink_weights,
    vector_params,
    embed_table,
    head_table,
    square_first,
    expand_first,
    shrink_first,
    vector_first,
    embed_first,
    head_first,
    square_second,
    expand_second,
    shrink_second,
    vector_second,
    embed_second,
    head_second,
):
    layers = square_weights.shape[0]
    global_rows = param_stride * layers
    total_tokens = token_ids.shape[0]

    vector_rows = vector_params.shape[0]
    square_own, expand_own, shrink_own = (
        square_weights.shape[2],
        expand_weights.shape[1],
        shrink_weights.shape[1],
    )

    def fetch_layer(layer_id):
        with_vectors = layer_id == 0
        shards = [
            square_weights[layer_id],
            expand_weights[layer_id][None],
            shrink_weights[layer_id][None],
        ]
        if with_vectors:
            shards.append(as_rows(vector_params))
        return gather_rows(
            shards,
            weight_portions(square_own, expand_own, shrink_own, with_vectors * square_own),
            layer_id,
        )

    fetched = [fetch_layer(layer_id) for layer_id in range(layers)]
    vectors_all = fetched[0][3][0, :, :vector_rows].T.astype(jnp.float32)
    global_params = vectors_all[global_rows:]
    blocks = [
        (
            fetched[layer_id][0],
            fetched[layer_id][1][0],
            fetched[layer_id][2][0],
            vectors_all[layer_id * param_stride : (layer_id + 1) * param_stride],
        )
        for layer_id in range(layers)
    ]

    columns = jnp.take(embed_table.astype(jnp.bfloat16), token_ids, axis=1)
    embedded = lax.all_to_all(
        columns, ("dp", "seq"), split_axis=1, concat_axis=0, tiled=True
    ).T.astype(jnp.float32)
    stream, norm_pull_zero = jax.vjp(layer_norm, embedded, global_params[0], global_params[1])
    saved_layers = []
    for layer_id in range(layers):
        stream, saved = layer_forward(stream, blocks[layer_id])
        saved_layers.append(saved)
    normed, norm_pull_last = jax.vjp(layer_norm, stream, global_params[2], global_params[3])
    dp_count = lax.axis_size("dp")
    features, vocab_own = head_table.shape
    vocab_part = vocab_own // dp_count
    head_cut = head_table.astype(jnp.bfloat16).reshape(features, dp_count, vocab_part)
    head_cols = lax.all_to_all(
        head_cut.transpose(1, 0, 2), "dp", split_axis=0, concat_axis=0, tiled=True
    ).reshape(dp_count * features, vocab_part)
    own_rows = normed.shape[0]
    rows_all = gather_rows([normed[None]], row_portions(own_rows), 10)[0][0]
    marks = lax.all_gather(jnp.stack([targets, loss_mask]), "dp", axis=1, tiled=True)
    first_column = lax.axis_index("seq") * vocab_own + lax.axis_index("dp") * vocab_part
    local_ids = marks[0] - first_column
    rows_per_block = min(logit_block, total_tokens)
    block_count = total_tokens // rows_per_block
    row_blocks = rows_all.reshape(block_count, rows_per_block, rows_all.shape[1])
    id_blocks = local_ids.reshape(block_count, rows_per_block)
    column_ids = jnp.arange(vocab_part, dtype=jnp.int32)[None, :]

    def block_stats(step_item):
        rows_now, ids_now = step_item
        logits = matmul(rows_now, head_cols)
        row_top = jnp.max(logits, axis=1)
        spread = jnp.sum(jnp.exp(logits - row_top[:, None]), axis=1)
        picked = jnp.sum(jnp.where(column_ids == ids_now[:, None], logits, 0.0), axis=1)
        return (row_top, spread, picked)

    stats = jnp.stack(lax.map(block_stats, (row_blocks, id_blocks))).reshape(3, total_tokens)
    stats_all = lax.all_gather(stats, ("dp", "seq"))
    row_top = jnp.max(stats_all[:, 0], axis=0)
    spread = jnp.sum(stats_all[:, 1] * jnp.exp(stats_all[:, 0] - row_top), axis=0)
    log_total = row_top + jnp.log(spread)
    counted = marks[1].astype(jnp.float32)
    losses = counted * (log_total - jnp.sum(stats_all[:, 2], axis=0))
    loss_all = jnp.sum(losses)
    weight_rows = counted / total_tokens

    def block_back(grad_head, step_item):
        rows_now, ids_now, log_now, weight_now = step_item
        logits = matmul(rows_now, head_cols)
        softmax_rows = jnp.exp(logits - log_now[:, None])
        hits = (column_ids == ids_now[:, None]).astype(jnp.float32)
        d_logits = ((softmax_rows - hits) * weight_now[:, None]).astype(jnp.bfloat16)
        return (grad_head + matmul_tn(rows_now, d_logits), matmul_nt(d_logits, head_cols).astype(jnp.bfloat16))

    grad_head, d_rows = lax.scan(
        block_back,
        jnp.zeros(head_cols.shape, jnp.float32),
        (
            row_blocks,
            id_blocks,
            log_total.reshape(block_count, rows_per_block),
            weight_rows.reshape(block_count, rows_per_block),
        ),
    )
    d_normed = scatter_rows(
        [d_rows.reshape(1, total_tokens, rows_all.shape[1])], row_portions(own_rows), 11
    )[0][0]
    g_head = (
        lax.all_to_all(
            grad_head.astype(jnp.bfloat16).reshape(dp_count, features, vocab_part),
            "dp",
            split_axis=0,
            concat_axis=0,
            tiled=True,
        )
        .transpose(1, 0, 2)
        .reshape(features, vocab_own)
        .astype(jnp.float32)
    )
    d_stream, d_gain_last, d_bias_last = norm_pull_last(d_normed)
    layer_grads = [None] * layers
    vector_grads = [None] * layers
    d_embedded = d_stream
    for layer_id in reversed(range(layers)):
        d_stream, grads = layer_backward(d_stream, saved_layers[layer_id], blocks[layer_id])
        vector_grads[layer_id] = grads[3]
        low_grads = [
            grads[0].astype(jnp.bfloat16),
            grads[1].astype(jnp.bfloat16)[None],
            grads[2].astype(jnp.bfloat16)[None],
        ]
        if layer_id == 0:
            d_embedded, d_gain_zero, d_bias_zero = norm_pull_zero(d_stream)
            all_vectors = jnp.concatenate(
                vector_grads
                + [jnp.stack([d_gain_zero, d_bias_zero, d_gain_last, d_bias_last])],
                axis=0,
            )
            low_grads.append(as_rows(all_vectors).astype(jnp.bfloat16))
        layer_grads[layer_id] = scatter_rows(
            low_grads,
            weight_portions(square_own, expand_own, shrink_own, (layer_id == 0) * square_own),
            layers + layer_id,
        )
    back_columns = lax.all_to_all(
        d_embedded.T.astype(jnp.bfloat16), ("dp", "seq"), split_axis=0, concat_axis=1, tiled=True
    )
    g_embed = jax.ops.segment_sum(
        back_columns.T.astype(jnp.float32), token_ids, num_segments=embed_table.shape[1]
    ).T
    g_square = jnp.stack([layer_grads[layer_id][0] for layer_id in range(layers)])
    g_expand = jnp.concatenate([layer_grads[layer_id][1] for layer_id in range(layers)])
    g_shrink = jnp.concatenate([layer_grads[layer_id][2] for layer_id in range(layers)])
    g_vector = layer_grads[0][3][0, :, :vector_rows].T
    gradients = (g_square, g_expand, g_shrink, g_vector, g_embed, g_head)
    square_part = jnp.zeros((), jnp.float32)
    for gradient in gradients:
        square_part = square_part + jnp.sum(gradient * gradient)
    loss_sum = loss_all
    square_sum = sum_everywhere(square_part, 12)
    grad_norm = jnp.sqrt(square_sum)
    scale = jnp.minimum(1.0, 0.5 / math.sqrt(total_tokens) / (grad_norm + 1e-06))
    weights = (
        square_weights,
        expand_weights,
        shrink_weights,
        vector_params,
        embed_table,
        head_table,
    )
    firsts = (square_first, expand_first, shrink_first, vector_first, embed_first, head_first)
    seconds = (
        square_second,
        expand_second,
        shrink_second,
        vector_second,
        embed_second,
        head_second,
    )
    updated = [
        adam_update(
            weights[slot],
            gradients[slot] * scale,
            firsts[slot],
            seconds[slot],
            LEARN_RATES[slot],
            DECAY_FLAGS[slot],
        )
        for slot in range(6)
    ]
    return (
        loss_sum,
        grad_norm,
        updated[0][0],
        updated[1][0],
        updated[2][0],
        updated[3][0],
        updated[4][0],
        updated[5][0],
        updated[0][1],
        updated[1][1],
        updated[2][1],
        updated[3][1],
        updated[4][1],
        updated[5][1],
        updated[0][2],
        updated[1][2],
        updated[2][2],
        updated[3][2],
        updated[4][2],
        updated[5][2],
    )


def solution(mesh):
    placed = (
        P(),
        P("dp"),
        P("dp"),
        P(None, None, ("dp", "seq"), None),
        P(None, ("dp", "seq"), None),
        P(None, ("dp", "seq"), None),
        P(None, ("dp", "seq")),
        P(("dp", "seq"), None),
        P("dp", "seq"),
        P(None, None, ("dp", "seq"), None),
        P(None, ("dp", "seq"), None),
        P(None, ("dp", "seq"), None),
        P(None, ("dp", "seq")),
        P(("dp", "seq"), None),
        P("dp", "seq"),
        P(None, None, ("dp", "seq"), None),
        P(None, ("dp", "seq"), None),
        P(None, ("dp", "seq"), None),
        P(None, ("dp", "seq")),
        P(("dp", "seq"), None),
        P("dp", "seq"),
    )
    return jax.shard_map(
        per_device,
        mesh=mesh,
        in_specs=placed,
        out_specs=(
            P(),
            P(),
            P(None, None, ("dp", "seq"), None),
            P(None, ("dp", "seq"), None),
            P(None, ("dp", "seq"), None),
            P(None, ("dp", "seq")),
            P(("dp", "seq"), None),
            P("dp", "seq"),
            P(None, None, ("dp", "seq"), None),
            P(None, ("dp", "seq"), None),
            P(None, ("dp", "seq"), None),
            P(None, ("dp", "seq")),
            P(("dp", "seq"), None),
            P("dp", "seq"),
            P(None, None, ("dp", "seq"), None),
            P(None, ("dp", "seq"), None),
            P(None, ("dp", "seq"), None),
            P(None, ("dp", "seq")),
            P(("dp", "seq"), None),
            P("dp", "seq"),
        ),
        check_vma=False,
    )
```

```python
import math

import jax
import jax.numpy as jnp
from jax import lax
from jax.experimental import pallas as pl
from jax.experimental.pallas import tpu as pltpu
from jax.sharding import PartitionSpec as P

STEP = 10
ON_MESH = pl.DeviceIdType.MESH


def place():
    dp, seq = lax.axis_index("dp"), lax.axis_index("seq")
    return dp, seq, dp // 2, lax.rem(dp, 2), seq // 2, lax.rem(seq, 2)


def greet(partners, extra):
    barrier = pltpu.get_barrier_semaphore()
    for partner in partners:
        pl.semaphore_signal(barrier, inc=1, device_id=partner, device_id_type=ON_MESH)
    for exists, partner in extra:
        @pl.when(exists)
        def _():
            pl.semaphore_signal(barrier, inc=1, device_id=partner, device_id_type=ON_MESH)
    peers = len(partners)
    for exists, partner in extra:
        peers = peers + exists.astype(jnp.int32)
    pl.semaphore_wait(barrier, peers)


class Sems:
    def __init__(self, send, recv, local):
        self.send, self.recv, self.local = send, recv, local
        self.ns = self.nr = self.nl = 0

    def pair(self):
        self.ns += 1
        return self.send.at[self.ns - 1], self.recv.at[self.ns - 1]

    def own(self):
        self.nl += 1
        return self.local.at[self.nl - 1]


def gather_blocks(tensors, portions, collective_id):
    count = len(tensors)
    dims = [t.shape for t in tensors]
    hops = 3
    pieces_total = sum(len(p) for p in portions)
    n_send = count + count + pieces_total * (1 + 2 * hops + 7)

    def kernel(*refs):
        ins, outs = refs[:count], refs[count : 2 * count]
        wide = refs[2 * count : 3 * count]
        half = refs[3 * count : 4 * count]
        send, recv, local = refs[4 * count :]
        dp, seq, z, y, x, c = place()
        core = (dp, seq + 1 - 2 * c)
        xway = (dp, seq + 2 - 4 * x)
        yway = (dp + 1 - 2 * y, seq)
        up, down = (dp + 2, seq), (dp - 2, seq)
        has_up, has_down = z < hops, z > 0
        greet([core, xway, yway], [(has_up, up), (has_down, down)])
        sems = Sems(send, recv, local)

        def cols(t, side):
            width = dims[t][2] // 2
            return pl.ds(pl.multiple_of(side * width, 128), width)

        first = []
        for t in range(count):
            rows = pl.ds(pl.multiple_of(c * dims[t][1], 8), dims[t][1])
            mine = pltpu.make_async_copy(ins[t].at[:, :, cols(t, c)], wide[t].at[:, rows, :], sems.own())
            ss, rs = sems.pair()
            other = pltpu.make_async_remote_copy(
                src_ref=ins[t].at[:, :, cols(t, 1 - c)], dst_ref=wide[t].at[:, rows, :],
                send_sem=ss, recv_sem=rs, device_id=core, device_id_type=ON_MESH)
            other.start()
            mine.start()
            first.append((mine, other))
        core_sems = [sems.pair() for t in range(count)]
        stay = []
        for t in range(count):
            first[t][0].wait()
            first[t][1].wait()
            half[t][...] = wide[t][...].astype(jnp.bfloat16)
            own = pltpu.make_async_copy(half[t], outs[t].at[:, z, y, x, :, cols(t, c)], sems.own())
            own.start()
            stay.append(own)

        def block(piece, zz, yy, xx):
            t, m0, m1, r0, r1 = piece
            return outs[t].at[m0:m1, zz, yy, xx, r0:r1, cols(t, c)]

        def to_core(p, zz, yy, xx, source=None):
            for piece in portions[p]:
                t = piece[0]
                region = block(piece, zz, yy, xx)
                pltpu.make_async_remote_copy(
                    src_ref=region if source is None else source(piece), dst_ref=region,
                    send_sem=core_sems[t][0], recv_sem=core_sems[t][1], device_id=core, device_id_type=ON_MESH).start()

        def message(p, where, device, source=None):
            copies = []
            for piece in portions[p]:
                ss, rs = sems.pair()
                region = block(piece, *where)
                copies.append(pltpu.make_async_remote_copy(
                    src_ref=region if source is None else source(piece), dst_ref=region,
                    send_sem=ss, recv_sem=rs, device_id=device, device_id_type=ON_MESH))
            return copies

        def start(copies):
            for copy in copies:
                copy.start()

        def arrive(copies):
            for copy in copies:
                copy.wait_recv()

        def sent(copies):
            for copy in copies:
                copy.wait_send()

        def from_half(piece):
            t, m0, m1, r0, r1 = piece
            return half[t].at[m0:m1, r0:r1, :]

        both = slice(0, 2)
        a_way, b_way = (yway, xway), (xway, yway)
        a_msgs = []
        for p in range(2):
            msg = message(p, (z, y, x), a_way[p], from_half)
            start(msg)
            a_msgs.append(msg)
        for own in stay:
            own.wait()
        for p in range(2):
            to_core(p, z, y, x, from_half)

        def pair_of(p, zz):
            return (zz, both, x) if p == 0 else (zz, y, both)

        def other_of(p, zz):
            return (zz, 1 - y, x) if p == 0 else (zz, y, 1 - x)

        def far_of(p, zz):
            return (zz, both, 1 - x) if p == 0 else (zz, 1 - y, both)

        zmsg = [[[message(p, pair_of(p, z - k), up) for k in range(hops)],
                 [message(p, pair_of(p, z + k), down) for k in range(hops)]] for p in range(2)]
        b_msgs = []
        for p in range(2):
            own = message(p, pair_of(p, z), b_way[p])
            ups = [message(p, pair_of(p, z - 1 - k), b_way[p]) for k in range(hops)]
            downs = [message(p, pair_of(p, z + 1 + k), b_way[p]) for k in range(hops)]
            b_msgs.append((own, ups, downs))

        for p in range(2):
            arrive(a_msgs[p])

            @pl.when(has_up)
            def _():
                start(zmsg[p][0][0])

            @pl.when(has_down)
            def _():
                start(zmsg[p][1][0])
            start(b_msgs[p][0])
            to_core(p, *other_of(p, z))

        def far_own(p):
            arrive(b_msgs[p][0])
            to_core(p, *far_of(p, z))

        def far_hop(p, k):
            @pl.when(z - 1 - k >= 0)
            def _():
                arrive(b_msgs[p][1][k])
                to_core(p, *far_of(p, z - 1 - k))

            @pl.when(z + 1 + k <= hops)
            def _():
                arrive(b_msgs[p][2][k])
                to_core(p, *far_of(p, z + 1 + k))

        for k in range(hops):
            for p in range(2):
                @pl.when(z - 1 - k >= 0)
                def _():
                    arrive(zmsg[p][0][k])
                    if k + 1 < hops:
                        @pl.when(has_up)
                        def _():
                            start(zmsg[p][0][k + 1])
                    start(b_msgs[p][1][k])
                    to_core(p, *pair_of(p, z - 1 - k))

                @pl.when(z + 1 + k <= hops)
                def _():
                    arrive(zmsg[p][1][k])
                    if k + 1 < hops:
                        @pl.when(has_down)
                        def _():
                            start(zmsg[p][1][k + 1])
                    start(b_msgs[p][2][k])
                    to_core(p, *pair_of(p, z + 1 + k))
            for p in range(2):
                if k == 0:
                    far_own(p)
                else:
                    far_hop(p, k - 1)
        for p in range(2):
            far_hop(p, hops - 1)

        for p in range(2):
            sent(a_msgs[p])
            sent(b_msgs[p][0])
            for k in range(hops):
                @pl.when((z - k >= 0) & has_up)
                def _():
                    sent(zmsg[p][0][k])

                @pl.when((z + k <= hops) & has_down)
                def _():
                    sent(zmsg[p][1][k])

                @pl.when(z - 1 - k >= 0)
                def _():
                    sent(b_msgs[p][1][k])

                @pl.when(z + 1 + k <= hops)
                def _():
                    sent(b_msgs[p][2][k])
        for t in range(count):
            whole = pltpu.make_async_remote_copy(
                src_ref=outs[t].at[:, :, :, :, :, cols(t, c)], dst_ref=outs[t].at[:, :, :, :, :, cols(t, 1 - c)],
                send_sem=core_sems[t][0], recv_sem=core_sems[t][1], device_id=core, device_id_type=ON_MESH)
            whole.wait_send()
            whole.wait_recv()

    outs = pl.pallas_call(
        kernel,
        out_shape=[jax.ShapeDtypeStruct((m, hops + 1, 2, 2, 2 * r, w), jnp.bfloat16) for m, r, w in dims],
        in_specs=[pl.BlockSpec(memory_space=pl.ANY)] * count,
        out_specs=[pl.BlockSpec(memory_space=pl.ANY)] * count,
        scratch_shapes=[pltpu.VMEM((m, 2 * r, w // 2), jnp.float32) for m, r, w in dims]
        + [pltpu.VMEM((m, 2 * r, w // 2), jnp.bfloat16) for m, r, w in dims]
        + [pltpu.SemaphoreType.DMA((n_send,)), pltpu.SemaphoreType.DMA((n_send,)), pltpu.SemaphoreType.DMA((2 * count,))],
        compiler_params=pltpu.CompilerParams(collective_id=collective_id, has_side_effects=True, vmem_limit_bytes=40 << 20),
    )(*tensors)
    return [o.reshape(m, (hops + 1) * 8 * r, w) for o, (m, r, w) in zip(outs, dims)]


def scatter_blocks(tensors, portions, rows_own, collective_id):
    count = len(tensors)
    hops = 3
    dims = [(t.shape[0], r, t.shape[2]) for t, r in zip(tensors, rows_own)]
    views = [t.reshape(m, hops + 1, 2, 2, 2 * r, w) for t, (m, r, w) in zip(tensors, dims)]
    pieces_total = sum(len(p) for p in portions)
    n_send = pieces_total * (2 + 4 + 2 * hops + 1) + count
    n_local = pieces_total * 2 + count
    flat = [(p, piece) for p in range(2) for piece in portions[p]]
    flat_dims = [(piece[2] - piece[1], piece[4] - piece[3], dims[piece[0]][2] // 2) for _, piece in flat]

    def kernel(*refs):
        ins, outs = refs[:count], refs[count : 2 * count]
        k0 = 2 * count
        acc = refs[k0 : k0 + count]
        crecv = refs[k0 + count : k0 + 2 * count]
        fin = refs[k0 + 2 * count : k0 + 3 * count]
        k0 += 3 * count
        n = len(flat)
        b_all, u_all, d_all, a_all = (refs[k0 + i * n : k0 + (i + 1) * n] for i in range(4))
        send, recv, local = refs[k0 + 4 * n :]
        index = {}
        for i, (p, piece) in enumerate(flat):
            index.setdefault(p, []).append((i, piece))
        dp, seq, z, y, x, c = place()
        core = (dp, seq + 1 - 2 * c)
        xway = (dp, seq + 2 - 4 * x)
        yway = (dp + 1 - 2 * y, seq)
        up, down = (dp + 2, seq), (dp - 2, seq)
        has_up, has_down = z < hops, z > 0
        greet([core, xway, yway], [(has_up, up), (has_down, down)])
        sems = Sems(send, recv, local)
        a_way, b_way = (yway, xway), (xway, yway)

        def cols(t, side):
            width = dims[t][2] // 2
            return pl.ds(pl.multiple_of(side * width, 128), width)

        def remote(src, dst, device):
            ss, rs = sems.pair()
            return pltpu.make_async_remote_copy(src_ref=src, dst_ref=dst, send_sem=ss, recv_sem=rs,
                                                device_id=device, device_id_type=ON_MESH)

        def place_of(p, zz, a, b):
            return (zz, a, b) if p == 0 else (zz, b, a)

        own_a, own_b = (y, x), (x, y)

        def add(dst, src, lead):
            def turn(i, _):
                where, rest = [], i
                for size in reversed(lead):
                    where.append(lax.rem(rest, size))
                    rest = rest // size
                where = tuple(reversed(where))
                dst[where] = (dst[where].astype(jnp.float32) + src[where].astype(jnp.float32)).astype(dst.dtype)
                return 0
            total = 1
            for size in lead:
                total *= size
            lax.fori_loop(0, total, turn, 0)

        everyz, both = slice(0, hops + 1), slice(0, 2)
        chunks = {}
        for far in (1, 0):
            for p in range(2):
                b = own_b[p] if far == 0 else 1 - own_b[p]
                made = []
                for i, piece in index[p]:
                    t, m0, m1, r0, r1 = piece
                    where = (slice(m0, m1),) + place_of(p, everyz, both, b) + (slice(r0, r1),)
                    there = remote(ins[t].at[where + (cols(t, 1 - c),)], crecv[t].at[where], core)
                    here = pltpu.make_async_copy(ins[t].at[where + (cols(t, c),)], acc[t].at[where], sems.own())
                    there.start()
                    here.start()
                    made.append((there, here, piece, where))
                chunks[far, p] = made

        def core_add(far, p):
            for there, here, piece, where in chunks[far, p]:
                t, m0, m1, r0, r1 = piece
                there.wait_recv()
                here.wait()
                add(acc[t].at[where], crecv[t].at[where], (m1 - m0, hops + 1, 2))

        zorder = (3, 0, 2, 1)
        b_msgs = {}
        for p in range(2):
            core_add(1, p)
            for zz in zorder:
                msgs = []
                for i, (t, m0, m1, r0, r1) in index[p]:
                    src = acc[t].at[(slice(m0, m1),) + place_of(p, zz, both, 1 - own_b[p]) + (slice(r0, r1),)]
                    msgs.append(remote(src, b_all[i].at[:, zz], b_way[p]))
                for msg in msgs:
                    msg.start()
                b_msgs[p, zz] = msgs
        for p in range(2):
            core_add(0, p)

        def b_add(p, zz):
            for msg in b_msgs[p, zz]:
                msg.wait_recv()
            for i, (t, m0, m1, r0, r1) in index[p]:
                dst = acc[t].at[(slice(m0, m1),) + place_of(p, zz, both, own_b[p]) + (slice(r0, r1),)]
                add(dst, b_all[i].at[:, zz], (m1 - m0, 2))

        def mine(p, i, piece, zz):
            t, m0, m1, r0, r1 = piece
            return acc[t].at[(slice(m0, m1),) + place_of(p, zz, both, own_b[p]) + (slice(r0, r1),)]

        up_msgs, down_msgs = {}, {}
        for p in range(2):
            for zz in range(hops + 1):
                up_msgs[p, zz] = [remote(mine(p, i, piece, zz), u_all[i].at[:, zz], up) for i, piece in index[p]] if zz > 0 else None
                down_msgs[p, zz] = [remote(mine(p, i, piece, zz), d_all[i].at[:, zz], down) for i, piece in index[p]] if zz < hops else None

        def z_add(p, zz, msgs, land):
            for msg in msgs[p, zz]:
                msg.wait_recv()
            for i, piece in index[p]:
                add(mine(p, i, piece, zz), land[i].at[:, zz], (piece[2] - piece[1], 2))

        def up_send(p, zz):
            @pl.when(z < zz)
            def _():
                @pl.when(z > 0)
                def _():
                    z_add(p, zz, up_msgs, u_all)
                for msg in up_msgs[p, zz]:
                    msg.start()

        def down_send(p, zz):
            @pl.when(z > zz)
            def _():
                @pl.when(z < hops)
                def _():
                    z_add(p, zz, down_msgs, d_all)
                for msg in down_msgs[p, zz]:
                    msg.start()

        for p in range(2):
            b_add(p, 3)
            up_send(p, 3)
            b_add(p, 0)
            down_send(p, 0)
        for p in range(2):
            b_add(p, 2)
            up_send(p, 2)
            b_add(p, 1)
            down_send(p, 1)
        for p in range(2):
            up_send(p, 1)
            down_send(p, 2)
        a_msgs = {}
        for p in range(2):
            for zz in range(hops + 1):
                @pl.when(z == zz)
                def _():
                    if zz > 0:
                        z_add(p, zz, up_msgs, u_all)
                    if zz < hops:
                        z_add(p, zz, down_msgs, d_all)
            msgs = []
            for i, (t, m0, m1, r0, r1) in index[p]:
                src = acc[t].at[(slice(m0, m1),) + place_of(p, z, 1 - own_a[p], own_b[p]) + (slice(r0, r1),)]
                msgs.append(remote(src, a_all[i], a_way[p]))
            for msg in msgs:
                msg.start()
            a_msgs[p] = msgs
        for p in range(2):
            for msg in a_msgs[p]:
                msg.wait_recv()
            for i, (t, m0, m1, r0, r1) in index[p]:
                for m in range(m0, m1):
                    part = acc[t][(m,) + place_of(p, z, own_a[p], own_b[p]) + (slice(r0, r1),)]
                    fin[t][m, r0:r1, :] = part.astype(jnp.float32) + a_all[i][m - m0].astype(jnp.float32)
        last = []
        for t in range(count):
            r = dims[t][1]
            other = remote(fin[t].at[:, pl.ds(pl.multiple_of((1 - c) * r, 8), r), :], outs[t].at[:, :, cols(t, c)], core)
            keep = pltpu.make_async_copy(fin[t].at[:, pl.ds(pl.multiple_of(c * r, 8), r), :], outs[t].at[:, :, cols(t, c)], sems.own())
            other.start()
            keep.start()
            last.append((other, keep))
        for made in chunks.values():
            for there, here, piece, where in made:
                there.wait_send()
        for msgs in list(b_msgs.values()) + list(a_msgs.values()):
            for msg in msgs:
                msg.wait_send()
        for p in range(2):
            for zz in range(hops + 1):
                if zz > 0:
                    @pl.when(z < zz)
                    def _():
                        for msg in up_msgs[p, zz]:
                            msg.wait_send()
                if zz < hops:
                    @pl.when(z > zz)
                    def _():
                        for msg in down_msgs[p, zz]:
                            msg.wait_send()
        for other, keep in last:
            keep.wait()
            other.wait()

    bf = jnp.bfloat16
    outs = pl.pallas_call(
        kernel,
        out_shape=[jax.ShapeDtypeStruct((m, r, w), jnp.float32) for m, r, w in dims],
        in_specs=[pl.BlockSpec(memory_space=pl.ANY)] * count,
        out_specs=[pl.BlockSpec(memory_space=pl.ANY)] * count,
        scratch_shapes=[pltpu.VMEM((m, hops + 1, 2, 2, 2 * r, w // 2), bf) for m, r, w in dims]
        + [pltpu.VMEM((m, hops + 1, 2, 2, 2 * r, w // 2), bf) for m, r, w in dims]
        + [pltpu.VMEM((m, 2 * r, w // 2), jnp.float32) for m, r, w in dims]
        + [pltpu.VMEM((m, hops + 1, 2, r, w), bf) for m, r, w in flat_dims] * 3
        + [pltpu.VMEM((m, r, w), bf) for m, r, w in flat_dims]
        + [pltpu.SemaphoreType.DMA((n_send,)), pltpu.SemaphoreType.DMA((n_send,)), pltpu.SemaphoreType.DMA((n_local,))],
        compiler_params=pltpu.CompilerParams(collective_id=collective_id, has_side_effects=True, vmem_limit_bytes=50 << 20),
    )(*views)
    return list(lax.optimization_barrier(outs))


def exchange_everywhere(value, combine, collective_id):
    sizes = (("dp", lax.axis_size("dp")), ("seq", lax.axis_size("seq")))
    steps = [(axis, 1 << bit) for axis, size in reversed(sizes) for bit in range(size.bit_length() - 1)]

    def kernel(in_ref, out_ref, leave, land, send, recv):
        dp, seq = lax.axis_index("dp"), lax.axis_index("seq")
        partners = []
        for axis, step in steps:
            mine = dp if axis == "dp" else seq
            other = mine + step - 2 * step * lax.rem(mine // step, 2)
            partners.append((other, seq) if axis == "dp" else (dp, other))
        greet(partners, [])
        leave[0] = in_ref[...]
        for k, partner in enumerate(partners):
            copy = pltpu.make_async_remote_copy(
                src_ref=leave.at[k],
                dst_ref=land.at[k],
                send_sem=send.at[k],
                recv_sem=recv.at[k],
                device_id=partner,
                device_id_type=ON_MESH,
            )
            copy.start()
            copy.wait()
            both = combine(leave[k], land[k])
            if k + 1 < len(steps):
                leave[k + 1] = both
            else:
                out_ref[...] = both

    n = len(steps)
    return pl.pallas_call(
        kernel,
        out_shape=jax.ShapeDtypeStruct(value.shape, jnp.float32),
        in_specs=[pl.BlockSpec(memory_space=pltpu.VMEM)],
        out_specs=pl.BlockSpec(memory_space=pltpu.VMEM),
        scratch_shapes=[
            pltpu.VMEM((n,) + value.shape, jnp.float32),
            pltpu.VMEM((n,) + value.shape, jnp.float32),
            pltpu.SemaphoreType.DMA((n,)),
            pltpu.SemaphoreType.DMA((n,)),
        ],
        compiler_params=pltpu.CompilerParams(collective_id=collective_id, has_side_effects=True),
    )(value)


def add_logs(left, right):
    return jnp.maximum(left, right) + jnp.log(1.0 + jnp.exp(-jnp.abs(left - right)))


def head_forward(rows_all, head_cols, local_ids, tile, sub):
    tokens, features = rows_all.shape
    width = head_cols.shape[1]

    def kernel(rows_ref, head_ref, ids_ref, p_ref, stats_ref):
        ids = jnp.transpose(jnp.broadcast_to(ids_ref[...], (128, tile)))[:, :1]
        lane = lax.broadcasted_iota(jnp.int32, (sub, 128), 1)
        column = lax.broadcasted_iota(jnp.int32, (sub, width), 1)
        for part in range(tile // sub):
            here = slice(part * sub, (part + 1) * sub)
            logits = jnp.dot(rows_ref[here, :], head_ref[...], preferred_element_type=jnp.float32)
            top = jnp.max(logits, axis=1, keepdims=True)
            picked = jnp.sum(jnp.where(column == ids[here], logits, 0.0), axis=1, keepdims=True)
            lifted = jnp.exp(logits - top)
            spread = jnp.sum(lifted, axis=1, keepdims=True)
            p_ref[here, :] = lifted.astype(jnp.bfloat16)
            table = jnp.where(lane == 0, top, jnp.where(lane == 1, spread, picked))
            stats_ref[:, here] = jnp.transpose(table)[:8]

    return pl.pallas_call(
        kernel,
        grid=(tokens // tile,),
        out_shape=[
            jax.ShapeDtypeStruct((tokens, width), jnp.bfloat16),
            jax.ShapeDtypeStruct((8, tokens), jnp.float32),
        ],
        in_specs=[
            pl.BlockSpec((tile, features), lambda i: (i, 0)),
            pl.BlockSpec((features, width), lambda i: (0, 0)),
            pl.BlockSpec((1, tile), lambda i: (0, i)),
        ],
        out_specs=[
            pl.BlockSpec((tile, width), lambda i: (i, 0)),
            pl.BlockSpec((8, tile), lambda i: (0, i)),
        ],
        compiler_params=pltpu.CompilerParams(vmem_limit_bytes=50 << 20),
    )(rows_all, head_cols, local_ids[None])


def head_backward(lifted, rows_all, head_cols, local_ids, factors, tile, sub):
    tokens, width = lifted.shape
    features = rows_all.shape[1]
    steps = tokens // tile

    def kernel(p_ref, rows_ref, head_ref, ids_ref, factor_ref, d_rows_ref, d_head_ref, squares_ref, d_logits, total):
        step = pl.program_id(0)
        ids = jnp.transpose(jnp.broadcast_to(ids_ref[...], (128, tile)))[:, :1]
        scales = jnp.transpose(jnp.concatenate([factor_ref[...]] * 16, axis=0))
        scale, hit = scales[:, :1], scales[:, 1:2]
        column = lax.broadcasted_iota(jnp.int32, (sub, width), 1)
        for part in range(tile // sub):
            here = slice(part * sub, (part + 1) * sub)
            d_logits[here, :] = jnp.where(
                column == ids[here], hit[here], p_ref[here, :].astype(jnp.float32) * scale[here]
            ).astype(jnp.bfloat16)
            d_rows_ref[here, :] = lax.dot_general(
                d_logits[here, :], head_ref[...], (((1,), (1,)), ((), ())), preferred_element_type=jnp.float32
            ).astype(jnp.bfloat16)
        term = lax.dot_general(
            rows_ref[...], d_logits[...], (((0,), (0,)), ((), ())), preferred_element_type=jnp.float32
        )

        @pl.when(step == 0)
        def _():
            total[...] = term

        @pl.when(step > 0)
        def _():
            total[...] += term

        @pl.when(step == steps - 1)
        def _():
            low = total[...].astype(jnp.bfloat16)
            d_head_ref[...] = low
            wide = low.astype(jnp.float32)
            squares_ref[...] = jnp.sum((wide * wide).reshape(features // 8, 8, width), axis=0)

    return pl.pallas_call(
        kernel,
        grid=(steps,),
        out_shape=[
            jax.ShapeDtypeStruct((tokens, features), jnp.bfloat16),
            jax.ShapeDtypeStruct((features, width), jnp.bfloat16),
            jax.ShapeDtypeStruct((8, width), jnp.float32),
        ],
        in_specs=[
            pl.BlockSpec((tile, width), lambda i: (i, 0)),
            pl.BlockSpec((tile, features), lambda i: (i, 0)),
            pl.BlockSpec((features, width), lambda i: (0, 0)),
            pl.BlockSpec((1, tile), lambda i: (0, i)),
            pl.BlockSpec((8, tile), lambda i: (0, i)),
        ],
        out_specs=[
            pl.BlockSpec((tile, features), lambda i: (i, 0)),
            pl.BlockSpec((features, width), lambda i: (0, 0)),
            pl.BlockSpec((8, width), lambda i: (0, 0)),
        ],
        scratch_shapes=[pltpu.VMEM((tile, width), jnp.bfloat16), pltpu.VMEM((features, width), jnp.float32)],
        compiler_params=pltpu.CompilerParams(vmem_limit_bytes=56 << 20),
    )(lifted, rows_all, head_cols, local_ids[None], factors)


def embed_gradient(columns, token_ids, vocab, block):
    features, tokens = columns.shape
    lanes = 128
    high_rows = -(-vocab // (8 * lanes)) * 8
    group = 2
    steps = tokens // block

    def kernel(columns_ref, ids_ref, out_ref, squares_ref):
        step = pl.program_id(0)
        ids = ids_ref[...]
        high = lax.broadcasted_iota(jnp.int32, (high_rows, block), 0) == lax.shift_right_logical(ids, 7)
        high = jnp.where(high, 1.0, 0.0).astype(jnp.bfloat16)
        low = lax.broadcasted_iota(jnp.int32, (lanes, block), 0) == jnp.bitwise_and(ids, lanes - 1)
        values = columns_ref[...].astype(jnp.float32)

        @pl.when(step == 0)
        def _():
            out_ref[...] = jnp.zeros_like(out_ref)

        for first in range(0, features, group):
            spread = jnp.concatenate(
                [jnp.where(low, values[f : f + 1], 0.0).astype(jnp.bfloat16) for f in range(first, first + group)], axis=0
            )
            term = lax.dot_general(high, spread, (((1,), (1,)), ((), ())), preferred_element_type=jnp.float32)
            for k in range(group):
                out_ref[first + k] += term[:, k * lanes : (k + 1) * lanes]

        @pl.when(step == steps - 1)
        def _():
            def turn(f, total):
                one = out_ref[f]
                return total + jnp.sum((one * one).reshape(high_rows // 8, 8, lanes), axis=0)
            squares_ref[...] = lax.fori_loop(0, features, turn, jnp.zeros((8, lanes), jnp.float32))

    sums, squares = pl.pallas_call(
        kernel,
        grid=(steps,),
        out_shape=[
            jax.ShapeDtypeStruct((features, high_rows, lanes), jnp.float32),
            jax.ShapeDtypeStruct((8, lanes), jnp.float32),
        ],
        in_specs=[pl.BlockSpec((features, block), lambda i: (0, i)), pl.BlockSpec((1, block), lambda i: (0, i))],
        out_specs=[
            pl.BlockSpec((features, high_rows, lanes), lambda i: (0, 0, 0)),
            pl.BlockSpec((8, lanes), lambda i: (0, 0)),
        ],
        compiler_params=pltpu.CompilerParams(vmem_limit_bytes=50 << 20),
    )(columns, token_ids[None])
    return sums[:, : vocab // lanes].reshape(features, vocab), squares


BOTH = ("dp", "seq")
mark_height = 8


def mark_rows(targets, loss_mask):
    own = targets.shape[0] // lax.axis_size("seq")
    first = lax.axis_index("seq") * own
    own_targets = lax.dynamic_slice_in_dim(targets, first, own)
    own_mask = lax.dynamic_slice_in_dim(loss_mask, first, own)
    rows = jnp.stack([own_targets // 256, own_targets % 256, own_mask]).astype(jnp.float32)
    return jnp.pad(rows, ((0, mark_height - 3), (0, 0)))[None]


def marks_of(gathered):
    rows = gathered[0].reshape(-1, mark_height, gathered.shape[2]).astype(jnp.float32)
    numbers = rows[:, :3].transpose(1, 0, 2).reshape(3, -1).astype(jnp.int32)
    return (numbers[0] * 256 + numbers[1], numbers[2])


def on_box():
    return lax.axis_size("dp") == 8 and lax.axis_size("seq") == 4


def gather_rows(tensors, portions, collective_id):
    if on_box():
        return gather_blocks(tensors, portions, collective_id)
    return gather_plain(tensors)


def gather_plain(tensors):
    return [lax.all_gather(t.astype(jnp.bfloat16), BOTH, axis=1, tiled=True) for t in tensors]


def scatter_rows(tensors, portions, collective_id):
    if on_box():
        devices = lax.axis_size("dp") * lax.axis_size("seq")
        rows = [t.shape[1] // devices for t in tensors]
        return scatter_blocks(tensors, portions, rows, collective_id)
    return scatter_plain(tensors)


def scatter_plain(tensors):
    return [
        lax.psum_scatter(t, BOTH, scatter_dimension=1, tiled=True).astype(jnp.float32) for t in tensors
    ]


def scatter_joined(tensors):
    square, expand, shrink = tensors
    width = square.shape[2]
    cut = [expand[:, :, k : k + width] for k in range(0, expand.shape[2], width)]
    both = lax.psum_scatter(
        jnp.concatenate([square] + cut), BOTH, scatter_dimension=1, tiled=True
    ).astype(jnp.float32)
    count = square.shape[0]
    return [
        both[:count],
        jnp.concatenate([both[k : k + 1] for k in range(count, both.shape[0])], axis=2),
        lax.psum_scatter(shrink, BOTH, scatter_dimension=1, tiled=True).astype(jnp.float32),
    ]


def weight_portions(square, expand, shrink, vectors, marks=0):
    first = [(1, 0, 1, 0, 2 * expand), (0, 0, 3, 0, 2 * square)]
    second = [(2, 0, 1, 0, 2 * shrink), (0, 3, 5, 0, 2 * square)]
    if vectors:
        second.append((3, 0, 1, 0, 2 * vectors))
    if marks:
        first.append((4, 0, 1, 0, 2 * marks))
    return [first, second]


def row_portions(rows):
    return [[(0, 0, 1, 0, rows)], [(0, 0, 1, rows, 2 * rows)]]


def as_rows(vectors):
    lanes = -(-vectors.shape[0] // 256) * 256
    return jnp.pad(vectors.T, ((0, 0), (0, lanes - vectors.shape[0])))[None]

EXACT_MATMUL = lax.Precision.HIGHEST
BETA_ONE = 0.9
BETA_TWO = 0.999
ADAM_EPS = 1e-08
WEIGHT_DECAY = 0.01
LEARN_RATES = (0.03, 0.03, 0.015, 0.5, 2.0, 0.05)
DECAY_FLAGS = (True, True, True, False, True, True)
param_stride = 11
head_tile = 1024
embed_block = 1024
scan_block = 256


def from_behind(value, axis, steps):
    count = lax.axis_size(axis)
    leading, last = (max(0, -steps), min(count, count - steps))
    return lax.ppermute(value, axis, [(source, source + steps) for source in range(leading, last)])


def carried_in(value, axis, join, neutral, backward):
    count, mine = (lax.axis_size(axis), lax.axis_index(axis))
    pieces = lax.all_gather(jnp.stack(value), axis)
    if backward:
        pieces = pieces[::-1]
        mine = count - 1 - mine
    running = neutral
    for position in range(count - 1):
        longer = join(running, tuple(pieces[position]))
        running = tuple(
            jnp.where(position < mine, new, old) for new, old in zip(longer, running)
        )
    return running


def layer_norm(values, gain, bias):
    centre = values - jnp.mean(values, axis=-1, keepdims=True)
    spread = jnp.mean(centre * centre, axis=-1, keepdims=True)
    return centre * lax.rsqrt(spread + 1e-05) * gain + bias


def matmul(left, right):
    return jnp.dot(left, right, preferred_element_type=jnp.float32)


def matmul_tn(left, right):
    return lax.dot_general(
        left, right, (((0,), (0,)), ((), ())), preferred_element_type=jnp.float32
    )


def matmul_nt(left, right):
    return lax.dot_general(
        left, right, (((1,), (1,)), ((), ())), preferred_element_type=jnp.float32
    )


def blend_all(normed, incoming, shares):
    earlier = jnp.concatenate([incoming, normed[:-1]], axis=0)
    return tuple(
        (
            normed * shares[member] + earlier * (1.0 - shares[member])
            for member in range(shares.shape[0])
        )
    )


def take_previous(normed):
    return from_behind(normed[-1:], "seq", 1)


def give_back(grad_first):
    return from_behind(grad_first, "seq", -1)


def block_ends(arriving_lookups, arriving_contents, logarithmic_fading_speed):
    decay_rate = jnp.exp(logarithmic_fading_speed)
    length = arriving_lookups.shape[0]
    ages = (length - 1.0 - jnp.arange(length, dtype=jnp.float32))[:, None]
    weight = jnp.exp(arriving_lookups - decay_rate * ages)
    return (jnp.sum(weight * arriving_contents, axis=0), jnp.sum(weight, axis=0))


def block_factor(logarithmic_fading_speed, length):
    return jnp.exp(-jnp.exp(logarithmic_fading_speed) * length)


def chain_combine(earlier, later):
    return (
        earlier[0] * later[2] + later[0],
        earlier[1] * later[2] + later[1],
        earlier[2] * later[2],
    )


def token_mixer_block(
    arriving_lookups,
    arriving_contents,
    logarithmic_fading_speed,
    present_reward,
    initial_numerator,
    initial_denominator,
):
    decay_rate = jnp.exp(logarithmic_fading_speed)
    length, channels = arriving_lookups.shape
    block_size = min(scan_block, length)
    block_count = length // block_size
    offsets = jnp.arange(block_size, dtype=jnp.float32)[:, None]
    lower_mask = (offsets > offsets.T).astype(jnp.float32)
    diagonal_amplifier = jnp.exp(present_reward)
    back_decay = jnp.exp(-decay_rate * (offsets - 1.0))
    carry_decay = jnp.exp(-decay_rate * offsets)
    tail_decay = jnp.exp(-decay_rate * (block_size - 1.0))
    full_decay = jnp.exp(-decay_rate * block_size)

    def sub_block(state, step_item):
        numerator, denominator = state
        key_block, value_block = step_item
        lifted = jnp.exp(key_block + decay_rate * offsets)
        prefix_sums = jnp.dot(
            lower_mask,
            jnp.concatenate([lifted * value_block, lifted], axis=1),
            precision=EXACT_MATMUL,
        )
        own_term = diagonal_amplifier * jnp.exp(key_block)
        top_part = (
            back_decay * prefix_sums[:, :channels]
            + carry_decay * numerator
            + own_term * value_block
        )
        low_part = back_decay * prefix_sums[:, channels:] + carry_decay * denominator + own_term
        next_num = tail_decay * jnp.sum(lifted * value_block, axis=0) + full_decay * numerator
        next_den = tail_decay * jnp.sum(lifted, axis=0) + full_decay * denominator
        return ((next_num, next_den), (top_part / low_part, low_part))

    shaped = (
        arriving_lookups.reshape(block_count, block_size, channels),
        arriving_contents.reshape(block_count, block_size, channels),
    )
    (end_num, end_den), (block_outs, denoms) = lax.scan(
        sub_block, (initial_numerator, initial_denominator), shaped
    )
    return (
        (block_outs.reshape(length, channels), end_num, end_den),
        denoms.reshape(length, channels),
    )


def layer_forward(stream, gathered):
    square, expand, shrink, params = gathered
    normed = layer_norm(stream, params[0], params[1])
    incoming_one = take_previous(normed)
    blended = blend_all(normed, incoming_one, params[2:5])
    mixed_key = blended[0].astype(jnp.bfloat16)
    mixed_value = blended[1].astype(jnp.bfloat16)
    mixed_gate = blended[2].astype(jnp.bfloat16)
    arriving_lookups = matmul(mixed_key, square[0])
    arriving_contents = matmul(mixed_value, square[1])
    gates_in = matmul(mixed_gate, square[2])
    length = arriving_lookups.shape[0]
    end_sums = block_ends(arriving_lookups, arriving_contents, params[5])
    zero_state = jnp.zeros_like(end_sums[0])
    one_state = jnp.ones_like(end_sums[0])
    factor = block_factor(params[5], length)
    initial_numerator, initial_denominator, spare_factor = carried_in(
        (end_sums[0], end_sums[1], factor),
        "seq",
        chain_combine,
        (zero_state, zero_state, one_state),
        False,
    )
    (mixed_out, spare_placeholder, spare_placeholder), spare_placeholder = token_mixer_block(
        arriving_lookups,
        arriving_contents,
        params[5],
        params[6],
        initial_numerator,
        initial_denominator,
    )
    gated = (jax.nn.sigmoid(gates_in) * mixed_out).astype(jnp.bfloat16)
    middle = stream + matmul(gated, square[3])
    normed_two = layer_norm(middle, params[7], params[8])
    incoming_two = take_previous(normed_two)
    blended_two = blend_all(normed_two, incoming_two, params[9:11])
    chan_key = blended_two[0].astype(jnp.bfloat16)
    chan_gate = blended_two[1].astype(jnp.bfloat16)
    pre_act = matmul(chan_key, expand)
    activated = jnp.square(jnp.maximum(pre_act, 0.0)).astype(jnp.bfloat16)
    chan_value = matmul(activated, shrink)
    gate_pre = matmul(chan_gate, square[4])
    result = middle + jax.nn.sigmoid(gate_pre) * chan_value
    saved = (
        stream,
        incoming_one,
        mixed_key,
        mixed_value,
        mixed_gate,
        arriving_lookups,
        arriving_contents,
        gates_in,
        initial_numerator,
        initial_denominator,
        gated,
        middle,
        incoming_two,
        chan_key,
        chan_gate,
        pre_act,
        activated,
        chan_value,
        gate_pre,
    )
    return (result, saved)


def norm_back(stream, incoming, params, first_row, share_rows, grads):
    normed, norm_pull = jax.vjp(layer_norm, stream, params[first_row], params[first_row + 1])
    shares = params[share_rows[0] : share_rows[1]]
    spare_placeholder, blend_pull = jax.vjp(blend_all, normed, incoming, shares)
    d_normed, d_incoming, d_shares = blend_pull(grads)
    from_next = give_back(d_incoming)
    d_normed = d_normed.at[-1].add(from_next[0])
    d_stream, d_gain, d_bias = norm_pull(d_normed)
    return (d_stream, jnp.stack([d_gain, d_bias]), d_shares)


def layer_backward(gradient, saved, gathered):
    square, expand, shrink, params = gathered
    (
        stream,
        incoming_one,
        mixed_key,
        mixed_value,
        mixed_gate,
        arriving_lookups,
        arriving_contents,
        gates_in,
        initial_numerator,
        initial_denominator,
        gated,
        middle,
        incoming_two,
        chan_key,
        chan_gate,
        pre_act,
        activated,
        chan_value,
        gate_pre,
    ) = saved
    gate_sig = jax.nn.sigmoid(gate_pre)
    d_value = (gradient * gate_sig).astype(jnp.bfloat16)
    d_gate_pre = (gradient * chan_value * gate_sig * (1.0 - gate_sig)).astype(jnp.bfloat16)
    g_shrink = matmul_tn(activated, d_value)
    d_active = matmul_nt(d_value, shrink)
    d_pre = (d_active * 2.0 * jnp.maximum(pre_act, 0.0)).astype(jnp.bfloat16)
    g_expand = matmul_tn(chan_key, d_pre)
    g_chan_gate = matmul_tn(chan_gate, d_gate_pre)
    d_chan_key = matmul_nt(d_pre, expand)
    d_chan_gate = matmul_nt(d_gate_pre, square[4])
    d_middle, second_norm_gradient, second_share_gradient = norm_back(
        middle, incoming_two, params, 7, (9, 11), (d_chan_key, d_chan_gate)
    )
    d_middle = d_middle + gradient
    d_output = d_middle.astype(jnp.bfloat16)
    g_output = matmul_tn(gated, d_output)
    d_gated = matmul_nt(d_output, square[3])
    (mixed_out, spare_placeholder, spare_placeholder), token_mixer_backward, denoms = jax.vjp(
        token_mixer_block,
        arriving_lookups,
        arriving_contents,
        params[5],
        params[6],
        initial_numerator,
        initial_denominator,
        has_aux=True,
    )
    gate_sig_one = jax.nn.sigmoid(gates_in)
    mixed_gradient = d_gated * gate_sig_one
    d_gates_in = (d_gated * mixed_out * gate_sig_one * (1.0 - gate_sig_one)).astype(jnp.bfloat16)
    length = arriving_lookups.shape[0]
    decay_rate = jnp.exp(params[5])
    carried = (
        jnp.exp(-decay_rate * jnp.arange(length, dtype=jnp.float32)[:, None])
        * mixed_gradient
        / denoms
    )
    zero_state = jnp.zeros_like(decay_rate)
    one_state = jnp.ones_like(decay_rate)
    factor = block_factor(params[5], length)
    following_numerator, following_denominator, spare_factor = carried_in(
        (jnp.sum(carried, axis=0), -jnp.sum(carried * mixed_out, axis=0), factor),
        "seq",
        chain_combine,
        (zero_state, zero_state, one_state),
        True,
    )
    (
        lookup_sensitivity,
        content_sensitivity,
        fading_sensitivity,
        reward_sensitivity,
        spare_placeholder,
        spare_placeholder,
    ) = token_mixer_backward((mixed_gradient, following_numerator, following_denominator))
    lookup_sensitivity = lookup_sensitivity.astype(jnp.bfloat16)
    content_sensitivity = content_sensitivity.astype(jnp.bfloat16)
    g_key = matmul_tn(mixed_key, lookup_sensitivity)
    g_value = matmul_tn(mixed_value, content_sensitivity)
    g_gate = matmul_tn(mixed_gate, d_gates_in)
    d_mixed_key = matmul_nt(lookup_sensitivity, square[0])
    d_mixed_value = matmul_nt(content_sensitivity, square[1])
    d_mixed_gate = matmul_nt(d_gates_in, square[2])
    d_stream, first_norm_gradient, first_share_gradient = norm_back(
        stream, incoming_one, params, 0, (2, 5), (d_mixed_key, d_mixed_value, d_mixed_gate)
    )
    d_stream = d_stream + d_middle
    g_square = jnp.stack([g_key, g_value, g_gate, g_output, g_chan_gate])
    g_params = jnp.concatenate(
        [
            first_norm_gradient,
            first_share_gradient,
            fading_sensitivity[None],
            reward_sensitivity[None],
            second_norm_gradient,
            second_share_gradient,
        ],
        axis=0,
    )
    return (d_stream, (g_square, g_expand, g_shrink, g_params))


def adam_update(weights, gradient, first, second, step_rate, decay_on):
    first_new = BETA_ONE * first + (1.0 - BETA_ONE) * gradient
    second_new = BETA_TWO * second + (1.0 - BETA_TWO) * gradient * gradient
    first_hat = first_new / (1.0 - BETA_ONE**STEP)
    second_hat = second_new / (1.0 - BETA_TWO**STEP)
    moved = first_hat / (jnp.sqrt(second_hat) + ADAM_EPS)
    if decay_on:
        moved = moved + WEIGHT_DECAY * weights
    return (weights - step_rate * moved, first_new, second_new)


def per_device(
    token_ids,
    targets,
    loss_mask,
    square_weights,
    expand_weights,
    shrink_weights,
    vector_params,
    embed_table,
    head_table,
    square_first,
    expand_first,
    shrink_first,
    vector_first,
    embed_first,
    head_first,
    square_second,
    expand_second,
    shrink_second,
    vector_second,
    embed_second,
    head_second,
):
    layers = square_weights.shape[0]
    global_rows = param_stride * layers
    total_tokens = token_ids.shape[0]

    vector_rows = vector_params.shape[0]
    square_own, expand_own, shrink_own = (
        square_weights.shape[2],
        expand_weights.shape[1],
        shrink_weights.shape[1],
    )

    def fetch_layer(layer_id):
        with_vectors = layer_id == 0
        shards = [
            square_weights[layer_id],
            expand_weights[layer_id][None],
            shrink_weights[layer_id][None],
        ]
        if with_vectors:
            shards.append(as_rows(vector_params))
            shards.append(mark_rows(targets, loss_mask))
        else:
            return gather_plain(shards)
        return gather_rows(
            shards,
            weight_portions(
                square_own,
                expand_own,
                shrink_own,
                with_vectors * square_own,
                with_vectors * mark_height,
            ),
            layer_id,
        )

    fetched = [fetch_layer(layer_id) for layer_id in range(layers)]
    vectors_all = fetched[0][3][0, :, :vector_rows].T.astype(jnp.float32)
    global_params = vectors_all[global_rows:]
    blocks = [
        (
            fetched[layer_id][0],
            fetched[layer_id][1][0],
            fetched[layer_id][2][0],
            vectors_all[layer_id * param_stride : (layer_id + 1) * param_stride],
        )
        for layer_id in range(layers)
    ]

    columns = jnp.take(embed_table.astype(jnp.bfloat16), token_ids, axis=1)
    embedded = lax.all_to_all(
        columns, ("dp", "seq"), split_axis=1, concat_axis=0, tiled=True
    ).T.astype(jnp.float32)
    stream, norm_pull_zero = jax.vjp(layer_norm, embedded, global_params[0], global_params[1])
    saved_layers = []
    for layer_id in range(layers):
        stream, saved = layer_forward(stream, blocks[layer_id])
        saved_layers.append(saved)
    normed, norm_pull_last = jax.vjp(layer_norm, stream, global_params[2], global_params[3])
    dp_count = lax.axis_size("dp")
    features, vocab_own = head_table.shape
    vocab_part = vocab_own // dp_count
    head_cut = head_table.astype(jnp.bfloat16).reshape(features, dp_count, vocab_part)
    head_cols = lax.all_to_all(
        head_cut.transpose(1, 0, 2), "dp", split_axis=0, concat_axis=0, tiled=True
    ).reshape(dp_count * features, vocab_part)
    own_rows = normed.shape[0]
    rows_all = gather_rows([normed[None]], row_portions(own_rows), 10)[0][0]
    all_targets, all_mask = marks_of(fetched[0][4])
    first_column = lax.axis_index("seq") * vocab_own + lax.axis_index("dp") * vocab_part
    local_ids = all_targets - first_column
    tile = min(head_tile, total_tokens)
    lifted, stats = head_forward(rows_all, head_cols, local_ids, tile, tile // 4)
    own_log = stats[0] + jnp.log(stats[1])
    log_total = exchange_everywhere(own_log.reshape(-1, 128), add_logs, 13).reshape(-1)
    counted = all_mask.astype(jnp.float32)
    picked_part = jnp.sum(counted * stats[2])
    weight_rows = counted / total_tokens
    factors = jnp.pad(
        jnp.stack(
            [
                jnp.exp(stats[0] - log_total) * weight_rows,
                (jnp.exp(stats[2] - log_total) - 1.0) * weight_rows,
            ]
        ),
        ((0, 6), (0, 0)),
    )
    d_rows, grad_head, head_squares = head_backward(
        lifted, rows_all, head_cols, local_ids, factors, tile, tile // 2
    )
    d_normed = scatter_rows(
        [d_rows[None]], row_portions(own_rows), 11
    )[0][0]
    g_head = (
        lax.all_to_all(
            grad_head.reshape(dp_count, features, vocab_part),
            "dp",
            split_axis=0,
            concat_axis=0,
            tiled=True,
        )
        .transpose(1, 0, 2)
        .reshape(features, vocab_own)
        .astype(jnp.float32)
    )
    d_stream, d_gain_last, d_bias_last = norm_pull_last(d_normed)
    layer_grads = [None] * layers
    vector_grads = [None] * layers
    d_embedded = d_stream
    for layer_id in reversed(range(layers)):
        d_stream, grads = layer_backward(d_stream, saved_layers[layer_id], blocks[layer_id])
        vector_grads[layer_id] = grads[3]
        low_grads = [
            grads[0].astype(jnp.bfloat16),
            grads[1].astype(jnp.bfloat16)[None],
            grads[2].astype(jnp.bfloat16)[None],
        ]
        if layer_id == 0:
            d_embedded, d_gain_zero, d_bias_zero = norm_pull_zero(d_stream)
            all_vectors = jnp.concatenate(
                vector_grads
                + [jnp.stack([d_gain_zero, d_bias_zero, d_gain_last, d_bias_last])],
                axis=0,
            )
            low_grads.append(as_rows(all_vectors).astype(jnp.bfloat16))
        if layer_id > 0:
            layer_grads[layer_id] = scatter_joined(low_grads)
        else:
            layer_grads[layer_id] = scatter_rows(
                low_grads, weight_portions(square_own, expand_own, shrink_own, square_own), layers
            )
    back_columns = lax.all_to_all(
        d_embedded.T.astype(jnp.bfloat16), ("dp", "seq"), split_axis=0, concat_axis=1, tiled=True
    )
    g_embed, embed_squares = embed_gradient(
        back_columns, token_ids, embed_table.shape[1], min(embed_block, total_tokens)
    )
    g_square = jnp.stack([layer_grads[layer_id][0] for layer_id in range(layers)])
    g_expand = jnp.concatenate([layer_grads[layer_id][1] for layer_id in range(layers)])
    g_shrink = jnp.concatenate([layer_grads[layer_id][2] for layer_id in range(layers)])
    g_vector = layer_grads[0][3][0, :, :vector_rows].T
    gradients = (g_square, g_expand, g_shrink, g_vector, g_embed, g_head)
    square_part = jnp.sum(embed_squares) + jnp.sum(head_squares)
    for gradient in gradients[:4]:
        square_part = square_part + jnp.sum(gradient * gradient)
    parts = jnp.stack([square_part, picked_part])
    parts = exchange_everywhere(jnp.broadcast_to(jnp.pad(parts, (0, 6))[:, None], (8, 128)), jnp.add, 12)
    square_sum = parts[0, 0]
    loss_sum = jnp.sum(counted * log_total) - parts[1, 0]
    grad_norm = jnp.sqrt(square_sum)
    scale = jnp.minimum(1.0, 0.5 / math.sqrt(total_tokens) / (grad_norm + 1e-06))
    weights = (
        square_weights,
        expand_weights,
        shrink_weights,
        vector_params,
        embed_table,
        head_table,
    )
    firsts = (square_first, expand_first, shrink_first, vector_first, embed_first, head_first)
    seconds = (
        square_second,
        expand_second,
        shrink_second,
        vector_second,
        embed_second,
        head_second,
    )
    updated = [
        adam_update(
            weights[slot],
            gradients[slot] * scale,
            firsts[slot],
            seconds[slot],
            LEARN_RATES[slot],
            DECAY_FLAGS[slot],
        )
        for slot in range(6)
    ]
    return (
        loss_sum,
        grad_norm,
        updated[0][0],
        updated[1][0],
        updated[2][0],
        updated[3][0],
        updated[4][0],
        updated[5][0],
        updated[0][1],
        updated[1][1],
        updated[2][1],
        updated[3][1],
        updated[4][1],
        updated[5][1],
        updated[0][2],
        updated[1][2],
        updated[2][2],
        updated[3][2],
        updated[4][2],
        updated[5][2],
    )


def solution(mesh):
    placed = (
        P(),
        P("dp"),
        P("dp"),
        P(None, None, ("dp", "seq"), None),
        P(None, ("dp", "seq"), None),
        P(None, ("dp", "seq"), None),
        P(None, ("dp", "seq")),
        P(("dp", "seq"), None),
        P("dp", "seq"),
        P(None, None, ("dp", "seq"), None),
        P(None, ("dp", "seq"), None),
        P(None, ("dp", "seq"), None),
        P(None, ("dp", "seq")),
        P(("dp", "seq"), None),
        P("dp", "seq"),
        P(None, None, ("dp", "seq"), None),
        P(None, ("dp", "seq"), None),
        P(None, ("dp", "seq"), None),
        P(None, ("dp", "seq")),
        P(("dp", "seq"), None),
        P("dp", "seq"),
    )
    return jax.shard_map(
        per_device,
        mesh=mesh,
        in_specs=placed,
        out_specs=(
            P(),
            P(),
            P(None, None, ("dp", "seq"), None),
            P(None, ("dp", "seq"), None),
            P(None, ("dp", "seq"), None),
            P(None, ("dp", "seq")),
            P(("dp", "seq"), None),
            P("dp", "seq"),
            P(None, None, ("dp", "seq"), None),
            P(None, ("dp", "seq"), None),
            P(None, ("dp", "seq"), None),
            P(None, ("dp", "seq")),
            P(("dp", "seq"), None),
            P("dp", "seq"),
            P(None, None, ("dp", "seq"), None),
            P(None, ("dp", "seq"), None),
            P(None, ("dp", "seq"), None),
            P(None, ("dp", "seq")),
            P(("dp", "seq"), None),
            P("dp", "seq"),
        ),
        check_vma=False,
    )
```

```python
import functools
import math

import jax
import jax.numpy as jnp
from jax import lax
from jax.experimental import pallas as pl
from jax.experimental.pallas import tpu as pltpu
from jax.sharding import PartitionSpec as P

STEP = 10
ON_MESH = pl.DeviceIdType.MESH


def place():
    dp, seq = lax.axis_index("dp"), lax.axis_index("seq")
    return dp, seq, dp // 2, lax.rem(dp, 2), seq // 2, lax.rem(seq, 2)


def greet(partners, extra):
    barrier = pltpu.get_barrier_semaphore()
    for partner in partners:
        pl.semaphore_signal(barrier, inc=1, device_id=partner, device_id_type=ON_MESH)
    for exists, partner in extra:
        @pl.when(exists)
        def _():
            pl.semaphore_signal(barrier, inc=1, device_id=partner, device_id_type=ON_MESH)
    peers = len(partners)
    for exists, partner in extra:
        peers = peers + exists.astype(jnp.int32)
    pl.semaphore_wait(barrier, peers)


class Sems:
    def __init__(self, send, recv, local):
        self.send, self.recv, self.local = send, recv, local
        self.ns = self.nr = self.nl = 0

    def pair(self):
        self.ns += 1
        return self.send.at[self.ns - 1], self.recv.at[self.ns - 1]

    def own(self):
        self.nl += 1
        return self.local.at[self.nl - 1]


def gather_blocks(tensors, portions, collective_id):
    count = len(tensors)
    dims = [t.shape for t in tensors]
    hops = 3
    pieces_total = sum(len(p) for p in portions)
    n_send = count + count + pieces_total * (7 + 2 * hops + 7)

    def kernel(*refs):
        ins, outs = refs[:count], refs[count : 2 * count]
        wide = refs[2 * count : 3 * count]
        half = refs[3 * count : 4 * count]
        send, recv, local = refs[4 * count :]
        dp, seq, z, y, x, c = place()
        core = (dp, seq + 1 - 2 * c)
        xway = (dp, seq + 2 - 4 * x)
        yway = (dp + 1 - 2 * y, seq)
        up, down = (dp + 2, seq), (dp - 2, seq)
        has_up, has_down = z < hops, z > 0
        greet([core, xway, yway], [(has_up, up), (has_down, down)])
        sems = Sems(send, recv, local)

        def cols(t, side):
            width = dims[t][2] // 2
            return pl.ds(pl.multiple_of(side * width, 128), width)

        first = []
        for t in range(count):
            rows = pl.ds(pl.multiple_of(c * dims[t][1], 8), dims[t][1])
            mine = pltpu.make_async_copy(ins[t].at[:, :, cols(t, c)], wide[t].at[:, rows, :], sems.own())
            ss, rs = sems.pair()
            other = pltpu.make_async_remote_copy(
                src_ref=ins[t].at[:, :, cols(t, 1 - c)], dst_ref=wide[t].at[:, rows, :],
                send_sem=ss, recv_sem=rs, device_id=core, device_id_type=ON_MESH)
            other.start()
            mine.start()
            first.append((mine, other))
        core_sems = [sems.pair() for t in range(count)]
        stay = []
        for t in range(count):
            first[t][0].wait()
            first[t][1].wait()
            half[t][...] = wide[t][...].astype(jnp.bfloat16)
            own = pltpu.make_async_copy(half[t], outs[t].at[:, z, y, x, :, cols(t, c)], sems.own())
            own.start()
            stay.append(own)

        def block(piece, zz, yy, xx):
            t, m0, m1, r0, r1 = piece
            return outs[t].at[m0:m1, zz, yy, xx, r0:r1, cols(t, c)]

        def to_core(p, zz, yy, xx, source=None):
            for piece in portions[p]:
                t = piece[0]
                region = block(piece, zz, yy, xx)
                pltpu.make_async_remote_copy(
                    src_ref=region if source is None else source(piece), dst_ref=region,
                    send_sem=core_sems[t][0], recv_sem=core_sems[t][1], device_id=core, device_id_type=ON_MESH).start()

        def message(p, where, device, source=None):
            copies = []
            for piece in portions[p]:
                ss, rs = sems.pair()
                region = block(piece, *where)
                copies.append(pltpu.make_async_remote_copy(
                    src_ref=region if source is None else source(piece), dst_ref=region,
                    send_sem=ss, recv_sem=rs, device_id=device, device_id_type=ON_MESH))
            return copies

        def start(copies):
            for copy in copies:
                copy.start()

        def arrive(copies):
            for copy in copies:
                copy.wait_recv()

        def sent(copies):
            for copy in copies:
                copy.wait_send()

        def from_half(piece):
            t, m0, m1, r0, r1 = piece
            return half[t].at[m0:m1, r0:r1, :]

        both = slice(0, 2)
        a_way, b_way = (yway, xway) * 2, (xway, yway) * 2
        ways = range(len(portions))

        def one_of(p, zz):
            return (zz, y, x)

        def pair_of(p, zz):
            return (zz, both, x) if p % 2 == 0 else (zz, y, both)

        def other_of(p, zz):
            return (zz, 1 - y, x) if p % 2 == 0 else (zz, y, 1 - x)

        def far_of(p, zz):
            return (zz, both, 1 - x) if p % 2 == 0 else (zz, 1 - y, both)

        def late(p):
            return p >= 2

        def event_z(e):
            return z if e == 0 else z - e if e <= hops else z + e - hops

        def happens(e):
            return z - e >= 0 if e <= hops else z + e - hops <= hops

        def when(e, what):
            if e == 0:
                what()
            else:
                pl.when(happens(e))(what)

        events = range(1 + 2 * hops)
        a_msgs, z_msgs, b_msgs = {}, {}, {}
        for p in ways:
            held = one_of if late(p) else pair_of
            for e in events if late(p) else (0,):
                a_msgs[p, e] = message(p, one_of(p, event_z(e)), a_way[p], from_half if e == 0 else None)
            for k in range(hops):
                source = from_half if late(p) and k == 0 else None
                z_msgs[p, 1 + k] = message(p, held(p, z - k), up, source)
                z_msgs[p, 1 + hops + k] = message(p, held(p, z + k), down, source)
            for e in events:
                b_msgs[p, e] = message(p, pair_of(p, event_z(e)), b_way[p])

        def start_z(p, e):
            @pl.when(has_up if e <= hops else has_down)
            def _():
                start(z_msgs[p, e])

        for p in ways:
            if late(p):
                start_z(p, 1)
                start_z(p, 1 + hops)
            start(a_msgs[p, 0])
        for own in stay:
            own.wait()
        for p in ways:
            to_core(p, z, y, x, from_half)
        for p in ways:
            if not late(p):
                arrive(a_msgs[p, 0])
                start_z(p, 1)
                start_z(p, 1 + hops)
                start(b_msgs[p, 0])
                to_core(p, *other_of(p, z))

        def z_event(p, e):
            def turn():
                arrive(z_msgs[p, e])
                if e % hops:
                    start_z(p, e + 1)
                if late(p):
                    start(a_msgs[p, e])
                    to_core(p, *one_of(p, event_z(e)))
                else:
                    start(b_msgs[p, e])
                    to_core(p, *pair_of(p, event_z(e)))
            when(e, turn)

        def a_event(p, e):
            def turn():
                arrive(a_msgs[p, e])
                start(b_msgs[p, e])
                to_core(p, *other_of(p, event_z(e)))
            when(e, turn)

        def b_event(p, e):
            def turn():
                arrive(b_msgs[p, e])
                to_core(p, *far_of(p, event_z(e)))
            when(e, turn)

        def at(hop):
            return (0,) if hop == 0 else (hop, hops + hop)

        for hop in range(hops + 3):
            if 1 <= hop <= hops:
                for p in ways:
                    for e in at(hop):
                        z_event(p, e)
            if hop - 1 in range(hops + 1):
                for p in ways:
                    for e in at(hop - 1):
                        if late(p):
                            a_event(p, e)
                        else:
                            b_event(p, e)
            if hop - 2 in range(hops + 1):
                for p in ways:
                    for e in at(hop - 2):
                        if late(p):
                            b_event(p, e)

        for (p, e), msg in list(a_msgs.items()) + list(b_msgs.items()):
            when(e, functools.partial(sent, msg))
        for (p, e), msg in z_msgs.items():
            k = (e - 1) % hops
            going = (z - k >= 0) & has_up if e <= hops else (z + k <= hops) & has_down
            pl.when(going)(functools.partial(sent, msg))
        for t in range(count):
            whole = pltpu.make_async_remote_copy(
                src_ref=outs[t].at[:, :, :, :, :, cols(t, c)], dst_ref=outs[t].at[:, :, :, :, :, cols(t, 1 - c)],
                send_sem=core_sems[t][0], recv_sem=core_sems[t][1], device_id=core, device_id_type=ON_MESH)
            whole.wait_send()
            whole.wait_recv()

    outs = pl.pallas_call(
        kernel,
        out_shape=[jax.ShapeDtypeStruct((m, hops + 1, 2, 2, 2 * r, w), jnp.bfloat16) for m, r, w in dims],
        in_specs=[pl.BlockSpec(memory_space=pl.ANY)] * count,
        out_specs=[pl.BlockSpec(memory_space=pl.ANY)] * count,
        scratch_shapes=[pltpu.VMEM((m, 2 * r, w // 2), jnp.float32) for m, r, w in dims]
        + [pltpu.VMEM((m, 2 * r, w // 2), jnp.bfloat16) for m, r, w in dims]
        + [pltpu.SemaphoreType.DMA((n_send,)), pltpu.SemaphoreType.DMA((n_send,)), pltpu.SemaphoreType.DMA((2 * count,))],
        compiler_params=pltpu.CompilerParams(collective_id=collective_id, has_side_effects=True, vmem_limit_bytes=40 << 20),
    )(*tensors)
    return [o.reshape(m, (hops + 1) * 8 * r, w) for o, (m, r, w) in zip(outs, dims)]


def scatter_blocks(tensors, portions, rows_own, collective_id):
    count = len(tensors)
    hops = 3
    dims = [(t.shape[0], r, t.shape[2]) for t, r in zip(tensors, rows_own)]
    views = [t.reshape(m, hops + 1, 2, 2, 2 * r, w) for t, (m, r, w) in zip(tensors, dims)]
    pieces_total = sum(len(p) for p in portions)
    n_send = pieces_total * (2 + 4 + 2 * hops + 4) + count
    n_local = pieces_total * 2 + count
    ways = range(len(portions))
    flat = [(p, piece) for p in ways for piece in portions[p]]
    flat_dims = [(piece[2] - piece[1], piece[4] - piece[3], dims[piece[0]][2] // 2) for _, piece in flat]

    def kernel(*refs):
        ins, outs = refs[:count], refs[count : 2 * count]
        k0 = 2 * count
        acc = refs[k0 : k0 + count]
        crecv = refs[k0 + count : k0 + 2 * count]
        fin = refs[k0 + 2 * count : k0 + 3 * count]
        k0 += 3 * count
        n = len(flat)
        b_all, u_all, d_all, a_all = (refs[k0 + i * n : k0 + (i + 1) * n] for i in range(4))
        send, recv, local = refs[k0 + 4 * n :]
        index = {}
        for i, (p, piece) in enumerate(flat):
            index.setdefault(p, []).append((i, piece))
        dp, seq, z, y, x, c = place()
        core = (dp, seq + 1 - 2 * c)
        xway = (dp, seq + 2 - 4 * x)
        yway = (dp + 1 - 2 * y, seq)
        up, down = (dp + 2, seq), (dp - 2, seq)
        has_up, has_down = z < hops, z > 0
        greet([core, xway, yway], [(has_up, up), (has_down, down)])
        sems = Sems(send, recv, local)
        a_way, b_way = (yway, xway) * 2, (xway, yway) * 2

        def cols(t, side):
            width = dims[t][2] // 2
            return pl.ds(pl.multiple_of(side * width, 128), width)

        def remote(src, dst, device):
            ss, rs = sems.pair()
            return pltpu.make_async_remote_copy(src_ref=src, dst_ref=dst, send_sem=ss, recv_sem=rs,
                                                device_id=device, device_id_type=ON_MESH)

        def place_of(p, zz, a, b):
            return (zz, a, b) if p % 2 == 0 else (zz, b, a)

        own_a, own_b = (y, x) * 2, (x, y) * 2

        def late(p):
            return p >= 2


        def add(dst, src, lead):
            def turn(i, _):
                where, rest = [], i
                for size in reversed(lead):
                    where.append(lax.rem(rest, size))
                    rest = rest // size
                where = tuple(reversed(where))
                dst[where] = (dst[where].astype(jnp.float32) + src[where].astype(jnp.float32)).astype(dst.dtype)
                return 0
            total = 1
            for size in lead:
                total *= size
            lax.fori_loop(0, total, turn, 0)

        everyz, both = slice(0, hops + 1), slice(0, 2)
        chunks = {}
        for far in (1, 0):
            for p in ways:
                b = own_b[p] if far == 0 else 1 - own_b[p]
                made = []
                for i, piece in index[p]:
                    t, m0, m1, r0, r1 = piece
                    where = (slice(m0, m1),) + place_of(p, everyz, both, b) + (slice(r0, r1),)
                    there = remote(ins[t].at[where + (cols(t, 1 - c),)], crecv[t].at[where], core)
                    here = pltpu.make_async_copy(ins[t].at[where + (cols(t, c),)], acc[t].at[where], sems.own())
                    there.start()
                    here.start()
                    made.append((there, here, piece, where))
                chunks[far, p] = made

        def core_add(far, p):
            for there, here, piece, where in chunks[far, p]:
                t, m0, m1, r0, r1 = piece
                there.wait_recv()
                here.wait()
                add(acc[t].at[where], crecv[t].at[where], (m1 - m0, hops + 1, 2))

        zorder = (3, 0, 2, 1)
        b_msgs = {}
        for p in ways:
            core_add(1, p)
            for zz in zorder:
                msgs = []
                for i, (t, m0, m1, r0, r1) in index[p]:
                    src = acc[t].at[(slice(m0, m1),) + place_of(p, zz, both, 1 - own_b[p]) + (slice(r0, r1),)]
                    msgs.append(remote(src, b_all[i].at[:, zz], b_way[p]))
                for msg in msgs:
                    msg.start()
                b_msgs[p, zz] = msgs
        for p in ways:
            core_add(0, p)

        def b_add(p, zz):
            for msg in b_msgs[p, zz]:
                msg.wait_recv()
            for i, (t, m0, m1, r0, r1) in index[p]:
                dst = acc[t].at[(slice(m0, m1),) + place_of(p, zz, both, own_b[p]) + (slice(r0, r1),)]
                add(dst, b_all[i].at[:, zz], (m1 - m0, 2))

        def mine(p, i, piece, zz):
            t, m0, m1, r0, r1 = piece
            a = own_a[p] if late(p) else both
            return acc[t].at[(slice(m0, m1),) + place_of(p, zz, a, own_b[p]) + (slice(r0, r1),)]

        def landing(p, land, i, zz):
            return land[i].at[:, zz, 0] if late(p) else land[i].at[:, zz]

        a_msgs = {}

        def a_start(p, zz):
            msgs = []
            for i, (t, m0, m1, r0, r1) in index[p]:
                src = acc[t].at[(slice(m0, m1),) + place_of(p, zz, 1 - own_a[p], own_b[p]) + (slice(r0, r1),)]
                msgs.append(remote(src, a_all[i].at[:, zz if late(p) else 0], a_way[p]))
            for msg in msgs:
                msg.start()
            a_msgs[p, zz if late(p) else 0] = msgs

        def a_add(p, zz):
            for msg in a_msgs[p, zz]:
                msg.wait_recv()
            for i, piece in index[p]:
                add(mine(p, i, piece, zz), a_all[i].at[:, zz], (piece[2] - piece[1],))

        up_msgs, down_msgs = {}, {}
        for p in ways:
            for zz in range(hops + 1):
                up_msgs[p, zz] = [remote(mine(p, i, piece, zz), landing(p, u_all, i, zz), up) for i, piece in index[p]] if zz > 0 else None
                down_msgs[p, zz] = [remote(mine(p, i, piece, zz), landing(p, d_all, i, zz), down) for i, piece in index[p]] if zz < hops else None

        def z_add(p, zz, msgs, land):
            for msg in msgs[p, zz]:
                msg.wait_recv()
            for i, piece in index[p]:
                lead = (piece[2] - piece[1],) if late(p) else (piece[2] - piece[1], 2)
                add(mine(p, i, piece, zz), landing(p, land, i, zz), lead)

        def up_send(p, zz):
            @pl.when(z < zz)
            def _():
                @pl.when(z > 0)
                def _():
                    z_add(p, zz, up_msgs, u_all)
                for msg in up_msgs[p, zz]:
                    msg.start()

        def down_send(p, zz):
            @pl.when(z > zz)
            def _():
                @pl.when(z < hops)
                def _():
                    z_add(p, zz, down_msgs, d_all)
                for msg in down_msgs[p, zz]:
                    msg.start()

        early_ways, late_ways = [p for p in ways if not late(p)], [p for p in ways if late(p)]
        for zz in zorder[:2]:
            for p in ways:
                b_add(p, zz)
                if late(p):
                    a_start(p, zz)
                elif zz == 3:
                    up_send(p, 3)
                else:
                    down_send(p, 0)
        for zz in zorder[2:]:
            for p in ways:
                b_add(p, zz)
                if late(p):
                    a_start(p, zz)
                elif zz == 2:
                    up_send(p, 2)
                else:
                    down_send(p, 1)
        for p in late_ways:
            a_add(p, 3)
            up_send(p, 3)
            a_add(p, 0)
            down_send(p, 0)
        for p in early_ways:
            up_send(p, 1)
            down_send(p, 2)
        for p in late_ways:
            a_add(p, 2)
            up_send(p, 2)
            a_add(p, 1)
            down_send(p, 1)
        for p in late_ways:
            up_send(p, 1)
            down_send(p, 2)
        for p in ways:
            for zz in range(hops + 1):
                @pl.when(z == zz)
                def _():
                    if zz > 0:
                        z_add(p, zz, up_msgs, u_all)
                    if zz < hops:
                        z_add(p, zz, down_msgs, d_all)
            if not late(p):
                a_start(p, z)
        for p in late_ways:
            for i, (t, m0, m1, r0, r1) in index[p]:
                for m in range(m0, m1):
                    fin[t][m, r0:r1, :] = acc[t][(m,) + place_of(p, z, own_a[p], own_b[p]) + (slice(r0, r1),)].astype(jnp.float32)
        for p in early_ways:
            for msg in a_msgs[p, 0]:
                msg.wait_recv()
            for i, (t, m0, m1, r0, r1) in index[p]:
                for m in range(m0, m1):
                    part = acc[t][(m,) + place_of(p, z, own_a[p], own_b[p]) + (slice(r0, r1),)]
                    fin[t][m, r0:r1, :] = part.astype(jnp.float32) + a_all[i][m - m0, 0].astype(jnp.float32)
        last = []
        for t in range(count):
            r = dims[t][1]
            other = remote(fin[t].at[:, pl.ds(pl.multiple_of((1 - c) * r, 8), r), :], outs[t].at[:, :, cols(t, c)], core)
            keep = pltpu.make_async_copy(fin[t].at[:, pl.ds(pl.multiple_of(c * r, 8), r), :], outs[t].at[:, :, cols(t, c)], sems.own())
            other.start()
            keep.start()
            last.append((other, keep))
        for made in chunks.values():
            for there, here, piece, where in made:
                there.wait_send()
        for msgs in list(b_msgs.values()) + list(a_msgs.values()):
            for msg in msgs:
                msg.wait_send()
        for p in ways:
            for zz in range(hops + 1):
                if zz > 0:
                    @pl.when(z < zz)
                    def _():
                        for msg in up_msgs[p, zz]:
                            msg.wait_send()
                if zz < hops:
                    @pl.when(z > zz)
                    def _():
                        for msg in down_msgs[p, zz]:
                            msg.wait_send()
        for other, keep in last:
            keep.wait()
            other.wait()

    bf = jnp.bfloat16
    outs = pl.pallas_call(
        kernel,
        out_shape=[jax.ShapeDtypeStruct((m, r, w), jnp.float32) for m, r, w in dims],
        in_specs=[pl.BlockSpec(memory_space=pl.ANY)] * count,
        out_specs=[pl.BlockSpec(memory_space=pl.ANY)] * count,
        scratch_shapes=[pltpu.VMEM((m, hops + 1, 2, 2, 2 * r, w // 2), bf) for m, r, w in dims]
        + [pltpu.VMEM((m, hops + 1, 2, 2, 2 * r, w // 2), bf) for m, r, w in dims]
        + [pltpu.VMEM((m, 2 * r, w // 2), jnp.float32) for m, r, w in dims]
        + [pltpu.VMEM((m, hops + 1, 2, r, w), bf) for m, r, w in flat_dims] * 3
        + [pltpu.VMEM((m, hops + 1, r, w), bf) for m, r, w in flat_dims]
        + [pltpu.SemaphoreType.DMA((n_send,)), pltpu.SemaphoreType.DMA((n_send,)), pltpu.SemaphoreType.DMA((n_local,))],
        compiler_params=pltpu.CompilerParams(collective_id=collective_id, has_side_effects=True, vmem_limit_bytes=50 << 20),
    )(*views)
    return list(lax.optimization_barrier(outs))


def exchange_everywhere(value, combine, collective_id):
    sizes = (("dp", lax.axis_size("dp")), ("seq", lax.axis_size("seq")))
    steps = [(axis, 1 << bit) for axis, size in reversed(sizes) for bit in range(size.bit_length() - 1)]

    def kernel(in_ref, out_ref, leave, land, send, recv):
        dp, seq = lax.axis_index("dp"), lax.axis_index("seq")
        partners = []
        for axis, step in steps:
            mine = dp if axis == "dp" else seq
            other = mine + step - 2 * step * lax.rem(mine // step, 2)
            partners.append((other, seq) if axis == "dp" else (dp, other))
        greet(partners, [])
        leave[0] = in_ref[...]
        for k, partner in enumerate(partners):
            copy = pltpu.make_async_remote_copy(
                src_ref=leave.at[k],
                dst_ref=land.at[k],
                send_sem=send.at[k],
                recv_sem=recv.at[k],
                device_id=partner,
                device_id_type=ON_MESH,
            )
            copy.start()
            copy.wait()
            both = combine(leave[k], land[k])
            if k + 1 < len(steps):
                leave[k + 1] = both
            else:
                out_ref[...] = both

    n = len(steps)
    return pl.pallas_call(
        kernel,
        out_shape=jax.ShapeDtypeStruct(value.shape, jnp.float32),
        in_specs=[pl.BlockSpec(memory_space=pltpu.VMEM)],
        out_specs=pl.BlockSpec(memory_space=pltpu.VMEM),
        scratch_shapes=[
            pltpu.VMEM((n,) + value.shape, jnp.float32),
            pltpu.VMEM((n,) + value.shape, jnp.float32),
            pltpu.SemaphoreType.DMA((n,)),
            pltpu.SemaphoreType.DMA((n,)),
        ],
        compiler_params=pltpu.CompilerParams(collective_id=collective_id, has_side_effects=True),
    )(value)


def add_logs(left, right):
    return jnp.maximum(left, right) + jnp.log(1.0 + jnp.exp(-jnp.abs(left - right)))


def head_forward(rows_all, head_cols, local_ids, tile, sub):
    tokens, features = rows_all.shape
    width = head_cols.shape[1]

    def kernel(rows_ref, head_ref, ids_ref, p_ref, stats_ref):
        ids = jnp.transpose(jnp.broadcast_to(ids_ref[...], (128, tile)))[:, :1]
        lane = lax.broadcasted_iota(jnp.int32, (sub, 128), 1)
        column = lax.broadcasted_iota(jnp.int32, (sub, width), 1)
        for part in range(tile // sub):
            here = slice(part * sub, (part + 1) * sub)
            logits = jnp.dot(rows_ref[here, :], head_ref[...], preferred_element_type=jnp.float32)
            top = jnp.max(logits, axis=1, keepdims=True)
            picked = jnp.sum(jnp.where(column == ids[here], logits, 0.0), axis=1, keepdims=True)
            lifted = jnp.exp(logits - top)
            spread = jnp.sum(lifted, axis=1, keepdims=True)
            p_ref[here, :] = lifted.astype(jnp.bfloat16)
            table = jnp.where(lane == 0, top, jnp.where(lane == 1, spread, picked))
            stats_ref[:, here] = jnp.transpose(table)[:8]

    return pl.pallas_call(
        kernel,
        grid=(tokens // tile,),
        out_shape=[
            jax.ShapeDtypeStruct((tokens, width), jnp.bfloat16),
            jax.ShapeDtypeStruct((8, tokens), jnp.float32),
        ],
        in_specs=[
            pl.BlockSpec((tile, features), lambda i: (i, 0)),
            pl.BlockSpec((features, width), lambda i: (0, 0)),
            pl.BlockSpec((1, tile), lambda i: (0, i)),
        ],
        out_specs=[
            pl.BlockSpec((tile, width), lambda i: (i, 0)),
            pl.BlockSpec((8, tile), lambda i: (0, i)),
        ],
        compiler_params=pltpu.CompilerParams(vmem_limit_bytes=50 << 20),
    )(rows_all, head_cols, local_ids[None])


def head_backward(lifted, rows_all, head_cols, local_ids, factors, tile, sub):
    tokens, width = lifted.shape
    features = rows_all.shape[1]
    steps = tokens // tile

    def kernel(p_ref, rows_ref, head_ref, ids_ref, factor_ref, d_rows_ref, d_head_ref, squares_ref, d_logits, total):
        step = pl.program_id(0)
        ids = jnp.transpose(jnp.broadcast_to(ids_ref[...], (128, tile)))[:, :1]
        scales = jnp.transpose(jnp.concatenate([factor_ref[...]] * 16, axis=0))
        scale, hit = scales[:, :1], scales[:, 1:2]
        column = lax.broadcasted_iota(jnp.int32, (sub, width), 1)
        for part in range(tile // sub):
            here = slice(part * sub, (part + 1) * sub)
            d_logits[here, :] = jnp.where(
                column == ids[here], hit[here], p_ref[here, :].astype(jnp.float32) * scale[here]
            ).astype(jnp.bfloat16)
            d_rows_ref[here, :] = lax.dot_general(
                d_logits[here, :], head_ref[...], (((1,), (1,)), ((), ())), preferred_element_type=jnp.float32
            ).astype(jnp.bfloat16)
        term = lax.dot_general(
            rows_ref[...], d_logits[...], (((0,), (0,)), ((), ())), preferred_element_type=jnp.float32
        )

        @pl.when(step == 0)
        def _():
            total[...] = term

        @pl.when(step > 0)
        def _():
            total[...] += term

        @pl.when(step == steps - 1)
        def _():
            low = total[...].astype(jnp.bfloat16)
            d_head_ref[...] = low
            wide = low.astype(jnp.float32)
            squares_ref[...] = jnp.sum((wide * wide).reshape(features // 8, 8, width), axis=0)

    return pl.pallas_call(
        kernel,
        grid=(steps,),
        out_shape=[
            jax.ShapeDtypeStruct((tokens, features), jnp.bfloat16),
            jax.ShapeDtypeStruct((features, width), jnp.bfloat16),
            jax.ShapeDtypeStruct((8, width), jnp.float32),
        ],
        in_specs=[
            pl.BlockSpec((tile, width), lambda i: (i, 0)),
            pl.BlockSpec((tile, features), lambda i: (i, 0)),
            pl.BlockSpec((features, width), lambda i: (0, 0)),
            pl.BlockSpec((1, tile), lambda i: (0, i)),
            pl.BlockSpec((8, tile), lambda i: (0, i)),
        ],
        out_specs=[
            pl.BlockSpec((tile, features), lambda i: (i, 0)),
            pl.BlockSpec((features, width), lambda i: (0, 0)),
            pl.BlockSpec((8, width), lambda i: (0, 0)),
        ],
        scratch_shapes=[pltpu.VMEM((tile, width), jnp.bfloat16), pltpu.VMEM((features, width), jnp.float32)],
        compiler_params=pltpu.CompilerParams(vmem_limit_bytes=56 << 20),
    )(lifted, rows_all, head_cols, local_ids[None], factors)


def head_backward_scattered(lifted, rows_all, head_cols, local_ids, factors, collective_id):
    tokens, width = lifted.shape
    features = rows_all.shape[1]
    hops, block = 3, tokens // 16
    rows, wing = block // 2, features // 2
    zorder = (3, 0, 2, 1)
    cuts = [slice(k, min(k + 512, width)) for k in range(0, width - 256, 512)]
    cuts[-1] = slice(cuts[-1].start, width)
    parts = (slice(0, rows), slice(rows, block))

    def kernel(p_hbm, rows_hbm, head_ref, ids_ref, factor_ref, out, d_head_ref, squares_ref,
               p_buf, r_buf, d_logits, total, acc, give, crecv, b_all, u_all, d_all, a_all, fin,
               in_sem, core_send, core_recv, send, recv, local):
        dp, seq, z, y, x, c = place()
        core = (dp, seq + 1 - 2 * c)
        xway = (dp, seq + 2 - 4 * x)
        yway = (dp + 1 - 2 * y, seq)
        up, down = (dp + 2, seq), (dp - 2, seq)
        has_up, has_down = z < hops, z > 0
        groups = ((1 - y, 1 - x), (y, 1 - x), (1 - y, x), (y, x))

        def fetch(slot, zz, yy, xx):
            return (
                pltpu.make_async_copy(p_hbm.at[zz, yy, xx], p_buf.at[slot], in_sem.at[slot, 0]),
                pltpu.make_async_copy(rows_hbm.at[zz, yy, xx], r_buf.at[slot], in_sem.at[slot, 1]),
            )

        for copy in fetch(0, zorder[0], *groups[0]):
            copy.start()
        greet([core, xway, yway], [(has_up, up), (has_down, down)])
        sems = Sems(send, recv, local)

        def remote(src, dst, device):
            ss, rs = sems.pair()
            return pltpu.make_async_remote_copy(src_ref=src, dst_ref=dst, send_sem=ss, recv_sem=rs,
                                                device_id=device, device_id_type=ON_MESH)

        def to_core(g, k, zz):
            yy, xx = groups[g]
            return pltpu.make_async_remote_copy(
                src_ref=give.at[k], dst_ref=crecv.at[zz, yy, xx], send_sem=core_send.at[g * 4 + k],
                recv_sem=core_recv.at[g * 4 + k], device_id=core, device_id_type=ON_MESH)

        total[...] = jnp.zeros_like(total)
        column = lax.broadcasted_iota(jnp.int32, (rows, width), 1)

        def zz_of(k):
            return jnp.where(k == 0, 3, jnp.where(k == 1, 0, jnp.where(k == 2, 2, 1)))

        def compute(g, k):
            yy, xx = groups[g]
            zz = zz_of(k)
            slot = lax.rem(k, 2)
            for copy in fetch(slot, zz, yy, xx):
                copy.wait()
            if g < 3:
                more = k < 4
            else:
                more = k < 3
            nyy, nxx = groups[min(g + 1, 3)]
            last = k == 3

            @pl.when(more)
            def _():
                for copy in fetch(1 - slot, jnp.where(last, 3, zz_of(k + 1)), jnp.where(last, nyy, yy), jnp.where(last, nxx, xx)):
                    copy.start()
            first = pl.multiple_of(((zz * 2 + yy) * 2 + xx) * block, block)
            here = pl.ds(first, block)
            ids = jnp.transpose(jnp.broadcast_to(ids_ref[:, here], (128, block)))[:, :1]
            scales = jnp.transpose(jnp.concatenate([factor_ref[:, here]] * 16, axis=0))
            if g > 0:
                to_core(g - 1, k, zz).wait_send()
            for part in parts:
                d_logits[part, :] = jnp.where(
                    column == ids[part], scales[part, 1:2], p_buf[slot, part, :].astype(jnp.float32) * scales[part, :1]
                ).astype(jnp.bfloat16)
                d_rows = lax.dot_general(
                    d_logits[part, :], head_ref[...], (((1,), (1,)), ((), ())), preferred_element_type=jnp.float32)
                left, right = d_rows[:, :wing], d_rows[:, wing:]
                acc[zz, yy, xx, part, :] = jnp.where(c == 0, left, right).astype(jnp.bfloat16)
                give[k, part, :] = jnp.where(c == 0, right, left).astype(jnp.bfloat16)
            to_core(g, k, zz).start()
            for cut in cuts:
                total[:, cut] += lax.dot_general(
                    r_buf[slot], d_logits[:, cut], (((0,), (0,)), ((), ())), preferred_element_type=jnp.float32)

        def add(dst, src):
            dst[...] = (dst[...].astype(jnp.float32) + src[...].astype(jnp.float32)).astype(dst.dtype)

        own_b = (x, y)
        own_a = (y, x)
        b_way, a_way = (xway, yway), (yway, xway)

        def spot(p, zz, a, b):
            yy, xx = (a, b) if p == 0 else (b, a)
            return acc.at[zz, yy, xx, parts[p]]

        b_msgs, z_up, z_down = {}, {}, {}
        for p in range(2):
            for zz in range(hops + 1):
                for near in range(2):
                    a = own_a[p] if near else 1 - own_a[p]
                    b_msgs[p, zz, near] = remote(spot(p, zz, a, 1 - own_b[p]), b_all.at[p, zz, a], b_way[p])
                    mine = spot(p, zz, a, own_b[p])
                    if zz > 0:
                        z_up[p, zz, near] = remote(mine, u_all.at[p, zz - 1, a], up)
                    if zz < hops:
                        z_down[p, zz, near] = remote(mine, d_all.at[p, zz, a], down)

        def core_add(g):
            yy, xx = groups[g]
            for k, zz in enumerate(zorder):
                to_core(g, k, zz).wait_recv()
                for part in parts:
                    add(acc.at[zz, yy, xx, part], crecv.at[zz, yy, xx, part])
                for p, near in (((0, 0), (1, 0)), ((0, 1),), ((1, 1),), ())[g]:
                    b_msgs[p, zz, near].start()

        def b_add(p, near):
            a = own_a[p] if near else 1 - own_a[p]
            for zz in zorder:
                b_msgs[p, zz, near].wait_recv()
                add(spot(p, zz, a, own_b[p]), b_all.at[p, zz, a])

        def z_take(p, zz, near, msgs, land):
            a = own_a[p] if near else 1 - own_a[p]
            msgs[p, zz, near].wait_recv()
            add(spot(p, zz, a, own_b[p]), land.at[p, zz - 1 if msgs is z_up else zz, a])

        def z_hop(p, near, hop):
            @pl.when(z == hop)
            def _():
                for zz in range(hops, hop, -1):
                    if hop > 0:
                        z_take(p, zz, near, z_up, u_all)
                    z_up[p, zz, near].start()

            @pl.when(z == hops - hop)
            def _():
                for zz in range(0, hops - hop):
                    if hop > 0:
                        z_take(p, zz, near, z_down, d_all)
                    z_down[p, zz, near].start()

        def run(g):
            def turn(k, _):
                compute(g, k)
                return 0
            lax.fori_loop(0, 4, turn, 0)

        run(0)
        core_add(0)
        run(1)
        core_add(1)
        b_add(1, 0)
        z_hop(1, 0, 0)
        run(2)
        core_add(2)
        b_add(0, 0)
        z_hop(0, 0, 0)
        z_hop(1, 0, 1)
        run(3)
        core_add(3)
        for p in range(2):
            b_add(p, 1)
            z_hop(p, 1, 0)
        z_hop(0, 0, 1)
        z_hop(1, 0, 2)
        for p in range(2):
            z_hop(p, 1, 1)
        z_hop(0, 0, 2)
        for p in range(2):
            z_hop(p, 1, 2)
        low = total[...].astype(jnp.bfloat16)
        d_head_ref[...] = low
        wide = low.astype(jnp.float32)
        squares_ref[...] = jnp.sum((wide * wide).reshape(features // 8, 8, width), axis=0)
        a_msgs = []
        for p in range(2):
            for zz in range(hops + 1):
                @pl.when(z == zz)
                def _():
                    for near in range(2):
                        if zz > 0:
                            z_take(p, zz, near, z_up, u_all)
                        if zz < hops:
                            z_take(p, zz, near, z_down, d_all)
            msg = remote(spot(p, z, 1 - own_a[p], own_b[p]), a_all.at[p], a_way[p])
            msg.start()
            a_msgs.append(msg)
        for p in range(2):
            a_msgs[p].wait_recv()
            fin[parts[p], :] = spot(p, z, own_a[p], own_b[p])[...].astype(jnp.float32) + a_all[p].astype(jnp.float32)
        side = pl.ds(pl.multiple_of(c * wing, 128), wing)
        other = remote(fin.at[pl.ds(pl.multiple_of((1 - c) * rows, 8), rows), :], out.at[:, side], core)
        keep = pltpu.make_async_copy(fin.at[pl.ds(pl.multiple_of(c * rows, 8), rows), :], out.at[:, side], sems.own())
        other.start()
        keep.start()
        for k in range(4):
            to_core(3, k, zorder[k]).wait_send()
        for msg in list(b_msgs.values()) + a_msgs:
            msg.wait_send()
        for zz in range(hops + 1):
            @pl.when(z < zz)
            def _():
                for p in range(2):
                    for near in range(2):
                        if zz > 0:
                            z_up[p, zz, near].wait_send()

            @pl.when(z > zz)
            def _():
                for p in range(2):
                    for near in range(2):
                        if zz < hops:
                            z_down[p, zz, near].wait_send()
        keep.wait()
        other.wait()

    bf = jnp.bfloat16
    n_send = 2 * 8 + 2 * 2 * 2 * hops + 2 + 1
    whole = pl.BlockSpec(memory_space=pltpu.VMEM)
    return pl.pallas_call(
        kernel,
        out_shape=[
            jax.ShapeDtypeStruct((rows, features), jnp.float32),
            jax.ShapeDtypeStruct((features, width), bf),
            jax.ShapeDtypeStruct((8, width), jnp.float32),
        ],
        in_specs=[pl.BlockSpec(memory_space=pl.ANY)] * 2 + [whole] * 3,
        out_specs=[pl.BlockSpec(memory_space=pl.ANY), whole, whole],
        scratch_shapes=[
            pltpu.VMEM((2, block, width), bf),
            pltpu.VMEM((2, block, features), bf),
            pltpu.VMEM((block, width), bf),
            pltpu.VMEM((features, width), jnp.float32),
            pltpu.VMEM((hops + 1, 2, 2, block, wing), bf),
            pltpu.VMEM((4, block, wing), bf),
            pltpu.VMEM((hops + 1, 2, 2, block, wing), bf),
            pltpu.VMEM((2, hops + 1, 2, rows, wing), bf),
            pltpu.VMEM((2, hops, 2, rows, wing), bf),
            pltpu.VMEM((2, hops, 2, rows, wing), bf),
            pltpu.VMEM((2, rows, wing), bf),
            pltpu.VMEM((block, wing), jnp.float32),
            pltpu.SemaphoreType.DMA((2, 2)),
            pltpu.SemaphoreType.DMA((16,)),
            pltpu.SemaphoreType.DMA((16,)),
            pltpu.SemaphoreType.DMA((n_send,)),
            pltpu.SemaphoreType.DMA((n_send,)),
            pltpu.SemaphoreType.DMA((1,)),
        ],
        compiler_params=pltpu.CompilerParams(collective_id=collective_id, has_side_effects=True, vmem_limit_bytes=60 << 20),
    )(
        lifted.reshape(hops + 1, 2, 2, block, width),
        rows_all.reshape(hops + 1, 2, 2, block, features),
        head_cols,
        local_ids[None],
        factors,
    )


def embed_gradient(columns, token_ids, vocab, block):
    features, tokens = columns.shape
    lanes = 128
    high_rows = -(-vocab // (8 * lanes)) * 8
    group = 2
    steps = tokens // block

    def kernel(columns_ref, ids_ref, out_ref, squares_ref):
        step = pl.program_id(0)
        ids = ids_ref[...]
        high = lax.broadcasted_iota(jnp.int32, (high_rows, block), 0) == lax.shift_right_logical(ids, 7)
        high = jnp.where(high, 1.0, 0.0).astype(jnp.bfloat16)
        low = lax.broadcasted_iota(jnp.int32, (lanes, block), 0) == jnp.bitwise_and(ids, lanes - 1)
        values = columns_ref[...].astype(jnp.float32)

        @pl.when(step == 0)
        def _():
            out_ref[...] = jnp.zeros_like(out_ref)

        for first in range(0, features, group):
            spread = jnp.concatenate(
                [jnp.where(low, values[f : f + 1], 0.0).astype(jnp.bfloat16) for f in range(first, first + group)], axis=0
            )
            term = lax.dot_general(high, spread, (((1,), (1,)), ((), ())), preferred_element_type=jnp.float32)
            for k in range(group):
                out_ref[first + k] += term[:, k * lanes : (k + 1) * lanes]

        @pl.when(step == steps - 1)
        def _():
            def turn(f, total):
                one = out_ref[f]
                return total + jnp.sum((one * one).reshape(high_rows // 8, 8, lanes), axis=0)
            squares_ref[...] = lax.fori_loop(0, features, turn, jnp.zeros((8, lanes), jnp.float32))

    sums, squares = pl.pallas_call(
        kernel,
        grid=(steps,),
        out_shape=[
            jax.ShapeDtypeStruct((features, high_rows, lanes), jnp.float32),
            jax.ShapeDtypeStruct((8, lanes), jnp.float32),
        ],
        in_specs=[pl.BlockSpec((features, block), lambda i: (0, i)), pl.BlockSpec((1, block), lambda i: (0, i))],
        out_specs=[
            pl.BlockSpec((features, high_rows, lanes), lambda i: (0, 0, 0)),
            pl.BlockSpec((8, lanes), lambda i: (0, 0)),
        ],
        compiler_params=pltpu.CompilerParams(vmem_limit_bytes=50 << 20),
    )(columns, token_ids[None])
    return sums[:, : vocab // lanes].reshape(features, vocab), squares


BOTH = ("dp", "seq")
mark_height = 8


def mark_rows(targets, loss_mask):
    own = targets.shape[0] // lax.axis_size("seq")
    first = lax.axis_index("seq") * own
    own_targets = lax.dynamic_slice_in_dim(targets, first, own)
    own_mask = lax.dynamic_slice_in_dim(loss_mask, first, own)
    rows = jnp.stack([own_targets // 256, own_targets % 256, own_mask]).astype(jnp.float32)
    return jnp.pad(rows, ((0, mark_height - 3), (0, 0)))[None]


def marks_of(gathered):
    rows = gathered[0].reshape(-1, mark_height, gathered.shape[2]).astype(jnp.float32)
    numbers = rows[:, :3].transpose(1, 0, 2).reshape(3, -1).astype(jnp.int32)
    return (numbers[0] * 256 + numbers[1], numbers[2])


def on_box():
    return lax.axis_size("dp") == 8 and lax.axis_size("seq") == 4


def gather_rows(tensors, portions, collective_id):
    if on_box():
        return gather_blocks(tensors, portions, collective_id)
    return gather_plain(tensors)


def gather_plain(tensors):
    return [lax.all_gather(t.astype(jnp.bfloat16), BOTH, axis=1, tiled=True) for t in tensors]


def scatter_rows(tensors, portions, collective_id):
    if on_box():
        devices = lax.axis_size("dp") * lax.axis_size("seq")
        rows = [t.shape[1] // devices for t in tensors]
        return scatter_blocks(tensors, portions, rows, collective_id)
    return scatter_plain(tensors)


def scatter_plain(tensors):
    return [
        lax.psum_scatter(t, BOTH, scatter_dimension=1, tiled=True).astype(jnp.float32) for t in tensors
    ]


def scatter_joined(tensors):
    square, expand, shrink = tensors
    width = square.shape[2]
    cut = [expand[:, :, k : k + width] for k in range(0, expand.shape[2], width)]
    both = lax.psum_scatter(
        jnp.concatenate([square] + cut), BOTH, scatter_dimension=1, tiled=True
    ).astype(jnp.float32)
    count = square.shape[0]
    return [
        both[:count],
        jnp.concatenate([both[k : k + 1] for k in range(count, both.shape[0])], axis=2),
        lax.psum_scatter(shrink, BOTH, scatter_dimension=1, tiled=True).astype(jnp.float32),
    ]


def weight_portions(square, expand, shrink, vectors, marks=0):
    split = 2 * square * 2 // 3
    first = [(1, 0, 1, 0, 2 * expand)]
    second = [(2, 0, 1, 0, 2 * shrink)]
    third = [(0, 0, 2, 0, 2 * square), (0, 2, 3, 0, split)]
    fourth = [(0, 3, 5, 0, 2 * square), (0, 2, 3, split, 2 * square)]
    if vectors:
        fourth.append((3, 0, 1, 0, 2 * vectors))
    if marks:
        fourth.append((4, 0, 1, 0, 2 * marks))
    return [first, second, third, fourth]


def row_portions(rows):
    ends = [0, rows * 5 // 8, rows * 10 // 8, rows * 13 // 8, 2 * rows]
    return [[(0, 0, 1, first, last)] for first, last in zip(ends, ends[1:])]


def as_rows(vectors):
    lanes = -(-vectors.shape[0] // 256) * 256
    return jnp.pad(vectors.T, ((0, 0), (0, lanes - vectors.shape[0])))[None]

EXACT_MATMUL = lax.Precision.HIGHEST
BETA_ONE = 0.9
BETA_TWO = 0.999
ADAM_EPS = 1e-08
WEIGHT_DECAY = 0.01
LEARN_RATES = (0.03, 0.03, 0.015, 0.5, 2.0, 0.05)
DECAY_FLAGS = (True, True, True, False, True, True)
param_stride = 11
head_tile = 1024
embed_block = 1024
scan_block = 256


def from_behind(value, axis, steps):
    count = lax.axis_size(axis)
    leading, last = (max(0, -steps), min(count, count - steps))
    return lax.ppermute(value, axis, [(source, source + steps) for source in range(leading, last)])


def carried_in(value, axis, join, neutral, backward):
    count, mine = (lax.axis_size(axis), lax.axis_index(axis))
    pieces = lax.all_gather(jnp.stack(value), axis)
    if backward:
        pieces = pieces[::-1]
        mine = count - 1 - mine
    running = neutral
    for position in range(count - 1):
        longer = join(running, tuple(pieces[position]))
        running = tuple(
            jnp.where(position < mine, new, old) for new, old in zip(longer, running)
        )
    return running


def layer_norm(values, gain, bias):
    centre = values - jnp.mean(values, axis=-1, keepdims=True)
    spread = jnp.mean(centre * centre, axis=-1, keepdims=True)
    return centre * lax.rsqrt(spread + 1e-05) * gain + bias


def matmul(left, right):
    return jnp.dot(left, right, preferred_element_type=jnp.float32)


def matmul_tn(left, right):
    return lax.dot_general(
        left, right, (((0,), (0,)), ((), ())), preferred_element_type=jnp.float32
    )


def matmul_nt(left, right):
    return lax.dot_general(
        left, right, (((1,), (1,)), ((), ())), preferred_element_type=jnp.float32
    )


def blend_all(normed, incoming, shares):
    earlier = jnp.concatenate([incoming, normed[:-1]], axis=0)
    return tuple(
        (
            normed * shares[member] + earlier * (1.0 - shares[member])
            for member in range(shares.shape[0])
        )
    )


def take_previous(normed):
    return from_behind(normed[-1:], "seq", 1)


def give_back(grad_first):
    return from_behind(grad_first, "seq", -1)


def block_ends(arriving_lookups, arriving_contents, logarithmic_fading_speed):
    decay_rate = jnp.exp(logarithmic_fading_speed)
    length = arriving_lookups.shape[0]
    ages = (length - 1.0 - jnp.arange(length, dtype=jnp.float32))[:, None]
    weight = jnp.exp(arriving_lookups - decay_rate * ages)
    return (jnp.sum(weight * arriving_contents, axis=0), jnp.sum(weight, axis=0))


def block_factor(logarithmic_fading_speed, length):
    return jnp.exp(-jnp.exp(logarithmic_fading_speed) * length)


def chain_combine(earlier, later):
    return (
        earlier[0] * later[2] + later[0],
        earlier[1] * later[2] + later[1],
        earlier[2] * later[2],
    )


def token_mixer_block(
    arriving_lookups,
    arriving_contents,
    logarithmic_fading_speed,
    present_reward,
    initial_numerator,
    initial_denominator,
):
    decay_rate = jnp.exp(logarithmic_fading_speed)
    length, channels = arriving_lookups.shape
    block_size = min(scan_block, length)
    block_count = length // block_size
    offsets = jnp.arange(block_size, dtype=jnp.float32)[:, None]
    lower_mask = (offsets > offsets.T).astype(jnp.float32)
    diagonal_amplifier = jnp.exp(present_reward)
    back_decay = jnp.exp(-decay_rate * (offsets - 1.0))
    carry_decay = jnp.exp(-decay_rate * offsets)
    tail_decay = jnp.exp(-decay_rate * (block_size - 1.0))
    full_decay = jnp.exp(-decay_rate * block_size)

    def sub_block(state, step_item):
        numerator, denominator = state
        key_block, value_block = step_item
        lifted = jnp.exp(key_block + decay_rate * offsets)
        prefix_sums = jnp.dot(
            lower_mask,
            jnp.concatenate([lifted * value_block, lifted], axis=1),
            precision=EXACT_MATMUL,
        )
        own_term = diagonal_amplifier * jnp.exp(key_block)
        top_part = (
            back_decay * prefix_sums[:, :channels]
            + carry_decay * numerator
            + own_term * value_block
        )
        low_part = back_decay * prefix_sums[:, channels:] + carry_decay * denominator + own_term
        next_num = tail_decay * jnp.sum(lifted * value_block, axis=0) + full_decay * numerator
        next_den = tail_decay * jnp.sum(lifted, axis=0) + full_decay * denominator
        return ((next_num, next_den), (top_part / low_part, low_part))

    shaped = (
        arriving_lookups.reshape(block_count, block_size, channels),
        arriving_contents.reshape(block_count, block_size, channels),
    )
    (end_num, end_den), (block_outs, denoms) = lax.scan(
        sub_block, (initial_numerator, initial_denominator), shaped
    )
    return (
        (block_outs.reshape(length, channels), end_num, end_den),
        denoms.reshape(length, channels),
    )


def layer_forward(stream, gathered):
    square, expand, shrink, params = gathered
    normed = layer_norm(stream, params[0], params[1])
    incoming_one = take_previous(normed)
    blended = blend_all(normed, incoming_one, params[2:5])
    mixed_key = blended[0].astype(jnp.bfloat16)
    mixed_value = blended[1].astype(jnp.bfloat16)
    mixed_gate = blended[2].astype(jnp.bfloat16)
    arriving_lookups = matmul(mixed_key, square[0])
    arriving_contents = matmul(mixed_value, square[1])
    gates_in = matmul(mixed_gate, square[2])
    length = arriving_lookups.shape[0]
    end_sums = block_ends(arriving_lookups, arriving_contents, params[5])
    zero_state = jnp.zeros_like(end_sums[0])
    one_state = jnp.ones_like(end_sums[0])
    factor = block_factor(params[5], length)
    initial_numerator, initial_denominator, spare_factor = carried_in(
        (end_sums[0], end_sums[1], factor),
        "seq",
        chain_combine,
        (zero_state, zero_state, one_state),
        False,
    )
    (mixed_out, spare_placeholder, spare_placeholder), spare_placeholder = token_mixer_block(
        arriving_lookups,
        arriving_contents,
        params[5],
        params[6],
        initial_numerator,
        initial_denominator,
    )
    gated = (jax.nn.sigmoid(gates_in) * mixed_out).astype(jnp.bfloat16)
    middle = stream + matmul(gated, square[3])
    normed_two = layer_norm(middle, params[7], params[8])
    incoming_two = take_previous(normed_two)
    blended_two = blend_all(normed_two, incoming_two, params[9:11])
    chan_key = blended_two[0].astype(jnp.bfloat16)
    chan_gate = blended_two[1].astype(jnp.bfloat16)
    pre_act = matmul(chan_key, expand)
    activated = jnp.square(jnp.maximum(pre_act, 0.0)).astype(jnp.bfloat16)
    chan_value = matmul(activated, shrink)
    gate_pre = matmul(chan_gate, square[4])
    result = middle + jax.nn.sigmoid(gate_pre) * chan_value
    saved = (
        stream,
        incoming_one,
        mixed_key,
        mixed_value,
        mixed_gate,
        arriving_lookups,
        arriving_contents,
        gates_in,
        initial_numerator,
        initial_denominator,
        gated,
        middle,
        incoming_two,
        chan_key,
        chan_gate,
        pre_act,
        activated,
        chan_value,
        gate_pre,
    )
    return (result, saved)


def norm_back(stream, incoming, params, first_row, share_rows, grads):
    normed, norm_pull = jax.vjp(layer_norm, stream, params[first_row], params[first_row + 1])
    shares = params[share_rows[0] : share_rows[1]]
    spare_placeholder, blend_pull = jax.vjp(blend_all, normed, incoming, shares)
    d_normed, d_incoming, d_shares = blend_pull(grads)
    from_next = give_back(d_incoming)
    d_normed = d_normed.at[-1].add(from_next[0])
    d_stream, d_gain, d_bias = norm_pull(d_normed)
    return (d_stream, jnp.stack([d_gain, d_bias]), d_shares)


def layer_backward(gradient, saved, gathered):
    square, expand, shrink, params = gathered
    (
        stream,
        incoming_one,
        mixed_key,
        mixed_value,
        mixed_gate,
        arriving_lookups,
        arriving_contents,
        gates_in,
        initial_numerator,
        initial_denominator,
        gated,
        middle,
        incoming_two,
        chan_key,
        chan_gate,
        pre_act,
        activated,
        chan_value,
        gate_pre,
    ) = saved
    gate_sig = jax.nn.sigmoid(gate_pre)
    d_value = (gradient * gate_sig).astype(jnp.bfloat16)
    d_gate_pre = (gradient * chan_value * gate_sig * (1.0 - gate_sig)).astype(jnp.bfloat16)
    g_shrink = matmul_tn(activated, d_value)
    d_active = matmul_nt(d_value, shrink)
    d_pre = (d_active * 2.0 * jnp.maximum(pre_act, 0.0)).astype(jnp.bfloat16)
    g_expand = matmul_tn(chan_key, d_pre)
    g_chan_gate = matmul_tn(chan_gate, d_gate_pre)
    d_chan_key = matmul_nt(d_pre, expand)
    d_chan_gate = matmul_nt(d_gate_pre, square[4])
    d_middle, second_norm_gradient, second_share_gradient = norm_back(
        middle, incoming_two, params, 7, (9, 11), (d_chan_key, d_chan_gate)
    )
    d_middle = d_middle + gradient
    d_output = d_middle.astype(jnp.bfloat16)
    g_output = matmul_tn(gated, d_output)
    d_gated = matmul_nt(d_output, square[3])
    (mixed_out, spare_placeholder, spare_placeholder), token_mixer_backward, denoms = jax.vjp(
        token_mixer_block,
        arriving_lookups,
        arriving_contents,
        params[5],
        params[6],
        initial_numerator,
        initial_denominator,
        has_aux=True,
    )
    gate_sig_one = jax.nn.sigmoid(gates_in)
    mixed_gradient = d_gated * gate_sig_one
    d_gates_in = (d_gated * mixed_out * gate_sig_one * (1.0 - gate_sig_one)).astype(jnp.bfloat16)
    length = arriving_lookups.shape[0]
    decay_rate = jnp.exp(params[5])
    carried = (
        jnp.exp(-decay_rate * jnp.arange(length, dtype=jnp.float32)[:, None])
        * mixed_gradient
        / denoms
    )
    zero_state = jnp.zeros_like(decay_rate)
    one_state = jnp.ones_like(decay_rate)
    factor = block_factor(params[5], length)
    following_numerator, following_denominator, spare_factor = carried_in(
        (jnp.sum(carried, axis=0), -jnp.sum(carried * mixed_out, axis=0), factor),
        "seq",
        chain_combine,
        (zero_state, zero_state, one_state),
        True,
    )
    (
        lookup_sensitivity,
        content_sensitivity,
        fading_sensitivity,
        reward_sensitivity,
        spare_placeholder,
        spare_placeholder,
    ) = token_mixer_backward((mixed_gradient, following_numerator, following_denominator))
    lookup_sensitivity = lookup_sensitivity.astype(jnp.bfloat16)
    content_sensitivity = content_sensitivity.astype(jnp.bfloat16)
    g_key = matmul_tn(mixed_key, lookup_sensitivity)
    g_value = matmul_tn(mixed_value, content_sensitivity)
    g_gate = matmul_tn(mixed_gate, d_gates_in)
    d_mixed_key = matmul_nt(lookup_sensitivity, square[0])
    d_mixed_value = matmul_nt(content_sensitivity, square[1])
    d_mixed_gate = matmul_nt(d_gates_in, square[2])
    d_stream, first_norm_gradient, first_share_gradient = norm_back(
        stream, incoming_one, params, 0, (2, 5), (d_mixed_key, d_mixed_value, d_mixed_gate)
    )
    d_stream = d_stream + d_middle
    g_square = jnp.stack([g_key, g_value, g_gate, g_output, g_chan_gate])
    g_params = jnp.concatenate(
        [
            first_norm_gradient,
            first_share_gradient,
            fading_sensitivity[None],
            reward_sensitivity[None],
            second_norm_gradient,
            second_share_gradient,
        ],
        axis=0,
    )
    return (d_stream, (g_square, g_expand, g_shrink, g_params))


def adam_update(weights, gradient, first, second, step_rate, decay_on):
    first_new = BETA_ONE * first + (1.0 - BETA_ONE) * gradient
    second_new = BETA_TWO * second + (1.0 - BETA_TWO) * gradient * gradient
    first_hat = first_new / (1.0 - BETA_ONE**STEP)
    second_hat = second_new / (1.0 - BETA_TWO**STEP)
    moved = first_hat / (jnp.sqrt(second_hat) + ADAM_EPS)
    if decay_on:
        moved = moved + WEIGHT_DECAY * weights
    return (weights - step_rate * moved, first_new, second_new)


def per_device(
    token_ids,
    targets,
    loss_mask,
    square_weights,
    expand_weights,
    shrink_weights,
    vector_params,
    embed_table,
    head_table,
    square_first,
    expand_first,
    shrink_first,
    vector_first,
    embed_first,
    head_first,
    square_second,
    expand_second,
    shrink_second,
    vector_second,
    embed_second,
    head_second,
):
    layers = square_weights.shape[0]
    global_rows = param_stride * layers
    total_tokens = token_ids.shape[0]

    vector_rows = vector_params.shape[0]
    square_own, expand_own, shrink_own = (
        square_weights.shape[2],
        expand_weights.shape[1],
        shrink_weights.shape[1],
    )

    def fetch_layer(layer_id):
        with_vectors = layer_id == 0
        shards = [
            square_weights[layer_id],
            expand_weights[layer_id][None],
            shrink_weights[layer_id][None],
        ]
        if with_vectors:
            shards.append(as_rows(vector_params))
            shards.append(mark_rows(targets, loss_mask))
        else:
            return gather_plain(shards)
        return gather_rows(
            shards,
            weight_portions(
                square_own,
                expand_own,
                shrink_own,
                with_vectors * square_own,
                with_vectors * mark_height,
            ),
            layer_id,
        )

    fetched = [fetch_layer(layer_id) for layer_id in range(layers)]
    vectors_all = fetched[0][3][0, :, :vector_rows].T.astype(jnp.float32)
    global_params = vectors_all[global_rows:]
    blocks = [
        (
            fetched[layer_id][0],
            fetched[layer_id][1][0],
            fetched[layer_id][2][0],
            vectors_all[layer_id * param_stride : (layer_id + 1) * param_stride],
        )
        for layer_id in range(layers)
    ]

    columns = jnp.take(embed_table.astype(jnp.bfloat16), token_ids, axis=1)
    embedded = lax.all_to_all(
        columns, ("dp", "seq"), split_axis=1, concat_axis=0, tiled=True
    ).T.astype(jnp.float32)
    stream, norm_pull_zero = jax.vjp(layer_norm, embedded, global_params[0], global_params[1])
    saved_layers = []
    for layer_id in range(layers):
        stream, saved = layer_forward(stream, blocks[layer_id])
        saved_layers.append(saved)
    normed, norm_pull_last = jax.vjp(layer_norm, stream, global_params[2], global_params[3])
    dp_count = lax.axis_size("dp")
    features, vocab_own = head_table.shape
    vocab_part = vocab_own // dp_count
    head_cut = head_table.astype(jnp.bfloat16).reshape(features, dp_count, vocab_part)
    head_cols = lax.all_to_all(
        head_cut.transpose(1, 0, 2), "dp", split_axis=0, concat_axis=0, tiled=True
    ).reshape(dp_count * features, vocab_part)
    own_rows = normed.shape[0]
    rows_all = gather_rows([normed[None]], row_portions(own_rows), 10)[0][0]
    all_targets, all_mask = marks_of(fetched[0][4])
    first_column = lax.axis_index("seq") * vocab_own + lax.axis_index("dp") * vocab_part
    local_ids = all_targets - first_column
    tile = min(head_tile, total_tokens)
    lifted, stats = head_forward(rows_all, head_cols, local_ids, tile, tile // 4)
    own_log = stats[0] + jnp.log(stats[1])
    log_total = exchange_everywhere(own_log.reshape(-1, 128), add_logs, 13).reshape(-1)
    counted = all_mask.astype(jnp.float32)
    picked_part = jnp.sum(counted * stats[2])
    weight_rows = counted / total_tokens
    factors = jnp.pad(
        jnp.stack(
            [
                jnp.exp(stats[0] - log_total) * weight_rows,
                (jnp.exp(stats[2] - log_total) - 1.0) * weight_rows,
            ]
        ),
        ((0, 6), (0, 0)),
    )
    if on_box():
        d_normed, grad_head, head_squares = head_backward_scattered(
            lifted, rows_all, head_cols, local_ids, factors, 11
        )
    else:
        d_rows, grad_head, head_squares = head_backward(
            lifted, rows_all, head_cols, local_ids, factors, tile, tile // 2
        )
        d_normed = scatter_plain([d_rows[None]])[0][0]
    g_head = (
        lax.all_to_all(
            grad_head.reshape(dp_count, features, vocab_part),
            "dp",
            split_axis=0,
            concat_axis=0,
            tiled=True,
        )
        .transpose(1, 0, 2)
        .reshape(features, vocab_own)
        .astype(jnp.float32)
    )
    d_stream, d_gain_last, d_bias_last = norm_pull_last(d_normed)
    layer_grads = [None] * layers
    vector_grads = [None] * layers
    d_embedded = d_stream
    for layer_id in reversed(range(layers)):
        d_stream, grads = layer_backward(d_stream, saved_layers[layer_id], blocks[layer_id])
        vector_grads[layer_id] = grads[3]
        low_grads = [
            grads[0].astype(jnp.bfloat16),
            grads[1].astype(jnp.bfloat16)[None],
            grads[2].astype(jnp.bfloat16)[None],
        ]
        if layer_id == 0:
            d_embedded, d_gain_zero, d_bias_zero = norm_pull_zero(d_stream)
            all_vectors = jnp.concatenate(
                vector_grads
                + [jnp.stack([d_gain_zero, d_bias_zero, d_gain_last, d_bias_last])],
                axis=0,
            )
            low_grads.append(as_rows(all_vectors).astype(jnp.bfloat16))
        if layer_id > 0:
            layer_grads[layer_id] = scatter_joined(low_grads)
        else:
            layer_grads[layer_id] = scatter_rows(
                low_grads, weight_portions(square_own, expand_own, shrink_own, square_own), layers
            )
    back_columns = lax.all_to_all(
        d_embedded.T.astype(jnp.bfloat16), ("dp", "seq"), split_axis=0, concat_axis=1, tiled=True
    )
    g_embed, embed_squares = embed_gradient(
        back_columns, token_ids, embed_table.shape[1], min(embed_block, total_tokens)
    )
    g_square = jnp.stack([layer_grads[layer_id][0] for layer_id in range(layers)])
    g_expand = jnp.concatenate([layer_grads[layer_id][1] for layer_id in range(layers)])
    g_shrink = jnp.concatenate([layer_grads[layer_id][2] for layer_id in range(layers)])
    g_vector = layer_grads[0][3][0, :, :vector_rows].T
    gradients = (g_square, g_expand, g_shrink, g_vector, g_embed, g_head)
    square_part = jnp.sum(embed_squares) + jnp.sum(head_squares)
    for gradient in gradients[:4]:
        square_part = square_part + jnp.sum(gradient * gradient)
    parts = jnp.stack([square_part, picked_part])
    parts = exchange_everywhere(jnp.broadcast_to(jnp.pad(parts, (0, 6))[:, None], (8, 128)), jnp.add, 12)
    square_sum = parts[0, 0]
    loss_sum = jnp.sum(counted * log_total) - parts[1, 0]
    grad_norm = jnp.sqrt(square_sum)
    scale = jnp.minimum(1.0, 0.5 / math.sqrt(total_tokens) / (grad_norm + 1e-06))
    weights = (
        square_weights,
        expand_weights,
        shrink_weights,
        vector_params,
        embed_table,
        head_table,
    )
    firsts = (square_first, expand_first, shrink_first, vector_first, embed_first, head_first)
    seconds = (
        square_second,
        expand_second,
        shrink_second,
        vector_second,
        embed_second,
        head_second,
    )
    updated = [
        adam_update(
            weights[slot],
            gradients[slot] * scale,
            firsts[slot],
            seconds[slot],
            LEARN_RATES[slot],
            DECAY_FLAGS[slot],
        )
        for slot in range(6)
    ]
    return (
        loss_sum,
        grad_norm,
        updated[0][0],
        updated[1][0],
        updated[2][0],
        updated[3][0],
        updated[4][0],
        updated[5][0],
        updated[0][1],
        updated[1][1],
        updated[2][1],
        updated[3][1],
        updated[4][1],
        updated[5][1],
        updated[0][2],
        updated[1][2],
        updated[2][2],
        updated[3][2],
        updated[4][2],
        updated[5][2],
    )


def solution(mesh):
    placed = (
        P(),
        P("dp"),
        P("dp"),
        P(None, None, ("dp", "seq"), None),
        P(None, ("dp", "seq"), None),
        P(None, ("dp", "seq"), None),
        P(None, ("dp", "seq")),
        P(("dp", "seq"), None),
        P("dp", "seq"),
        P(None, None, ("dp", "seq"), None),
        P(None, ("dp", "seq"), None),
        P(None, ("dp", "seq"), None),
        P(None, ("dp", "seq")),
        P(("dp", "seq"), None),
        P("dp", "seq"),
        P(None, None, ("dp", "seq"), None),
        P(None, ("dp", "seq"), None),
        P(None, ("dp", "seq"), None),
        P(None, ("dp", "seq")),
        P(("dp", "seq"), None),
        P("dp", "seq"),
    )
    return jax.shard_map(
        per_device,
        mesh=mesh,
        in_specs=placed,
        out_specs=(
            P(),
            P(),
            P(None, None, ("dp", "seq"), None),
            P(None, ("dp", "seq"), None),
            P(None, ("dp", "seq"), None),
            P(None, ("dp", "seq")),
            P(("dp", "seq"), None),
            P("dp", "seq"),
            P(None, None, ("dp", "seq"), None),
            P(None, ("dp", "seq"), None),
            P(None, ("dp", "seq"), None),
            P(None, ("dp", "seq")),
            P(("dp", "seq"), None),
            P("dp", "seq"),
            P(None, None, ("dp", "seq"), None),
            P(None, ("dp", "seq"), None),
            P(None, ("dp", "seq"), None),
            P(None, ("dp", "seq")),
            P(("dp", "seq"), None),
            P("dp", "seq"),
        ),
        check_vma=False,
    )
```

```python
import functools
import math

import jax
import jax.numpy as jnp
from jax import lax
from jax.experimental import pallas as pl
from jax.experimental.pallas import tpu as pltpu
from jax.sharding import PartitionSpec as P

STEP = 10
ON_MESH = pl.DeviceIdType.MESH


def place():
    dp, seq = lax.axis_index("dp"), lax.axis_index("seq")
    return dp, seq, dp // 2, lax.rem(dp, 2), seq // 2, lax.rem(seq, 2)


def greet(partners, extra):
    barrier = pltpu.get_barrier_semaphore()
    for partner in partners:
        pl.semaphore_signal(barrier, inc=1, device_id=partner, device_id_type=ON_MESH)
    for exists, partner in extra:
        @pl.when(exists)
        def _():
            pl.semaphore_signal(barrier, inc=1, device_id=partner, device_id_type=ON_MESH)
    peers = len(partners)
    for exists, partner in extra:
        peers = peers + exists.astype(jnp.int32)
    pl.semaphore_wait(barrier, peers)


class Sems:
    def __init__(self, send, recv, local):
        self.send, self.recv, self.local = send, recv, local
        self.ns = self.nr = self.nl = 0

    def pair(self):
        self.ns += 1
        return self.send.at[self.ns - 1], self.recv.at[self.ns - 1]

    def own(self):
        self.nl += 1
        return self.local.at[self.nl - 1]


def gather_blocks(tensors, portions, collective_id):
    count = len(tensors)
    dims = [t.shape for t in tensors]
    hops = 3
    pieces_total = sum(len(p) for p in portions)
    n_send = count + count + pieces_total * (7 + 2 * hops + 7)

    def kernel(*refs):
        ins, outs = refs[:count], refs[count : 2 * count]
        wide = refs[2 * count : 3 * count]
        half = refs[3 * count : 4 * count]
        send, recv, local = refs[4 * count :]
        dp, seq, z, y, x, c = place()
        core = (dp, seq + 1 - 2 * c)
        xway = (dp, seq + 2 - 4 * x)
        yway = (dp + 1 - 2 * y, seq)
        up, down = (dp + 2, seq), (dp - 2, seq)
        has_up, has_down = z < hops, z > 0
        greet([core, xway, yway], [(has_up, up), (has_down, down)])
        sems = Sems(send, recv, local)

        def cols(t, side):
            width = dims[t][2] // 2
            return pl.ds(pl.multiple_of(side * width, 128), width)

        first = []
        for t in range(count):
            rows = pl.ds(pl.multiple_of(c * dims[t][1], 8), dims[t][1])
            mine = pltpu.make_async_copy(ins[t].at[:, :, cols(t, c)], wide[t].at[:, rows, :], sems.own())
            ss, rs = sems.pair()
            other = pltpu.make_async_remote_copy(
                src_ref=ins[t].at[:, :, cols(t, 1 - c)], dst_ref=wide[t].at[:, rows, :],
                send_sem=ss, recv_sem=rs, device_id=core, device_id_type=ON_MESH)
            other.start()
            mine.start()
            first.append((mine, other))
        core_sems = [sems.pair() for t in range(count)]
        stay = []
        for t in range(count):
            first[t][0].wait()
            first[t][1].wait()
            half[t][...] = wide[t][...].astype(jnp.bfloat16)
            own = pltpu.make_async_copy(half[t], outs[t].at[:, z, y, x, :, cols(t, c)], sems.own())
            own.start()
            stay.append(own)

        def block(piece, zz, yy, xx):
            t, m0, m1, r0, r1 = piece
            return outs[t].at[m0:m1, zz, yy, xx, r0:r1, cols(t, c)]

        def to_core(p, zz, yy, xx, source=None):
            for piece in portions[p]:
                t = piece[0]
                region = block(piece, zz, yy, xx)
                pltpu.make_async_remote_copy(
                    src_ref=region if source is None else source(piece), dst_ref=region,
                    send_sem=core_sems[t][0], recv_sem=core_sems[t][1], device_id=core, device_id_type=ON_MESH).start()

        def message(p, where, device, source=None):
            copies = []
            for piece in portions[p]:
                ss, rs = sems.pair()
                region = block(piece, *where)
                copies.append(pltpu.make_async_remote_copy(
                    src_ref=region if source is None else source(piece), dst_ref=region,
                    send_sem=ss, recv_sem=rs, device_id=device, device_id_type=ON_MESH))
            return copies

        def start(copies):
            for copy in copies:
                copy.start()

        def arrive(copies):
            for copy in copies:
                copy.wait_recv()

        def sent(copies):
            for copy in copies:
                copy.wait_send()

        def from_half(piece):
            t, m0, m1, r0, r1 = piece
            return half[t].at[m0:m1, r0:r1, :]

        both = slice(0, 2)
        a_way, b_way = (yway, xway) * 2, (xway, yway) * 2
        ways = range(len(portions))

        def one_of(p, zz):
            return (zz, y, x)

        def pair_of(p, zz):
            return (zz, both, x) if p % 2 == 0 else (zz, y, both)

        def other_of(p, zz):
            return (zz, 1 - y, x) if p % 2 == 0 else (zz, y, 1 - x)

        def far_of(p, zz):
            return (zz, both, 1 - x) if p % 2 == 0 else (zz, 1 - y, both)

        def late(p):
            return p >= 2

        def event_z(e):
            return z if e == 0 else z - e if e <= hops else z + e - hops

        def happens(e):
            return z - e >= 0 if e <= hops else z + e - hops <= hops

        def when(e, what):
            if e == 0:
                what()
            else:
                pl.when(happens(e))(what)

        events = range(1 + 2 * hops)
        a_msgs, z_msgs, b_msgs = {}, {}, {}
        for p in ways:
            held = one_of if late(p) else pair_of
            for e in events if late(p) else (0,):
                a_msgs[p, e] = message(p, one_of(p, event_z(e)), a_way[p], from_half if e == 0 else None)
            for k in range(hops):
                source = from_half if late(p) and k == 0 else None
                z_msgs[p, 1 + k] = message(p, held(p, z - k), up, source)
                z_msgs[p, 1 + hops + k] = message(p, held(p, z + k), down, source)
            for e in events:
                b_msgs[p, e] = message(p, pair_of(p, event_z(e)), b_way[p])

        def start_z(p, e):
            @pl.when(has_up if e <= hops else has_down)
            def _():
                start(z_msgs[p, e])

        for p in ways:
            if late(p):
                start_z(p, 1)
                start_z(p, 1 + hops)
            start(a_msgs[p, 0])
        for own in stay:
            own.wait()
        for p in ways:
            to_core(p, z, y, x, from_half)
        for p in ways:
            if not late(p):
                arrive(a_msgs[p, 0])
                start_z(p, 1)
                start_z(p, 1 + hops)
                start(b_msgs[p, 0])
                to_core(p, *other_of(p, z))

        def z_event(p, e):
            def turn():
                arrive(z_msgs[p, e])
                if e % hops:
                    start_z(p, e + 1)
                if late(p):
                    start(a_msgs[p, e])
                    to_core(p, *one_of(p, event_z(e)))
                else:
                    start(b_msgs[p, e])
                    to_core(p, *pair_of(p, event_z(e)))
            when(e, turn)

        def a_event(p, e):
            def turn():
                arrive(a_msgs[p, e])
                start(b_msgs[p, e])
                to_core(p, *other_of(p, event_z(e)))
            when(e, turn)

        def b_event(p, e):
            def turn():
                arrive(b_msgs[p, e])
                to_core(p, *far_of(p, event_z(e)))
            when(e, turn)

        def at(hop):
            return (0,) if hop == 0 else (hop, hops + hop)

        for hop in range(hops + 3):
            if 1 <= hop <= hops:
                for p in ways:
                    for e in at(hop):
                        z_event(p, e)
            if hop - 1 in range(hops + 1):
                for p in ways:
                    for e in at(hop - 1):
                        if late(p):
                            a_event(p, e)
                        else:
                            b_event(p, e)
            if hop - 2 in range(hops + 1):
                for p in ways:
                    for e in at(hop - 2):
                        if late(p):
                            b_event(p, e)

        for (p, e), msg in list(a_msgs.items()) + list(b_msgs.items()):
            when(e, functools.partial(sent, msg))
        for (p, e), msg in z_msgs.items():
            k = (e - 1) % hops
            going = (z - k >= 0) & has_up if e <= hops else (z + k <= hops) & has_down
            pl.when(going)(functools.partial(sent, msg))
        for t in range(count):
            whole = pltpu.make_async_remote_copy(
                src_ref=outs[t].at[:, :, :, :, :, cols(t, c)], dst_ref=outs[t].at[:, :, :, :, :, cols(t, 1 - c)],
                send_sem=core_sems[t][0], recv_sem=core_sems[t][1], device_id=core, device_id_type=ON_MESH)
            whole.wait_send()
            whole.wait_recv()

    outs = pl.pallas_call(
        kernel,
        out_shape=[jax.ShapeDtypeStruct((m, hops + 1, 2, 2, 2 * r, w), jnp.bfloat16) for m, r, w in dims],
        in_specs=[pl.BlockSpec(memory_space=pl.ANY)] * count,
        out_specs=[pl.BlockSpec(memory_space=pl.ANY)] * count,
        scratch_shapes=[pltpu.VMEM((m, 2 * r, w // 2), jnp.float32) for m, r, w in dims]
        + [pltpu.VMEM((m, 2 * r, w // 2), jnp.bfloat16) for m, r, w in dims]
        + [pltpu.SemaphoreType.DMA((n_send,)), pltpu.SemaphoreType.DMA((n_send,)), pltpu.SemaphoreType.DMA((2 * count,))],
        compiler_params=pltpu.CompilerParams(collective_id=collective_id, has_side_effects=True, vmem_limit_bytes=40 << 20),
    )(*tensors)
    return [o.reshape(m, (hops + 1) * 8 * r, w) for o, (m, r, w) in zip(outs, dims)]


def scatter_blocks(tensors, portions, rows_own, collective_id):
    count = len(tensors)
    hops = 3
    dims = [(t.shape[0], r, t.shape[2]) for t, r in zip(tensors, rows_own)]
    views = [t.reshape(m, hops + 1, 2, 2, 2 * r, w) for t, (m, r, w) in zip(tensors, dims)]
    pieces_total = sum(len(p) for p in portions)
    n_send = pieces_total * (2 + 4 + 2 * hops + 4) + count
    n_local = pieces_total * 2 + count
    ways = range(len(portions))
    flat = [(p, piece) for p in ways for piece in portions[p]]
    flat_dims = [(piece[2] - piece[1], piece[4] - piece[3], dims[piece[0]][2] // 2) for _, piece in flat]

    def kernel(*refs):
        ins, outs = refs[:count], refs[count : 2 * count]
        k0 = 2 * count
        acc = refs[k0 : k0 + count]
        crecv = refs[k0 + count : k0 + 2 * count]
        fin = refs[k0 + 2 * count : k0 + 3 * count]
        k0 += 3 * count
        n = len(flat)
        b_all, u_all, d_all, a_all = (refs[k0 + i * n : k0 + (i + 1) * n] for i in range(4))
        send, recv, local = refs[k0 + 4 * n :]
        index = {}
        for i, (p, piece) in enumerate(flat):
            index.setdefault(p, []).append((i, piece))
        dp, seq, z, y, x, c = place()
        core = (dp, seq + 1 - 2 * c)
        xway = (dp, seq + 2 - 4 * x)
        yway = (dp + 1 - 2 * y, seq)
        up, down = (dp + 2, seq), (dp - 2, seq)
        has_up, has_down = z < hops, z > 0
        greet([core, xway, yway], [(has_up, up), (has_down, down)])
        sems = Sems(send, recv, local)
        a_way, b_way = (yway, xway) * 2, (xway, yway) * 2

        def cols(t, side):
            width = dims[t][2] // 2
            return pl.ds(pl.multiple_of(side * width, 128), width)

        def remote(src, dst, device):
            ss, rs = sems.pair()
            return pltpu.make_async_remote_copy(src_ref=src, dst_ref=dst, send_sem=ss, recv_sem=rs,
                                                device_id=device, device_id_type=ON_MESH)

        def place_of(p, zz, a, b):
            return (zz, a, b) if p % 2 == 0 else (zz, b, a)

        own_a, own_b = (y, x) * 2, (x, y) * 2

        def late(p):
            return p >= 2


        def add(dst, src, lead):
            def turn(i, _):
                where, rest = [], i
                for size in reversed(lead):
                    where.append(lax.rem(rest, size))
                    rest = rest // size
                where = tuple(reversed(where))
                dst[where] = (dst[where].astype(jnp.float32) + src[where].astype(jnp.float32)).astype(dst.dtype)
                return 0
            total = 1
            for size in lead:
                total *= size
            lax.fori_loop(0, total, turn, 0)

        everyz, both = slice(0, hops + 1), slice(0, 2)
        chunks = {}
        for far in (1, 0):
            for p in ways:
                b = own_b[p] if far == 0 else 1 - own_b[p]
                made = []
                for i, piece in index[p]:
                    t, m0, m1, r0, r1 = piece
                    where = (slice(m0, m1),) + place_of(p, everyz, both, b) + (slice(r0, r1),)
                    there = remote(ins[t].at[where + (cols(t, 1 - c),)], crecv[t].at[where], core)
                    here = pltpu.make_async_copy(ins[t].at[where + (cols(t, c),)], acc[t].at[where], sems.own())
                    there.start()
                    here.start()
                    made.append((there, here, piece, where))
                chunks[far, p] = made

        def core_add(far, p):
            for there, here, piece, where in chunks[far, p]:
                t, m0, m1, r0, r1 = piece
                there.wait_recv()
                here.wait()
                add(acc[t].at[where], crecv[t].at[where], (m1 - m0, hops + 1, 2))

        zorder = (3, 0, 2, 1)
        b_msgs = {}
        for p in ways:
            core_add(1, p)
            for zz in zorder:
                msgs = []
                for i, (t, m0, m1, r0, r1) in index[p]:
                    src = acc[t].at[(slice(m0, m1),) + place_of(p, zz, both, 1 - own_b[p]) + (slice(r0, r1),)]
                    msgs.append(remote(src, b_all[i].at[:, zz], b_way[p]))
                for msg in msgs:
                    msg.start()
                b_msgs[p, zz] = msgs
        for p in ways:
            core_add(0, p)

        def b_add(p, zz):
            for msg in b_msgs[p, zz]:
                msg.wait_recv()
            for i, (t, m0, m1, r0, r1) in index[p]:
                dst = acc[t].at[(slice(m0, m1),) + place_of(p, zz, both, own_b[p]) + (slice(r0, r1),)]
                add(dst, b_all[i].at[:, zz], (m1 - m0, 2))

        def mine(p, i, piece, zz):
            t, m0, m1, r0, r1 = piece
            a = own_a[p] if late(p) else both
            return acc[t].at[(slice(m0, m1),) + place_of(p, zz, a, own_b[p]) + (slice(r0, r1),)]

        def landing(p, land, i, zz):
            return land[i].at[:, zz, 0] if late(p) else land[i].at[:, zz]

        a_msgs = {}

        def a_start(p, zz):
            msgs = []
            for i, (t, m0, m1, r0, r1) in index[p]:
                src = acc[t].at[(slice(m0, m1),) + place_of(p, zz, 1 - own_a[p], own_b[p]) + (slice(r0, r1),)]
                msgs.append(remote(src, a_all[i].at[:, zz if late(p) else 0], a_way[p]))
            for msg in msgs:
                msg.start()
            a_msgs[p, zz if late(p) else 0] = msgs

        def a_add(p, zz):
            for msg in a_msgs[p, zz]:
                msg.wait_recv()
            for i, piece in index[p]:
                add(mine(p, i, piece, zz), a_all[i].at[:, zz], (piece[2] - piece[1],))

        up_msgs, down_msgs = {}, {}
        for p in ways:
            for zz in range(hops + 1):
                up_msgs[p, zz] = [remote(mine(p, i, piece, zz), landing(p, u_all, i, zz), up) for i, piece in index[p]] if zz > 0 else None
                down_msgs[p, zz] = [remote(mine(p, i, piece, zz), landing(p, d_all, i, zz), down) for i, piece in index[p]] if zz < hops else None

        def z_add(p, zz, msgs, land):
            for msg in msgs[p, zz]:
                msg.wait_recv()
            for i, piece in index[p]:
                lead = (piece[2] - piece[1],) if late(p) else (piece[2] - piece[1], 2)
                add(mine(p, i, piece, zz), landing(p, land, i, zz), lead)

        def up_send(p, zz):
            @pl.when(z < zz)
            def _():
                @pl.when(z > 0)
                def _():
                    z_add(p, zz, up_msgs, u_all)
                for msg in up_msgs[p, zz]:
                    msg.start()

        def down_send(p, zz):
            @pl.when(z > zz)
            def _():
                @pl.when(z < hops)
                def _():
                    z_add(p, zz, down_msgs, d_all)
                for msg in down_msgs[p, zz]:
                    msg.start()

        early_ways, late_ways = [p for p in ways if not late(p)], [p for p in ways if late(p)]
        for zz in zorder[:2]:
            for p in ways:
                b_add(p, zz)
                if late(p):
                    a_start(p, zz)
                elif zz == 3:
                    up_send(p, 3)
                else:
                    down_send(p, 0)
        for zz in zorder[2:]:
            for p in ways:
                b_add(p, zz)
                if late(p):
                    a_start(p, zz)
                elif zz == 2:
                    up_send(p, 2)
                else:
                    down_send(p, 1)
        for p in late_ways:
            a_add(p, 3)
            up_send(p, 3)
            a_add(p, 0)
            down_send(p, 0)
        for p in early_ways:
            up_send(p, 1)
            down_send(p, 2)
        for p in late_ways:
            a_add(p, 2)
            up_send(p, 2)
            a_add(p, 1)
            down_send(p, 1)
        for p in late_ways:
            up_send(p, 1)
            down_send(p, 2)
        for p in ways:
            for zz in range(hops + 1):
                @pl.when(z == zz)
                def _():
                    if zz > 0:
                        z_add(p, zz, up_msgs, u_all)
                    if zz < hops:
                        z_add(p, zz, down_msgs, d_all)
            if not late(p):
                a_start(p, z)
        for p in late_ways:
            for i, (t, m0, m1, r0, r1) in index[p]:
                for m in range(m0, m1):
                    fin[t][m, r0:r1, :] = acc[t][(m,) + place_of(p, z, own_a[p], own_b[p]) + (slice(r0, r1),)].astype(jnp.float32)
        for p in early_ways:
            for msg in a_msgs[p, 0]:
                msg.wait_recv()
            for i, (t, m0, m1, r0, r1) in index[p]:
                for m in range(m0, m1):
                    part = acc[t][(m,) + place_of(p, z, own_a[p], own_b[p]) + (slice(r0, r1),)]
                    fin[t][m, r0:r1, :] = part.astype(jnp.float32) + a_all[i][m - m0, 0].astype(jnp.float32)
        last = []
        for t in range(count):
            r = dims[t][1]
            other = remote(fin[t].at[:, pl.ds(pl.multiple_of((1 - c) * r, 8), r), :], outs[t].at[:, :, cols(t, c)], core)
            keep = pltpu.make_async_copy(fin[t].at[:, pl.ds(pl.multiple_of(c * r, 8), r), :], outs[t].at[:, :, cols(t, c)], sems.own())
            other.start()
            keep.start()
            last.append((other, keep))
        for made in chunks.values():
            for there, here, piece, where in made:
                there.wait_send()
        for msgs in list(b_msgs.values()) + list(a_msgs.values()):
            for msg in msgs:
                msg.wait_send()
        for p in ways:
            for zz in range(hops + 1):
                if zz > 0:
                    @pl.when(z < zz)
                    def _():
                        for msg in up_msgs[p, zz]:
                            msg.wait_send()
                if zz < hops:
                    @pl.when(z > zz)
                    def _():
                        for msg in down_msgs[p, zz]:
                            msg.wait_send()
        for other, keep in last:
            keep.wait()
            other.wait()

    bf = jnp.bfloat16
    outs = pl.pallas_call(
        kernel,
        out_shape=[jax.ShapeDtypeStruct((m, r, w), jnp.float32) for m, r, w in dims],
        in_specs=[pl.BlockSpec(memory_space=pl.ANY)] * count,
        out_specs=[pl.BlockSpec(memory_space=pl.ANY)] * count,
        scratch_shapes=[pltpu.VMEM((m, hops + 1, 2, 2, 2 * r, w // 2), bf) for m, r, w in dims]
        + [pltpu.VMEM((m, hops + 1, 2, 2, 2 * r, w // 2), bf) for m, r, w in dims]
        + [pltpu.VMEM((m, 2 * r, w // 2), jnp.float32) for m, r, w in dims]
        + [pltpu.VMEM((m, hops + 1, 2, r, w), bf) for m, r, w in flat_dims] * 3
        + [pltpu.VMEM((m, hops + 1, r, w), bf) for m, r, w in flat_dims]
        + [pltpu.SemaphoreType.DMA((n_send,)), pltpu.SemaphoreType.DMA((n_send,)), pltpu.SemaphoreType.DMA((n_local,))],
        compiler_params=pltpu.CompilerParams(collective_id=collective_id, has_side_effects=True, vmem_limit_bytes=60 << 20),
    )(*views)
    return list(lax.optimization_barrier(outs))


def exchange_everywhere(value, combine, collective_id):
    sizes = (("dp", lax.axis_size("dp")), ("seq", lax.axis_size("seq")))
    steps = [(axis, 1 << bit) for axis, size in reversed(sizes) for bit in range(size.bit_length() - 1)]

    def kernel(in_ref, out_ref, leave, land, send, recv):
        dp, seq = lax.axis_index("dp"), lax.axis_index("seq")
        partners = []
        for axis, step in steps:
            mine = dp if axis == "dp" else seq
            other = mine + step - 2 * step * lax.rem(mine // step, 2)
            partners.append((other, seq) if axis == "dp" else (dp, other))
        greet(partners, [])
        leave[0] = in_ref[...]
        for k, partner in enumerate(partners):
            copy = pltpu.make_async_remote_copy(
                src_ref=leave.at[k],
                dst_ref=land.at[k],
                send_sem=send.at[k],
                recv_sem=recv.at[k],
                device_id=partner,
                device_id_type=ON_MESH,
            )
            copy.start()
            copy.wait()
            both = combine(leave[k], land[k])
            if k + 1 < len(steps):
                leave[k + 1] = both
            else:
                out_ref[...] = both

    n = len(steps)
    return pl.pallas_call(
        kernel,
        out_shape=jax.ShapeDtypeStruct(value.shape, jnp.float32),
        in_specs=[pl.BlockSpec(memory_space=pltpu.VMEM)],
        out_specs=pl.BlockSpec(memory_space=pltpu.VMEM),
        scratch_shapes=[
            pltpu.VMEM((n,) + value.shape, jnp.float32),
            pltpu.VMEM((n,) + value.shape, jnp.float32),
            pltpu.SemaphoreType.DMA((n,)),
            pltpu.SemaphoreType.DMA((n,)),
        ],
        compiler_params=pltpu.CompilerParams(collective_id=collective_id, has_side_effects=True),
    )(value)


def add_logs(left, right):
    return jnp.maximum(left, right) + jnp.log(1.0 + jnp.exp(-jnp.abs(left - right)))


def head_forward(rows_all, head_cols, masked, local_ids, tile, sub):
    tokens, features = rows_all.shape
    width = head_cols.shape[1]

    def kernel(rows_ref, head_ref, masked_ref, ids_ref, p_ref, stats_ref):
        ids = jnp.transpose(jnp.broadcast_to(ids_ref[...], (128, tile)))[:, :1]
        lane = lax.broadcasted_iota(jnp.int32, (sub, 128), 1)
        column = lax.broadcasted_iota(jnp.int32, (sub, width), 1)
        for part in range(tile // sub):
            here = slice(part * sub, (part + 1) * sub)
            logits = jnp.dot(rows_ref[here, :], head_ref[...], preferred_element_type=jnp.float32)
            logits = logits + masked_ref[...]
            top = jnp.max(logits, axis=1, keepdims=True)
            picked = jnp.sum(jnp.where(column == ids[here], logits, 0.0), axis=1, keepdims=True)
            lifted = jnp.exp(logits - top)
            spread = jnp.sum(lifted, axis=1, keepdims=True)
            p_ref[here, :] = lifted.astype(jnp.bfloat16)
            table = jnp.where(lane == 0, top, jnp.where(lane == 1, spread, picked))
            stats_ref[:, here] = jnp.transpose(table)[:8]

    return pl.pallas_call(
        kernel,
        grid=(tokens // tile,),
        out_shape=[
            jax.ShapeDtypeStruct((tokens, width), jnp.bfloat16),
            jax.ShapeDtypeStruct((8, tokens), jnp.float32),
        ],
        in_specs=[
            pl.BlockSpec((tile, features), lambda i: (i, 0)),
            pl.BlockSpec((features, width), lambda i: (0, 0)),
            pl.BlockSpec((1, width), lambda i: (0, 0)),
            pl.BlockSpec((1, tile), lambda i: (0, i)),
        ],
        out_specs=[
            pl.BlockSpec((tile, width), lambda i: (i, 0)),
            pl.BlockSpec((8, tile), lambda i: (0, i)),
        ],
        compiler_params=pltpu.CompilerParams(vmem_limit_bytes=50 << 20),
    )(rows_all, head_cols, masked, local_ids[None])


def head_backward(lifted, rows_all, head_cols, local_ids, factors, tile, sub):
    tokens, width = lifted.shape
    features = rows_all.shape[1]
    steps = tokens // tile

    def kernel(p_ref, rows_ref, head_ref, ids_ref, factor_ref, d_rows_ref, d_head_ref, squares_ref, d_logits, total):
        step = pl.program_id(0)
        ids = jnp.transpose(jnp.broadcast_to(ids_ref[...], (128, tile)))[:, :1]
        scales = jnp.transpose(jnp.concatenate([factor_ref[...]] * 16, axis=0))
        scale, hit = scales[:, :1], scales[:, 1:2]
        column = lax.broadcasted_iota(jnp.int32, (sub, width), 1)
        for part in range(tile // sub):
            here = slice(part * sub, (part + 1) * sub)
            d_logits[here, :] = jnp.where(
                column == ids[here], hit[here], p_ref[here, :].astype(jnp.float32) * scale[here]
            ).astype(jnp.bfloat16)
            d_rows_ref[here, :] = lax.dot_general(
                d_logits[here, :], head_ref[...], (((1,), (1,)), ((), ())), preferred_element_type=jnp.float32
            ).astype(jnp.bfloat16)
        term = lax.dot_general(
            rows_ref[...], d_logits[...], (((0,), (0,)), ((), ())), preferred_element_type=jnp.float32
        )

        @pl.when(step == 0)
        def _():
            total[...] = term

        @pl.when(step > 0)
        def _():
            total[...] += term

        @pl.when(step == steps - 1)
        def _():
            low = total[...].astype(jnp.bfloat16)
            d_head_ref[...] = low
            wide = low.astype(jnp.float32)
            squares_ref[...] = jnp.sum((wide * wide).reshape(features // 8, 8, width), axis=0)

    return pl.pallas_call(
        kernel,
        grid=(steps,),
        out_shape=[
            jax.ShapeDtypeStruct((tokens, features), jnp.bfloat16),
            jax.ShapeDtypeStruct((features, width), jnp.bfloat16),
            jax.ShapeDtypeStruct((8, width), jnp.float32),
        ],
        in_specs=[
            pl.BlockSpec((tile, width), lambda i: (i, 0)),
            pl.BlockSpec((tile, features), lambda i: (i, 0)),
            pl.BlockSpec((features, width), lambda i: (0, 0)),
            pl.BlockSpec((1, tile), lambda i: (0, i)),
            pl.BlockSpec((8, tile), lambda i: (0, i)),
        ],
        out_specs=[
            pl.BlockSpec((tile, features), lambda i: (i, 0)),
            pl.BlockSpec((features, width), lambda i: (0, 0)),
            pl.BlockSpec((8, width), lambda i: (0, 0)),
        ],
        scratch_shapes=[pltpu.VMEM((tile, width), jnp.bfloat16), pltpu.VMEM((features, width), jnp.float32)],
        compiler_params=pltpu.CompilerParams(vmem_limit_bytes=56 << 20),
    )(lifted, rows_all, head_cols, local_ids[None], factors)


def head_backward_scattered(lifted, rows_all, head_cols, local_ids, factors, collective_id):
    tokens, width = lifted.shape
    features = rows_all.shape[1]
    hops, block = 3, tokens // 16
    rows, wing = block // 2, features // 2
    zorder = (3, 0, 2, 1)
    cuts = [slice(k, min(k + 512, width)) for k in range(0, width - 256, 512)]
    cuts[-1] = slice(cuts[-1].start, width)
    parts = (slice(0, rows), slice(rows, block))

    def kernel(p_hbm, rows_hbm, head_ref, ids_ref, factor_ref, out, d_head_ref, squares_ref,
               p_buf, r_buf, d_logits, total, acc, give, crecv, b_all, u_all, d_all, a_all, fin,
               in_sem, core_send, core_recv, send, recv, local):
        dp, seq, z, y, x, c = place()
        core = (dp, seq + 1 - 2 * c)
        xway = (dp, seq + 2 - 4 * x)
        yway = (dp + 1 - 2 * y, seq)
        up, down = (dp + 2, seq), (dp - 2, seq)
        has_up, has_down = z < hops, z > 0
        groups = ((1 - y, 1 - x), (y, 1 - x), (1 - y, x), (y, x))

        def fetch(slot, zz, yy, xx):
            return (
                pltpu.make_async_copy(p_hbm.at[zz, yy, xx], p_buf.at[slot], in_sem.at[slot, 0]),
                pltpu.make_async_copy(rows_hbm.at[zz, yy, xx], r_buf.at[slot], in_sem.at[slot, 1]),
            )

        for copy in fetch(0, zorder[0], *groups[0]):
            copy.start()
        greet([core, xway, yway], [(has_up, up), (has_down, down)])
        sems = Sems(send, recv, local)

        def remote(src, dst, device):
            ss, rs = sems.pair()
            return pltpu.make_async_remote_copy(src_ref=src, dst_ref=dst, send_sem=ss, recv_sem=rs,
                                                device_id=device, device_id_type=ON_MESH)

        def to_core(g, k, zz):
            yy, xx = groups[g]
            return pltpu.make_async_remote_copy(
                src_ref=give.at[k], dst_ref=crecv.at[zz, yy, xx], send_sem=core_send.at[g * 4 + k],
                recv_sem=core_recv.at[g * 4 + k], device_id=core, device_id_type=ON_MESH)

        total[...] = jnp.zeros_like(total)
        column = lax.broadcasted_iota(jnp.int32, (rows, width), 1)

        def zz_of(k):
            return jnp.where(k == 0, 3, jnp.where(k == 1, 0, jnp.where(k == 2, 2, 1)))

        def compute(g, k):
            yy, xx = groups[g]
            zz = zz_of(k)
            slot = lax.rem(k, 2)
            for copy in fetch(slot, zz, yy, xx):
                copy.wait()
            if g < 3:
                more = k < 4
            else:
                more = k < 3
            nyy, nxx = groups[min(g + 1, 3)]
            last = k == 3

            @pl.when(more)
            def _():
                for copy in fetch(1 - slot, jnp.where(last, 3, zz_of(k + 1)), jnp.where(last, nyy, yy), jnp.where(last, nxx, xx)):
                    copy.start()
            first = pl.multiple_of(((zz * 2 + yy) * 2 + xx) * block, block)
            here = pl.ds(first, block)
            ids = jnp.transpose(jnp.broadcast_to(ids_ref[:, here], (128, block)))[:, :1]
            scales = jnp.transpose(jnp.concatenate([factor_ref[:, here]] * 16, axis=0))
            if g > 0:
                to_core(g - 1, k, zz).wait_send()
            for part in parts:
                d_logits[part, :] = jnp.where(
                    column == ids[part], scales[part, 1:2], p_buf[slot, part, :].astype(jnp.float32) * scales[part, :1]
                ).astype(jnp.bfloat16)
                d_rows = lax.dot_general(
                    d_logits[part, :], head_ref[...], (((1,), (1,)), ((), ())), preferred_element_type=jnp.float32)
                left, right = d_rows[:, :wing], d_rows[:, wing:]
                acc[zz, yy, xx, part, :] = jnp.where(c == 0, left, right).astype(jnp.bfloat16)
                give[k, part, :] = jnp.where(c == 0, right, left).astype(jnp.bfloat16)
            to_core(g, k, zz).start()
            for cut in cuts:
                total[:, cut] += lax.dot_general(
                    r_buf[slot], d_logits[:, cut], (((0,), (0,)), ((), ())), preferred_element_type=jnp.float32)

        def add(dst, src):
            dst[...] = (dst[...].astype(jnp.float32) + src[...].astype(jnp.float32)).astype(dst.dtype)

        own_b = (x, y)
        own_a = (y, x)
        b_way, a_way = (xway, yway), (yway, xway)

        def spot(p, zz, a, b):
            yy, xx = (a, b) if p == 0 else (b, a)
            return acc.at[zz, yy, xx, parts[p]]

        b_msgs, z_up, z_down = {}, {}, {}
        for p in range(2):
            for zz in range(hops + 1):
                for near in range(2):
                    a = own_a[p] if near else 1 - own_a[p]
                    b_msgs[p, zz, near] = remote(spot(p, zz, a, 1 - own_b[p]), b_all.at[p, zz, a], b_way[p])
                    mine = spot(p, zz, a, own_b[p])
                    if zz > 0:
                        z_up[p, zz, near] = remote(mine, u_all.at[p, zz - 1, a], up)
                    if zz < hops:
                        z_down[p, zz, near] = remote(mine, d_all.at[p, zz, a], down)

        def core_add(g):
            yy, xx = groups[g]
            for k, zz in enumerate(zorder):
                to_core(g, k, zz).wait_recv()
                for part in parts:
                    add(acc.at[zz, yy, xx, part], crecv.at[zz, yy, xx, part])
                for p, near in (((0, 0), (1, 0)), ((0, 1),), ((1, 1),), ())[g]:
                    b_msgs[p, zz, near].start()

        def b_add(p, near):
            a = own_a[p] if near else 1 - own_a[p]
            for zz in zorder:
                b_msgs[p, zz, near].wait_recv()
                add(spot(p, zz, a, own_b[p]), b_all.at[p, zz, a])

        def z_take(p, zz, near, msgs, land):
            a = own_a[p] if near else 1 - own_a[p]
            msgs[p, zz, near].wait_recv()
            add(spot(p, zz, a, own_b[p]), land.at[p, zz - 1 if msgs is z_up else zz, a])

        def z_hop(p, near, hop):
            @pl.when(z == hop)
            def _():
                for zz in range(hops, hop, -1):
                    if hop > 0:
                        z_take(p, zz, near, z_up, u_all)
                    z_up[p, zz, near].start()

            @pl.when(z == hops - hop)
            def _():
                for zz in range(0, hops - hop):
                    if hop > 0:
                        z_take(p, zz, near, z_down, d_all)
                    z_down[p, zz, near].start()

        def run(g):
            def turn(k, _):
                compute(g, k)
                return 0
            lax.fori_loop(0, 4, turn, 0)

        run(0)
        core_add(0)
        run(1)
        core_add(1)
        b_add(1, 0)
        z_hop(1, 0, 0)
        run(2)
        core_add(2)
        b_add(0, 0)
        z_hop(0, 0, 0)
        z_hop(1, 0, 1)
        run(3)
        core_add(3)
        for p in range(2):
            b_add(p, 1)
            z_hop(p, 1, 0)
        z_hop(0, 0, 1)
        z_hop(1, 0, 2)
        for p in range(2):
            z_hop(p, 1, 1)
        z_hop(0, 0, 2)
        for p in range(2):
            z_hop(p, 1, 2)
        low = total[...].astype(jnp.bfloat16)
        d_head_ref[...] = low
        wide = low.astype(jnp.float32)
        squares_ref[...] = jnp.sum((wide * wide).reshape(features // 8, 8, width), axis=0)
        a_msgs = []
        for p in range(2):
            for zz in range(hops + 1):
                @pl.when(z == zz)
                def _():
                    for near in range(2):
                        if zz > 0:
                            z_take(p, zz, near, z_up, u_all)
                        if zz < hops:
                            z_take(p, zz, near, z_down, d_all)
            msg = remote(spot(p, z, 1 - own_a[p], own_b[p]), a_all.at[p], a_way[p])
            msg.start()
            a_msgs.append(msg)
        for p in range(2):
            a_msgs[p].wait_recv()
            fin[parts[p], :] = spot(p, z, own_a[p], own_b[p])[...].astype(jnp.float32) + a_all[p].astype(jnp.float32)
        side = pl.ds(pl.multiple_of(c * wing, 128), wing)
        other = remote(fin.at[pl.ds(pl.multiple_of((1 - c) * rows, 8), rows), :], out.at[:, side], core)
        keep = pltpu.make_async_copy(fin.at[pl.ds(pl.multiple_of(c * rows, 8), rows), :], out.at[:, side], sems.own())
        other.start()
        keep.start()
        for k in range(4):
            to_core(3, k, zorder[k]).wait_send()
        for msg in list(b_msgs.values()) + a_msgs:
            msg.wait_send()
        for zz in range(hops + 1):
            @pl.when(z < zz)
            def _():
                for p in range(2):
                    for near in range(2):
                        if zz > 0:
                            z_up[p, zz, near].wait_send()

            @pl.when(z > zz)
            def _():
                for p in range(2):
                    for near in range(2):
                        if zz < hops:
                            z_down[p, zz, near].wait_send()
        keep.wait()
        other.wait()

    bf = jnp.bfloat16
    n_send = 2 * 8 + 2 * 2 * 2 * hops + 2 + 1
    whole = pl.BlockSpec(memory_space=pltpu.VMEM)
    return pl.pallas_call(
        kernel,
        out_shape=[
            jax.ShapeDtypeStruct((rows, features), jnp.float32),
            jax.ShapeDtypeStruct((features, width), bf),
            jax.ShapeDtypeStruct((8, width), jnp.float32),
        ],
        in_specs=[pl.BlockSpec(memory_space=pl.ANY)] * 2 + [whole] * 3,
        out_specs=[pl.BlockSpec(memory_space=pl.ANY), whole, whole],
        scratch_shapes=[
            pltpu.VMEM((2, block, width), bf),
            pltpu.VMEM((2, block, features), bf),
            pltpu.VMEM((block, width), bf),
            pltpu.VMEM((features, width), jnp.float32),
            pltpu.VMEM((hops + 1, 2, 2, block, wing), bf),
            pltpu.VMEM((4, block, wing), bf),
            pltpu.VMEM((hops + 1, 2, 2, block, wing), bf),
            pltpu.VMEM((2, hops + 1, 2, rows, wing), bf),
            pltpu.VMEM((2, hops, 2, rows, wing), bf),
            pltpu.VMEM((2, hops, 2, rows, wing), bf),
            pltpu.VMEM((2, rows, wing), bf),
            pltpu.VMEM((block, wing), jnp.float32),
            pltpu.SemaphoreType.DMA((2, 2)),
            pltpu.SemaphoreType.DMA((16,)),
            pltpu.SemaphoreType.DMA((16,)),
            pltpu.SemaphoreType.DMA((n_send,)),
            pltpu.SemaphoreType.DMA((n_send,)),
            pltpu.SemaphoreType.DMA((1,)),
        ],
        compiler_params=pltpu.CompilerParams(collective_id=collective_id, has_side_effects=True, vmem_limit_bytes=60 << 20),
    )(
        lifted.reshape(hops + 1, 2, 2, block, width),
        rows_all.reshape(hops + 1, 2, 2, block, features),
        head_cols,
        local_ids[None],
        factors,
    )


def embed_gradient(columns, token_ids, vocab, block):
    features, tokens = columns.shape
    lanes = 128
    high_rows = -(-vocab // (8 * lanes)) * 8
    group = 2
    steps = tokens // block

    def kernel(columns_ref, ids_ref, out_ref, squares_ref):
        step = pl.program_id(0)
        ids = ids_ref[...]
        high = lax.broadcasted_iota(jnp.int32, (high_rows, block), 0) == lax.shift_right_logical(ids, 7)
        high = jnp.where(high, 1.0, 0.0).astype(jnp.bfloat16)
        low = lax.broadcasted_iota(jnp.int32, (lanes, block), 0) == jnp.bitwise_and(ids, lanes - 1)
        values = columns_ref[...].astype(jnp.float32)

        @pl.when(step == 0)
        def _():
            out_ref[...] = jnp.zeros_like(out_ref)

        for first in range(0, features, group):
            spread = jnp.concatenate(
                [jnp.where(low, values[f : f + 1], 0.0).astype(jnp.bfloat16) for f in range(first, first + group)], axis=0
            )
            term = lax.dot_general(high, spread, (((1,), (1,)), ((), ())), preferred_element_type=jnp.float32)
            for k in range(group):
                out_ref[first + k] += term[:, k * lanes : (k + 1) * lanes]

        @pl.when(step == steps - 1)
        def _():
            def turn(f, total):
                one = out_ref[f]
                return total + jnp.sum((one * one).reshape(high_rows // 8, 8, lanes), axis=0)
            squares_ref[...] = lax.fori_loop(0, features, turn, jnp.zeros((8, lanes), jnp.float32))

    sums, squares = pl.pallas_call(
        kernel,
        grid=(steps,),
        out_shape=[
            jax.ShapeDtypeStruct((features, high_rows, lanes), jnp.float32),
            jax.ShapeDtypeStruct((8, lanes), jnp.float32),
        ],
        in_specs=[pl.BlockSpec((features, block), lambda i: (0, i)), pl.BlockSpec((1, block), lambda i: (0, i))],
        out_specs=[
            pl.BlockSpec((features, high_rows, lanes), lambda i: (0, 0, 0)),
            pl.BlockSpec((8, lanes), lambda i: (0, 0)),
        ],
        compiler_params=pltpu.CompilerParams(vmem_limit_bytes=50 << 20),
    )(columns, token_ids[None])
    return sums[:, : vocab // lanes].reshape(features, vocab), squares


BOTH = ("dp", "seq")
mark_height = 8


def mark_rows(targets, loss_mask):
    own = targets.shape[0] // lax.axis_size("seq")
    first = lax.axis_index("seq") * own
    own_targets = lax.dynamic_slice_in_dim(targets, first, own)
    own_mask = lax.dynamic_slice_in_dim(loss_mask, first, own)
    rows = jnp.stack([own_targets // 256, own_targets % 256, own_mask]).astype(jnp.float32)
    return jnp.pad(rows, ((0, mark_height - 3), (0, 0)))[None]


def marks_of(gathered):
    rows = gathered[0].reshape(-1, mark_height, gathered.shape[2]).astype(jnp.float32)
    numbers = rows[:, :3].transpose(1, 0, 2).reshape(3, -1).astype(jnp.int32)
    return (numbers[0] * 256 + numbers[1], numbers[2])


def on_box():
    return lax.axis_size("dp") == 8 and lax.axis_size("seq") == 4


def gather_rows(tensors, portions, collective_id):
    if on_box():
        return gather_blocks(tensors, portions, collective_id)
    return gather_plain(tensors)


def gather_plain(tensors):
    return [lax.all_gather(t.astype(jnp.bfloat16), BOTH, axis=1, tiled=True) for t in tensors]


def scatter_rows(tensors, portions, collective_id):
    if on_box():
        devices = lax.axis_size("dp") * lax.axis_size("seq")
        rows = [t.shape[1] // devices for t in tensors]
        return scatter_blocks(tensors, portions, rows, collective_id)
    return scatter_plain(tensors)


def scatter_plain(tensors):
    return [
        lax.psum_scatter(t, BOTH, scatter_dimension=1, tiled=True).astype(jnp.float32) for t in tensors
    ]


def gradient_portions(square, expand, shrink):
    return [
        [(1, 0, 1, 0, 2 * expand), (0, 0, 1, 0, 2 * square)],
        [(2, 0, 1, 0, 2 * shrink), (4, 0, 1, 0, 2 * square)],
        [(0, 1, 5, 0, 2 * square)],
        [(4, 1, 5, 0, 2 * square), (3, 0, 1, 0, 2 * square)],
    ]


def weight_portions(square, expand, shrink, vectors, marks=0):
    split = 2 * square * 2 // 3
    first = [(1, 0, 1, 0, 2 * expand)]
    second = [(2, 0, 1, 0, 2 * shrink)]
    third = [(0, 0, 2, 0, 2 * square), (0, 2, 3, 0, split)]
    fourth = [(0, 3, 5, 0, 2 * square), (0, 2, 3, split, 2 * square)]
    if vectors:
        fourth.append((3, 0, 1, 0, 2 * vectors))
    if marks:
        fourth.append((4, 0, 1, 0, 2 * marks))
    return [first, second, third, fourth]


def row_portions(rows):
    ends = [0, rows * 5 // 8, rows * 10 // 8, rows * 13 // 8, 2 * rows]
    return [[(0, 0, 1, first, last)] for first, last in zip(ends, ends[1:])]


def as_rows(vectors):
    lanes = -(-vectors.shape[0] // 256) * 256
    return jnp.pad(vectors.T, ((0, 0), (0, lanes - vectors.shape[0])))[None]

EXACT_MATMUL = lax.Precision.HIGHEST
BETA_ONE = 0.9
BETA_TWO = 0.999
ADAM_EPS = 1e-08
WEIGHT_DECAY = 0.01
LEARN_RATES = (0.03, 0.03, 0.015, 0.5, 2.0, 0.05)
DECAY_FLAGS = (True, True, True, False, True, True)
param_stride = 11
head_tile = 1024
embed_block = 1024
far_below = -1e30
scan_block = 256


def from_behind(value, axis, steps):
    count = lax.axis_size(axis)
    leading, last = (max(0, -steps), min(count, count - steps))
    return lax.ppermute(value, axis, [(source, source + steps) for source in range(leading, last)])


def carried_in(value, axis, join, neutral, backward):
    count, mine = (lax.axis_size(axis), lax.axis_index(axis))
    pieces = lax.all_gather(jnp.stack(value), axis)
    if backward:
        pieces = pieces[::-1]
        mine = count - 1 - mine
    running = neutral
    for position in range(count - 1):
        longer = join(running, tuple(pieces[position]))
        running = tuple(
            jnp.where(position < mine, new, old) for new, old in zip(longer, running)
        )
    return running


def layer_norm(values, gain, bias):
    centre = values - jnp.mean(values, axis=-1, keepdims=True)
    spread = jnp.mean(centre * centre, axis=-1, keepdims=True)
    return centre * lax.rsqrt(spread + 1e-05) * gain + bias


def matmul(left, right):
    return jnp.dot(left, right, preferred_element_type=jnp.float32)


def matmul_tn(left, right):
    return lax.dot_general(
        left, right, (((0,), (0,)), ((), ())), preferred_element_type=jnp.float32
    )


def matmul_nt(left, right):
    return lax.dot_general(
        left, right, (((1,), (1,)), ((), ())), preferred_element_type=jnp.float32
    )


def blend_all(normed, incoming, shares):
    earlier = jnp.concatenate([incoming, normed[:-1]], axis=0)
    return tuple(
        (
            normed * shares[member] + earlier * (1.0 - shares[member])
            for member in range(shares.shape[0])
        )
    )


def take_previous(normed):
    return from_behind(normed[-1:], "seq", 1)


def give_back(grad_first):
    return from_behind(grad_first, "seq", -1)


def block_ends(arriving_lookups, arriving_contents, logarithmic_fading_speed):
    decay_rate = jnp.exp(logarithmic_fading_speed)
    length = arriving_lookups.shape[0]
    ages = (length - 1.0 - jnp.arange(length, dtype=jnp.float32))[:, None]
    weight = jnp.exp(arriving_lookups - decay_rate * ages)
    return (jnp.sum(weight * arriving_contents, axis=0), jnp.sum(weight, axis=0))


def block_factor(logarithmic_fading_speed, length):
    return jnp.exp(-jnp.exp(logarithmic_fading_speed) * length)


def chain_combine(earlier, later):
    return (
        earlier[0] * later[2] + later[0],
        earlier[1] * later[2] + later[1],
        earlier[2] * later[2],
    )


def token_mixer_block(
    arriving_lookups,
    arriving_contents,
    logarithmic_fading_speed,
    present_reward,
    initial_numerator,
    initial_denominator,
):
    decay_rate = jnp.exp(logarithmic_fading_speed)
    length, channels = arriving_lookups.shape
    block_size = min(scan_block, length)
    block_count = length // block_size
    offsets = jnp.arange(block_size, dtype=jnp.float32)[:, None]
    lower_mask = (offsets > offsets.T).astype(jnp.float32)
    diagonal_amplifier = jnp.exp(present_reward)
    back_decay = jnp.exp(-decay_rate * (offsets - 1.0))
    carry_decay = jnp.exp(-decay_rate * offsets)
    tail_decay = jnp.exp(-decay_rate * (block_size - 1.0))
    full_decay = jnp.exp(-decay_rate * block_size)

    def sub_block(state, step_item):
        numerator, denominator = state
        key_block, value_block = step_item
        lifted = jnp.exp(key_block + decay_rate * offsets)
        prefix_sums = jnp.dot(
            lower_mask,
            jnp.concatenate([lifted * value_block, lifted], axis=1),
            precision=EXACT_MATMUL,
        )
        own_term = diagonal_amplifier * jnp.exp(key_block)
        top_part = (
            back_decay * prefix_sums[:, :channels]
            + carry_decay * numerator
            + own_term * value_block
        )
        low_part = back_decay * prefix_sums[:, channels:] + carry_decay * denominator + own_term
        next_num = tail_decay * jnp.sum(lifted * value_block, axis=0) + full_decay * numerator
        next_den = tail_decay * jnp.sum(lifted, axis=0) + full_decay * denominator
        return ((next_num, next_den), (top_part / low_part, low_part))

    shaped = (
        arriving_lookups.reshape(block_count, block_size, channels),
        arriving_contents.reshape(block_count, block_size, channels),
    )
    (end_num, end_den), (block_outs, denoms) = lax.scan(
        sub_block, (initial_numerator, initial_denominator), shaped
    )
    return (
        (block_outs.reshape(length, channels), end_num, end_den),
        denoms.reshape(length, channels),
    )


def layer_forward(stream, gathered):
    square, expand, shrink, params = gathered
    normed = layer_norm(stream, params[0], params[1])
    incoming_one = take_previous(normed)
    blended = blend_all(normed, incoming_one, params[2:5])
    mixed_key = blended[0].astype(jnp.bfloat16)
    mixed_value = blended[1].astype(jnp.bfloat16)
    mixed_gate = blended[2].astype(jnp.bfloat16)
    arriving_lookups = matmul(mixed_key, square[0])
    arriving_contents = matmul(mixed_value, square[1])
    gates_in = matmul(mixed_gate, square[2])
    length = arriving_lookups.shape[0]
    end_sums = block_ends(arriving_lookups, arriving_contents, params[5])
    zero_state = jnp.zeros_like(end_sums[0])
    one_state = jnp.ones_like(end_sums[0])
    factor = block_factor(params[5], length)
    initial_numerator, initial_denominator, spare_factor = carried_in(
        (end_sums[0], end_sums[1], factor),
        "seq",
        chain_combine,
        (zero_state, zero_state, one_state),
        False,
    )
    (mixed_out, spare_placeholder, spare_placeholder), spare_placeholder = token_mixer_block(
        arriving_lookups,
        arriving_contents,
        params[5],
        params[6],
        initial_numerator,
        initial_denominator,
    )
    gated = (jax.nn.sigmoid(gates_in) * mixed_out).astype(jnp.bfloat16)
    middle = stream + matmul(gated, square[3])
    normed_two = layer_norm(middle, params[7], params[8])
    incoming_two = take_previous(normed_two)
    blended_two = blend_all(normed_two, incoming_two, params[9:11])
    chan_key = blended_two[0].astype(jnp.bfloat16)
    chan_gate = blended_two[1].astype(jnp.bfloat16)
    pre_act = matmul(chan_key, expand)
    activated = jnp.square(jnp.maximum(pre_act, 0.0)).astype(jnp.bfloat16)
    chan_value = matmul(activated, shrink)
    gate_pre = matmul(chan_gate, square[4])
    result = middle + jax.nn.sigmoid(gate_pre) * chan_value
    saved = (
        stream,
        incoming_one,
        mixed_key,
        mixed_value,
        mixed_gate,
        arriving_lookups,
        arriving_contents,
        gates_in,
        initial_numerator,
        initial_denominator,
        gated,
        middle,
        incoming_two,
        chan_key,
        chan_gate,
        pre_act,
        activated,
        chan_value,
        gate_pre,
    )
    return (result, saved)


def norm_back(stream, incoming, params, first_row, share_rows, grads):
    normed, norm_pull = jax.vjp(layer_norm, stream, params[first_row], params[first_row + 1])
    shares = params[share_rows[0] : share_rows[1]]
    spare_placeholder, blend_pull = jax.vjp(blend_all, normed, incoming, shares)
    d_normed, d_incoming, d_shares = blend_pull(grads)
    from_next = give_back(d_incoming)
    d_normed = d_normed.at[-1].add(from_next[0])
    d_stream, d_gain, d_bias = norm_pull(d_normed)
    return (d_stream, jnp.stack([d_gain, d_bias]), d_shares)


def layer_backward(gradient, saved, gathered):
    square, expand, shrink, params = gathered
    (
        stream,
        incoming_one,
        mixed_key,
        mixed_value,
        mixed_gate,
        arriving_lookups,
        arriving_contents,
        gates_in,
        initial_numerator,
        initial_denominator,
        gated,
        middle,
        incoming_two,
        chan_key,
        chan_gate,
        pre_act,
        activated,
        chan_value,
        gate_pre,
    ) = saved
    gate_sig = jax.nn.sigmoid(gate_pre)
    d_value = (gradient * gate_sig).astype(jnp.bfloat16)
    d_gate_pre = (gradient * chan_value * gate_sig * (1.0 - gate_sig)).astype(jnp.bfloat16)
    g_shrink = matmul_tn(activated, d_value)
    d_active = matmul_nt(d_value, shrink)
    d_pre = (d_active * 2.0 * jnp.maximum(pre_act, 0.0)).astype(jnp.bfloat16)
    g_expand = matmul_tn(chan_key, d_pre)
    g_chan_gate = matmul_tn(chan_gate, d_gate_pre)
    d_chan_key = matmul_nt(d_pre, expand)
    d_chan_gate = matmul_nt(d_gate_pre, square[4])
    d_middle, second_norm_gradient, second_share_gradient = norm_back(
        middle, incoming_two, params, 7, (9, 11), (d_chan_key, d_chan_gate)
    )
    d_middle = d_middle + gradient
    d_output = d_middle.astype(jnp.bfloat16)
    g_output = matmul_tn(gated, d_output)
    d_gated = matmul_nt(d_output, square[3])
    (mixed_out, spare_placeholder, spare_placeholder), token_mixer_backward, denoms = jax.vjp(
        token_mixer_block,
        arriving_lookups,
        arriving_contents,
        params[5],
        params[6],
        initial_numerator,
        initial_denominator,
        has_aux=True,
    )
    gate_sig_one = jax.nn.sigmoid(gates_in)
    mixed_gradient = d_gated * gate_sig_one
    d_gates_in = (d_gated * mixed_out * gate_sig_one * (1.0 - gate_sig_one)).astype(jnp.bfloat16)
    length = arriving_lookups.shape[0]
    decay_rate = jnp.exp(params[5])
    carried = (
        jnp.exp(-decay_rate * jnp.arange(length, dtype=jnp.float32)[:, None])
        * mixed_gradient
        / denoms
    )
    zero_state = jnp.zeros_like(decay_rate)
    one_state = jnp.ones_like(decay_rate)
    factor = block_factor(params[5], length)
    following_numerator, following_denominator, spare_factor = carried_in(
        (jnp.sum(carried, axis=0), -jnp.sum(carried * mixed_out, axis=0), factor),
        "seq",
        chain_combine,
        (zero_state, zero_state, one_state),
        True,
    )
    (
        lookup_sensitivity,
        content_sensitivity,
        fading_sensitivity,
        reward_sensitivity,
        spare_placeholder,
        spare_placeholder,
    ) = token_mixer_backward((mixed_gradient, following_numerator, following_denominator))
    lookup_sensitivity = lookup_sensitivity.astype(jnp.bfloat16)
    content_sensitivity = content_sensitivity.astype(jnp.bfloat16)
    g_key = matmul_tn(mixed_key, lookup_sensitivity)
    g_value = matmul_tn(mixed_value, content_sensitivity)
    g_gate = matmul_tn(mixed_gate, d_gates_in)
    d_mixed_key = matmul_nt(lookup_sensitivity, square[0])
    d_mixed_value = matmul_nt(content_sensitivity, square[1])
    d_mixed_gate = matmul_nt(d_gates_in, square[2])
    d_stream, first_norm_gradient, first_share_gradient = norm_back(
        stream, incoming_one, params, 0, (2, 5), (d_mixed_key, d_mixed_value, d_mixed_gate)
    )
    d_stream = d_stream + d_middle
    g_square = jnp.stack([g_key, g_value, g_gate, g_output, g_chan_gate])
    g_params = jnp.concatenate(
        [
            first_norm_gradient,
            first_share_gradient,
            fading_sensitivity[None],
            reward_sensitivity[None],
            second_norm_gradient,
            second_share_gradient,
        ],
        axis=0,
    )
    return (d_stream, (g_square, g_expand, g_shrink, g_params))


def adam_update(weights, gradient, first, second, step_rate, decay_on):
    first_new = BETA_ONE * first + (1.0 - BETA_ONE) * gradient
    second_new = BETA_TWO * second + (1.0 - BETA_TWO) * gradient * gradient
    first_hat = first_new / (1.0 - BETA_ONE**STEP)
    second_hat = second_new / (1.0 - BETA_TWO**STEP)
    moved = first_hat / (jnp.sqrt(second_hat) + ADAM_EPS)
    if decay_on:
        moved = moved + WEIGHT_DECAY * weights
    return (weights - step_rate * moved, first_new, second_new)


def adam_columns(weights, pieces, first, second, scale, slot):
    rows, columns = weights.shape
    width = pieces.shape[2]

    def kernel(w_ref, g_ref, first_ref, second_ref, scale_ref, w_out, first_out, second_out):
        gradient = g_ref[0].astype(jnp.float32) * scale_ref[0]
        w_out[...], first_out[...], second_out[...] = adam_update(
            w_ref[...], gradient, first_ref[...], second_ref[...], LEARN_RATES[slot], DECAY_FLAGS[slot]
        )

    block = pl.BlockSpec((rows, width), lambda i: (0, i))
    return pl.pallas_call(
        kernel,
        grid=(-(-columns // width),),
        out_shape=[jax.ShapeDtypeStruct(weights.shape, jnp.float32)] * 3,
        in_specs=[
            block,
            pl.BlockSpec((1, rows, width), lambda i: (i, 0, 0)),
            block,
            block,
            pl.BlockSpec(memory_space=pltpu.SMEM),
        ],
        out_specs=[block] * 3,
        compiler_params=pltpu.CompilerParams(vmem_limit_bytes=40 << 20),
    )(weights, pieces, first, second, scale[None])


def per_device(
    token_ids,
    targets,
    loss_mask,
    square_weights,
    expand_weights,
    shrink_weights,
    vector_params,
    embed_table,
    head_table,
    square_first,
    expand_first,
    shrink_first,
    vector_first,
    embed_first,
    head_first,
    square_second,
    expand_second,
    shrink_second,
    vector_second,
    embed_second,
    head_second,
):
    layers = square_weights.shape[0]
    global_rows = param_stride * layers
    total_tokens = token_ids.shape[0]

    vector_rows = vector_params.shape[0]
    square_own, expand_own, shrink_own = (
        square_weights.shape[2],
        expand_weights.shape[1],
        shrink_weights.shape[1],
    )

    def fetch_layer(layer_id):
        with_vectors = layer_id == 0
        shards = [
            square_weights[layer_id],
            expand_weights[layer_id][None],
            shrink_weights[layer_id][None],
        ]
        if with_vectors:
            shards.append(as_rows(vector_params))
            shards.append(mark_rows(targets, loss_mask))
        else:
            return gather_plain(shards)
        return gather_rows(
            shards,
            weight_portions(
                square_own,
                expand_own,
                shrink_own,
                with_vectors * square_own,
                with_vectors * mark_height,
            ),
            layer_id,
        )

    fetched = [fetch_layer(layer_id) for layer_id in range(layers)]
    vectors_all = fetched[0][3][0, :, :vector_rows].T.astype(jnp.float32)
    global_params = vectors_all[global_rows:]
    blocks = [
        (
            fetched[layer_id][0],
            fetched[layer_id][1][0],
            fetched[layer_id][2][0],
            vectors_all[layer_id * param_stride : (layer_id + 1) * param_stride],
        )
        for layer_id in range(layers)
    ]

    columns = jnp.take(embed_table.astype(jnp.bfloat16), token_ids, axis=1)
    embedded = lax.all_to_all(
        columns, ("dp", "seq"), split_axis=1, concat_axis=0, tiled=True
    ).T.astype(jnp.float32)
    stream, norm_pull_zero = jax.vjp(layer_norm, embedded, global_params[0], global_params[1])
    saved_layers = []
    for layer_id in range(layers):
        stream, saved = layer_forward(stream, blocks[layer_id])
        saved_layers.append(saved)
    normed, norm_pull_last = jax.vjp(layer_norm, stream, global_params[2], global_params[3])
    dp_count = lax.axis_size("dp")
    features, vocab_own = head_table.shape
    vocab_part = -(-vocab_own // (dp_count * 128)) * 128
    head_cut = jnp.pad(
        head_table.astype(jnp.bfloat16), ((0, 0), (0, dp_count * vocab_part - vocab_own))
    ).reshape(features, dp_count, vocab_part)
    head_cols = lax.all_to_all(
        head_cut.transpose(1, 0, 2), "dp", split_axis=0, concat_axis=0, tiled=True
    ).reshape(dp_count * features, vocab_part)
    valid = jnp.clip(vocab_own - lax.axis_index("dp") * vocab_part, 0, vocab_part)
    masked = jnp.where(jnp.arange(vocab_part) < valid, 0.0, far_below)[None]
    own_rows = normed.shape[0]
    rows_all = gather_rows([normed[None]], row_portions(own_rows), 10)[0][0]
    all_targets, all_mask = marks_of(fetched[0][4])
    first_column = lax.axis_index("seq") * vocab_own + lax.axis_index("dp") * vocab_part
    local_ids = all_targets - first_column
    local_ids = jnp.where(local_ids < valid, local_ids, -1)
    tile = min(head_tile, total_tokens)
    lifted, stats = head_forward(rows_all, head_cols, masked, local_ids, tile, tile // 4)
    own_log = stats[0] + jnp.log(stats[1])
    log_total = exchange_everywhere(own_log.reshape(-1, 128), add_logs, 13).reshape(-1)
    counted = all_mask.astype(jnp.float32)
    picked_part = jnp.sum(counted * stats[2])
    weight_rows = counted / total_tokens
    factors = jnp.pad(
        jnp.stack(
            [
                jnp.exp(stats[0] - log_total) * weight_rows,
                (jnp.exp(stats[2] - log_total) - 1.0) * weight_rows,
            ]
        ),
        ((0, 6), (0, 0)),
    )
    if on_box():
        d_normed, grad_head, head_squares = head_backward_scattered(
            lifted, rows_all, head_cols, local_ids, factors, 11
        )
    else:
        d_rows, grad_head, head_squares = head_backward(
            lifted, rows_all, head_cols, local_ids, factors, tile, tile // 2
        )
        d_normed = scatter_plain([d_rows[None]])[0][0]
    g_head = lax.all_to_all(
        grad_head.reshape(dp_count, features, vocab_part), "dp", split_axis=0, concat_axis=0, tiled=True
    )
    d_stream, d_gain_last, d_bias_last = norm_pull_last(d_normed)
    layer_grads = [None] * layers
    vector_grads = [None] * layers
    later_squares = []
    d_embedded = d_stream
    for layer_id in reversed(range(layers)):
        d_stream, grads = layer_backward(d_stream, saved_layers[layer_id], blocks[layer_id])
        vector_grads[layer_id] = grads[3]
        low_grads = [
            grads[0].astype(jnp.bfloat16),
            grads[1].astype(jnp.bfloat16)[None],
            grads[2].astype(jnp.bfloat16)[None],
        ]
        if layer_id == 0:
            d_embedded, d_gain_zero, d_bias_zero = norm_pull_zero(d_stream)
            all_vectors = jnp.concatenate(
                vector_grads
                + [jnp.stack([d_gain_zero, d_bias_zero, d_gain_last, d_bias_last])],
                axis=0,
            )
            low_grads.append(as_rows(all_vectors).astype(jnp.bfloat16))
        if layer_id > 0:
            layer_grads[layer_id] = [None] + scatter_plain(low_grads[1:])
            later_squares.append(low_grads[0])
    summed = scatter_rows(
        low_grads + later_squares,
        gradient_portions(square_own, expand_own, shrink_own),
        layers,
    )
    layer_grads[0] = summed[:4]
    for layer_id, square_sum in zip(reversed(range(1, layers)), summed[4:]):
        layer_grads[layer_id][0] = square_sum
    back_columns = lax.all_to_all(
        d_embedded.T.astype(jnp.bfloat16), ("dp", "seq"), split_axis=0, concat_axis=1, tiled=True
    )
    g_embed, embed_squares = embed_gradient(
        back_columns, token_ids, embed_table.shape[1], min(embed_block, total_tokens)
    )
    g_square = jnp.stack([layer_grads[layer_id][0] for layer_id in range(layers)])
    g_expand = jnp.concatenate([layer_grads[layer_id][1] for layer_id in range(layers)])
    g_shrink = jnp.concatenate([layer_grads[layer_id][2] for layer_id in range(layers)])
    g_vector = layer_grads[0][3][0, :, :vector_rows].T
    gradients = (g_square, g_expand, g_shrink, g_vector, g_embed, g_head)
    square_part = jnp.sum(embed_squares) + jnp.sum(head_squares)
    for gradient in gradients[:4]:
        square_part = square_part + jnp.sum(gradient * gradient)
    parts = jnp.stack([square_part, picked_part])
    parts = exchange_everywhere(jnp.broadcast_to(jnp.pad(parts, (0, 6))[:, None], (8, 128)), jnp.add, 12)
    square_sum = parts[0, 0]
    loss_sum = jnp.sum(counted * log_total) - parts[1, 0]
    grad_norm = jnp.sqrt(square_sum)
    scale = jnp.minimum(1.0, 0.5 / math.sqrt(total_tokens) / (grad_norm + 1e-06))
    weights = (
        square_weights,
        expand_weights,
        shrink_weights,
        vector_params,
        embed_table,
        head_table,
    )
    firsts = (square_first, expand_first, shrink_first, vector_first, embed_first, head_first)
    seconds = (
        square_second,
        expand_second,
        shrink_second,
        vector_second,
        embed_second,
        head_second,
    )
    updated = [
        adam_update(
            weights[slot],
            gradients[slot] * scale,
            firsts[slot],
            seconds[slot],
            LEARN_RATES[slot],
            DECAY_FLAGS[slot],
        )
        for slot in range(5)
    ]
    updated.append(adam_columns(head_table, g_head, head_first, head_second, scale, 5))
    return (
        loss_sum,
        grad_norm,
        updated[0][0],
        updated[1][0],
        updated[2][0],
        updated[3][0],
        updated[4][0],
        updated[5][0],
        updated[0][1],
        updated[1][1],
        updated[2][1],
        updated[3][1],
        updated[4][1],
        updated[5][1],
        updated[0][2],
        updated[1][2],
        updated[2][2],
        updated[3][2],
        updated[4][2],
        updated[5][2],
    )


def solution(mesh):
    placed = (
        P(),
        P("dp"),
        P("dp"),
        P(None, None, ("dp", "seq"), None),
        P(None, ("dp", "seq"), None),
        P(None, ("dp", "seq"), None),
        P(None, ("dp", "seq")),
        P(("dp", "seq"), None),
        P("dp", "seq"),
        P(None, None, ("dp", "seq"), None),
        P(None, ("dp", "seq"), None),
        P(None, ("dp", "seq"), None),
        P(None, ("dp", "seq")),
        P(("dp", "seq"), None),
        P("dp", "seq"),
        P(None, None, ("dp", "seq"), None),
        P(None, ("dp", "seq"), None),
        P(None, ("dp", "seq"), None),
        P(None, ("dp", "seq")),
        P(("dp", "seq"), None),
        P("dp", "seq"),
    )
    return jax.shard_map(
        per_device,
        mesh=mesh,
        in_specs=placed,
        out_specs=(
            P(),
            P(),
            P(None, None, ("dp", "seq"), None),
            P(None, ("dp", "seq"), None),
            P(None, ("dp", "seq"), None),
            P(None, ("dp", "seq")),
            P(("dp", "seq"), None),
            P("dp", "seq"),
            P(None, None, ("dp", "seq"), None),
            P(None, ("dp", "seq"), None),
            P(None, ("dp", "seq"), None),
            P(None, ("dp", "seq")),
            P(("dp", "seq"), None),
            P("dp", "seq"),
            P(None, None, ("dp", "seq"), None),
            P(None, ("dp", "seq"), None),
            P(None, ("dp", "seq"), None),
            P(None, ("dp", "seq")),
            P(("dp", "seq"), None),
            P("dp", "seq"),
        ),
        check_vma=False,
    )
```

```python
import functools
import math

import jax
import jax.numpy as jnp
from jax import lax
from jax.experimental import pallas as pl
from jax.experimental.pallas import tpu as pltpu
from jax.sharding import PartitionSpec as P

STEP = 10
ON_MESH = pl.DeviceIdType.MESH


def place():
    dp, seq = lax.axis_index("dp"), lax.axis_index("seq")
    return dp, seq, dp // 2, lax.rem(dp, 2), seq // 2, lax.rem(seq, 2)


def greet(partners, extra):
    barrier = pltpu.get_barrier_semaphore()
    for partner in partners:
        pl.semaphore_signal(barrier, inc=1, device_id=partner, device_id_type=ON_MESH)
    for exists, partner in extra:
        @pl.when(exists)
        def _():
            pl.semaphore_signal(barrier, inc=1, device_id=partner, device_id_type=ON_MESH)
    peers = len(partners)
    for exists, partner in extra:
        peers = peers + exists.astype(jnp.int32)
    pl.semaphore_wait(barrier, peers)


class Sems:
    def __init__(self, send, recv, local):
        self.send, self.recv, self.local = send, recv, local
        self.ns = self.nr = self.nl = 0

    def pair(self):
        self.ns += 1
        return self.send.at[self.ns - 1], self.recv.at[self.ns - 1]

    def own(self):
        self.nl += 1
        return self.local.at[self.nl - 1]


def gather_blocks(tensors, portions, collective_id):
    count = len(tensors)
    dims = [t.shape for t in tensors]
    hops = 3
    pieces_total = sum(len(p) for p in portions)
    n_send = count + count + pieces_total * (7 + 2 * hops + 7)

    def kernel(*refs):
        ins, outs = refs[:count], refs[count : 2 * count]
        wide = refs[2 * count : 3 * count]
        half = refs[3 * count : 4 * count]
        send, recv, local = refs[4 * count :]
        dp, seq, z, y, x, c = place()
        core = (dp, seq + 1 - 2 * c)
        xway = (dp, seq + 2 - 4 * x)
        yway = (dp + 1 - 2 * y, seq)
        up, down = (dp + 2, seq), (dp - 2, seq)
        has_up, has_down = z < hops, z > 0
        greet([core, xway, yway], [(has_up, up), (has_down, down)])
        sems = Sems(send, recv, local)

        def cols(t, side):
            width = dims[t][2] // 2
            return pl.ds(pl.multiple_of(side * width, 128), width)

        first = []
        for t in range(count):
            rows = pl.ds(pl.multiple_of(c * dims[t][1], 8), dims[t][1])
            mine = pltpu.make_async_copy(ins[t].at[:, :, cols(t, c)], wide[t].at[:, rows, :], sems.own())
            ss, rs = sems.pair()
            other = pltpu.make_async_remote_copy(
                src_ref=ins[t].at[:, :, cols(t, 1 - c)], dst_ref=wide[t].at[:, rows, :],
                send_sem=ss, recv_sem=rs, device_id=core, device_id_type=ON_MESH)
            other.start()
            mine.start()
            first.append((mine, other))
        core_sems = [sems.pair() for t in range(count)]
        stay = []
        for t in range(count):
            first[t][0].wait()
            first[t][1].wait()
            half[t][...] = wide[t][...].astype(jnp.bfloat16)
            own = pltpu.make_async_copy(half[t], outs[t].at[:, z, y, x, :, cols(t, c)], sems.own())
            own.start()
            stay.append(own)

        def block(piece, zz, yy, xx):
            t, m0, m1, r0, r1 = piece
            return outs[t].at[m0:m1, zz, yy, xx, r0:r1, cols(t, c)]

        def to_core(p, zz, yy, xx, source=None):
            for piece in portions[p]:
                t = piece[0]
                region = block(piece, zz, yy, xx)
                pltpu.make_async_remote_copy(
                    src_ref=region if source is None else source(piece), dst_ref=region,
                    send_sem=core_sems[t][0], recv_sem=core_sems[t][1], device_id=core, device_id_type=ON_MESH).start()

        def message(p, where, device, source=None):
            copies = []
            for piece in portions[p]:
                ss, rs = sems.pair()
                region = block(piece, *where)
                copies.append(pltpu.make_async_remote_copy(
                    src_ref=region if source is None else source(piece), dst_ref=region,
                    send_sem=ss, recv_sem=rs, device_id=device, device_id_type=ON_MESH))
            return copies

        def start(copies):
            for copy in copies:
                copy.start()

        def arrive(copies):
            for copy in copies:
                copy.wait_recv()

        def sent(copies):
            for copy in copies:
                copy.wait_send()

        def from_half(piece):
            t, m0, m1, r0, r1 = piece
            return half[t].at[m0:m1, r0:r1, :]

        both = slice(0, 2)
        a_way, b_way = (yway, xway) * 2, (xway, yway) * 2
        ways = range(len(portions))

        def one_of(p, zz):
            return (zz, y, x)

        def pair_of(p, zz):
            return (zz, both, x) if p % 2 == 0 else (zz, y, both)

        def other_of(p, zz):
            return (zz, 1 - y, x) if p % 2 == 0 else (zz, y, 1 - x)

        def far_of(p, zz):
            return (zz, both, 1 - x) if p % 2 == 0 else (zz, 1 - y, both)

        def late(p):
            return p >= 2

        def event_z(e):
            return z if e == 0 else z - e if e <= hops else z + e - hops

        def happens(e):
            return z - e >= 0 if e <= hops else z + e - hops <= hops

        def when(e, what):
            if e == 0:
                what()
            else:
                pl.when(happens(e))(what)

        events = range(1 + 2 * hops)
        a_msgs, z_msgs, b_msgs = {}, {}, {}
        for p in ways:
            held = one_of if late(p) else pair_of
            for e in events if late(p) else (0,):
                a_msgs[p, e] = message(p, one_of(p, event_z(e)), a_way[p], from_half if e == 0 else None)
            for k in range(hops):
                source = from_half if late(p) and k == 0 else None
                z_msgs[p, 1 + k] = message(p, held(p, z - k), up, source)
                z_msgs[p, 1 + hops + k] = message(p, held(p, z + k), down, source)
            for e in events:
                b_msgs[p, e] = message(p, pair_of(p, event_z(e)), b_way[p])

        def start_z(p, e):
            @pl.when(has_up if e <= hops else has_down)
            def _():
                start(z_msgs[p, e])

        for p in ways:
            if late(p):
                start_z(p, 1)
                start_z(p, 1 + hops)
            start(a_msgs[p, 0])
        for own in stay:
            own.wait()
        for p in ways:
            to_core(p, z, y, x, from_half)
        for p in ways:
            if not late(p):
                arrive(a_msgs[p, 0])
                start_z(p, 1)
                start_z(p, 1 + hops)
                start(b_msgs[p, 0])
                to_core(p, *other_of(p, z))

        def z_event(p, e):
            def turn():
                arrive(z_msgs[p, e])
                if e % hops:
                    start_z(p, e + 1)
                if late(p):
                    start(a_msgs[p, e])
                    to_core(p, *one_of(p, event_z(e)))
                else:
                    start(b_msgs[p, e])
                    to_core(p, *pair_of(p, event_z(e)))
            when(e, turn)

        def a_event(p, e):
            def turn():
                arrive(a_msgs[p, e])
                start(b_msgs[p, e])
                to_core(p, *other_of(p, event_z(e)))
            when(e, turn)

        def b_event(p, e):
            def turn():
                arrive(b_msgs[p, e])
                to_core(p, *far_of(p, event_z(e)))
            when(e, turn)

        def at(hop):
            return (0,) if hop == 0 else (hop, hops + hop)

        for hop in range(hops + 3):
            if 1 <= hop <= hops:
                for p in ways:
                    for e in at(hop):
                        z_event(p, e)
            if hop - 1 in range(hops + 1):
                for p in ways:
                    for e in at(hop - 1):
                        if late(p):
                            a_event(p, e)
                        else:
                            b_event(p, e)
            if hop - 2 in range(hops + 1):
                for p in ways:
                    for e in at(hop - 2):
                        if late(p):
                            b_event(p, e)

        for (p, e), msg in list(a_msgs.items()) + list(b_msgs.items()):
            when(e, functools.partial(sent, msg))
        for (p, e), msg in z_msgs.items():
            k = (e - 1) % hops
            going = (z - k >= 0) & has_up if e <= hops else (z + k <= hops) & has_down
            pl.when(going)(functools.partial(sent, msg))
        for t in range(count):
            whole = pltpu.make_async_remote_copy(
                src_ref=outs[t].at[:, :, :, :, :, cols(t, c)], dst_ref=outs[t].at[:, :, :, :, :, cols(t, 1 - c)],
                send_sem=core_sems[t][0], recv_sem=core_sems[t][1], device_id=core, device_id_type=ON_MESH)
            whole.wait_send()
            whole.wait_recv()

    outs = pl.pallas_call(
        kernel,
        out_shape=[jax.ShapeDtypeStruct((m, hops + 1, 2, 2, 2 * r, w), jnp.bfloat16) for m, r, w in dims],
        in_specs=[pl.BlockSpec(memory_space=pl.ANY)] * count,
        out_specs=[pl.BlockSpec(memory_space=pl.ANY)] * count,
        scratch_shapes=[pltpu.VMEM((m, 2 * r, w // 2), jnp.float32) for m, r, w in dims]
        + [pltpu.VMEM((m, 2 * r, w // 2), jnp.bfloat16) for m, r, w in dims]
        + [pltpu.SemaphoreType.DMA((n_send,)), pltpu.SemaphoreType.DMA((n_send,)), pltpu.SemaphoreType.DMA((2 * count,))],
        compiler_params=pltpu.CompilerParams(collective_id=collective_id, has_side_effects=True, vmem_limit_bytes=40 << 20),
    )(*tensors)
    return [o.reshape(m, (hops + 1) * 8 * r, w) for o, (m, r, w) in zip(outs, dims)]


def scatter_blocks(tensors, portions, rows_own, collective_id):
    count = len(tensors)
    hops = 3
    dims = [(t.shape[0], r, t.shape[2]) for t, r in zip(tensors, rows_own)]
    views = [t.reshape(m, hops + 1, 2, 2, 2 * r, w) for t, (m, r, w) in zip(tensors, dims)]
    pieces_total = sum(len(p) for p in portions)
    n_send = pieces_total * (2 + 4 + 2 * hops + 4) + count
    n_local = pieces_total * 2 + count
    ways = range(len(portions))
    flat = [(p, piece) for p in ways for piece in portions[p]]
    flat_dims = [(piece[2] - piece[1], piece[4] - piece[3], dims[piece[0]][2] // 2) for _, piece in flat]

    def kernel(*refs):
        ins, outs = refs[:count], refs[count : 2 * count]
        k0 = 2 * count
        acc = refs[k0 : k0 + count]
        crecv = refs[k0 + count : k0 + 2 * count]
        fin = refs[k0 + 2 * count : k0 + 3 * count]
        k0 += 3 * count
        n = len(flat)
        b_all, u_all, d_all, a_all = (refs[k0 + i * n : k0 + (i + 1) * n] for i in range(4))
        send, recv, local = refs[k0 + 4 * n :]
        index = {}
        for i, (p, piece) in enumerate(flat):
            index.setdefault(p, []).append((i, piece))
        dp, seq, z, y, x, c = place()
        core = (dp, seq + 1 - 2 * c)
        xway = (dp, seq + 2 - 4 * x)
        yway = (dp + 1 - 2 * y, seq)
        up, down = (dp + 2, seq), (dp - 2, seq)
        has_up, has_down = z < hops, z > 0
        greet([core, xway, yway], [(has_up, up), (has_down, down)])
        sems = Sems(send, recv, local)
        a_way, b_way = (yway, xway) * 2, (xway, yway) * 2

        def cols(t, side):
            width = dims[t][2] // 2
            return pl.ds(pl.multiple_of(side * width, 128), width)

        def remote(src, dst, device):
            ss, rs = sems.pair()
            return pltpu.make_async_remote_copy(src_ref=src, dst_ref=dst, send_sem=ss, recv_sem=rs,
                                                device_id=device, device_id_type=ON_MESH)

        def place_of(p, zz, a, b):
            return (zz, a, b) if p % 2 == 0 else (zz, b, a)

        own_a, own_b = (y, x) * 2, (x, y) * 2

        def late(p):
            return p >= 2


        def add(dst, src, lead):
            def turn(i, _):
                where, rest = [], i
                for size in reversed(lead):
                    where.append(lax.rem(rest, size))
                    rest = rest // size
                where = tuple(reversed(where))
                dst[where] = (dst[where].astype(jnp.float32) + src[where].astype(jnp.float32)).astype(dst.dtype)
                return 0
            total = 1
            for size in lead:
                total *= size
            lax.fori_loop(0, total, turn, 0)

        everyz, both = slice(0, hops + 1), slice(0, 2)
        chunks = {}
        for far in (1, 0):
            for p in ways:
                b = own_b[p] if far == 0 else 1 - own_b[p]
                made = []
                for i, piece in index[p]:
                    t, m0, m1, r0, r1 = piece
                    where = (slice(m0, m1),) + place_of(p, everyz, both, b) + (slice(r0, r1),)
                    there = remote(ins[t].at[where + (cols(t, 1 - c),)], crecv[t].at[where], core)
                    here = pltpu.make_async_copy(ins[t].at[where + (cols(t, c),)], acc[t].at[where], sems.own())
                    there.start()
                    here.start()
                    made.append((there, here, piece, where))
                chunks[far, p] = made

        def core_add(far, p):
            for there, here, piece, where in chunks[far, p]:
                t, m0, m1, r0, r1 = piece
                there.wait_recv()
                here.wait()
                add(acc[t].at[where], crecv[t].at[where], (m1 - m0, hops + 1, 2))

        zorder = (3, 0, 2, 1)
        b_msgs = {}
        for p in ways:
            core_add(1, p)
            for zz in zorder:
                msgs = []
                for i, (t, m0, m1, r0, r1) in index[p]:
                    src = acc[t].at[(slice(m0, m1),) + place_of(p, zz, both, 1 - own_b[p]) + (slice(r0, r1),)]
                    msgs.append(remote(src, b_all[i].at[:, zz], b_way[p]))
                for msg in msgs:
                    msg.start()
                b_msgs[p, zz] = msgs
        for p in ways:
            core_add(0, p)

        def b_add(p, zz):
            for msg in b_msgs[p, zz]:
                msg.wait_recv()
            for i, (t, m0, m1, r0, r1) in index[p]:
                dst = acc[t].at[(slice(m0, m1),) + place_of(p, zz, both, own_b[p]) + (slice(r0, r1),)]
                add(dst, b_all[i].at[:, zz], (m1 - m0, 2))

        def mine(p, i, piece, zz):
            t, m0, m1, r0, r1 = piece
            a = own_a[p] if late(p) else both
            return acc[t].at[(slice(m0, m1),) + place_of(p, zz, a, own_b[p]) + (slice(r0, r1),)]

        def landing(p, land, i, zz):
            return land[i].at[:, zz, 0] if late(p) else land[i].at[:, zz]

        a_msgs = {}

        def a_start(p, zz):
            msgs = []
            for i, (t, m0, m1, r0, r1) in index[p]:
                src = acc[t].at[(slice(m0, m1),) + place_of(p, zz, 1 - own_a[p], own_b[p]) + (slice(r0, r1),)]
                msgs.append(remote(src, a_all[i].at[:, zz if late(p) else 0], a_way[p]))
            for msg in msgs:
                msg.start()
            a_msgs[p, zz if late(p) else 0] = msgs

        def a_add(p, zz):
            for msg in a_msgs[p, zz]:
                msg.wait_recv()
            for i, piece in index[p]:
                add(mine(p, i, piece, zz), a_all[i].at[:, zz], (piece[2] - piece[1],))

        up_msgs, down_msgs = {}, {}
        for p in ways:
            for zz in range(hops + 1):
                up_msgs[p, zz] = [remote(mine(p, i, piece, zz), landing(p, u_all, i, zz), up) for i, piece in index[p]] if zz > 0 else None
                down_msgs[p, zz] = [remote(mine(p, i, piece, zz), landing(p, d_all, i, zz), down) for i, piece in index[p]] if zz < hops else None

        def z_add(p, zz, msgs, land):
            for msg in msgs[p, zz]:
                msg.wait_recv()
            for i, piece in index[p]:
                lead = (piece[2] - piece[1],) if late(p) else (piece[2] - piece[1], 2)
                add(mine(p, i, piece, zz), landing(p, land, i, zz), lead)

        def up_send(p, zz):
            @pl.when(z < zz)
            def _():
                @pl.when(z > 0)
                def _():
                    z_add(p, zz, up_msgs, u_all)
                for msg in up_msgs[p, zz]:
                    msg.start()

        def down_send(p, zz):
            @pl.when(z > zz)
            def _():
                @pl.when(z < hops)
                def _():
                    z_add(p, zz, down_msgs, d_all)
                for msg in down_msgs[p, zz]:
                    msg.start()

        early_ways, late_ways = [p for p in ways if not late(p)], [p for p in ways if late(p)]
        for zz in zorder[:2]:
            for p in ways:
                b_add(p, zz)
                if late(p):
                    a_start(p, zz)
                elif zz == 3:
                    up_send(p, 3)
                else:
                    down_send(p, 0)
        for zz in zorder[2:]:
            for p in ways:
                b_add(p, zz)
                if late(p):
                    a_start(p, zz)
                elif zz == 2:
                    up_send(p, 2)
                else:
                    down_send(p, 1)
        for p in late_ways:
            a_add(p, 3)
            up_send(p, 3)
            a_add(p, 0)
            down_send(p, 0)
        for p in early_ways:
            up_send(p, 1)
            down_send(p, 2)
        for p in late_ways:
            a_add(p, 2)
            up_send(p, 2)
            a_add(p, 1)
            down_send(p, 1)
        for p in late_ways:
            up_send(p, 1)
            down_send(p, 2)
        for p in ways:
            for zz in range(hops + 1):
                @pl.when(z == zz)
                def _():
                    if zz > 0:
                        z_add(p, zz, up_msgs, u_all)
                    if zz < hops:
                        z_add(p, zz, down_msgs, d_all)
            if not late(p):
                a_start(p, z)
        for p in late_ways:
            for i, (t, m0, m1, r0, r1) in index[p]:
                for m in range(m0, m1):
                    fin[t][m, r0:r1, :] = acc[t][(m,) + place_of(p, z, own_a[p], own_b[p]) + (slice(r0, r1),)].astype(jnp.float32)
        for p in early_ways:
            for msg in a_msgs[p, 0]:
                msg.wait_recv()
            for i, (t, m0, m1, r0, r1) in index[p]:
                for m in range(m0, m1):
                    part = acc[t][(m,) + place_of(p, z, own_a[p], own_b[p]) + (slice(r0, r1),)]
                    fin[t][m, r0:r1, :] = part.astype(jnp.float32) + a_all[i][m - m0, 0].astype(jnp.float32)
        last = []
        for t in range(count):
            r = dims[t][1]
            other = remote(fin[t].at[:, pl.ds(pl.multiple_of((1 - c) * r, 8), r), :], outs[t].at[:, :, cols(t, c)], core)
            keep = pltpu.make_async_copy(fin[t].at[:, pl.ds(pl.multiple_of(c * r, 8), r), :], outs[t].at[:, :, cols(t, c)], sems.own())
            other.start()
            keep.start()
            last.append((other, keep))
        for made in chunks.values():
            for there, here, piece, where in made:
                there.wait_send()
        for msgs in list(b_msgs.values()) + list(a_msgs.values()):
            for msg in msgs:
                msg.wait_send()
        for p in ways:
            for zz in range(hops + 1):
                if zz > 0:
                    @pl.when(z < zz)
                    def _():
                        for msg in up_msgs[p, zz]:
                            msg.wait_send()
                if zz < hops:
                    @pl.when(z > zz)
                    def _():
                        for msg in down_msgs[p, zz]:
                            msg.wait_send()
        for other, keep in last:
            keep.wait()
            other.wait()

    bf = jnp.bfloat16
    outs = pl.pallas_call(
        kernel,
        out_shape=[jax.ShapeDtypeStruct((m, r, w), jnp.float32) for m, r, w in dims],
        in_specs=[pl.BlockSpec(memory_space=pl.ANY)] * count,
        out_specs=[pl.BlockSpec(memory_space=pl.ANY)] * count,
        scratch_shapes=[pltpu.VMEM((m, hops + 1, 2, 2, 2 * r, w // 2), bf) for m, r, w in dims]
        + [pltpu.VMEM((m, hops + 1, 2, 2, 2 * r, w // 2), bf) for m, r, w in dims]
        + [pltpu.VMEM((m, 2 * r, w // 2), jnp.float32) for m, r, w in dims]
        + [pltpu.VMEM((m, hops + 1, 2, r, w), bf) for m, r, w in flat_dims] * 3
        + [pltpu.VMEM((m, hops + 1, r, w), bf) for m, r, w in flat_dims]
        + [pltpu.SemaphoreType.DMA((n_send,)), pltpu.SemaphoreType.DMA((n_send,)), pltpu.SemaphoreType.DMA((n_local,))],
        compiler_params=pltpu.CompilerParams(collective_id=collective_id, has_side_effects=True, vmem_limit_bytes=60 << 20),
    )(*views)
    return list(lax.optimization_barrier(outs))


def exchange_everywhere(value, combine, collective_id):
    sizes = (("dp", lax.axis_size("dp")), ("seq", lax.axis_size("seq")))
    steps = [(axis, 1 << bit) for axis, size in reversed(sizes) for bit in range(size.bit_length() - 1)]

    def kernel(in_ref, out_ref, leave, land, send, recv):
        dp, seq = lax.axis_index("dp"), lax.axis_index("seq")
        partners = []
        for axis, step in steps:
            mine = dp if axis == "dp" else seq
            other = mine + step - 2 * step * lax.rem(mine // step, 2)
            partners.append((other, seq) if axis == "dp" else (dp, other))
        greet(partners, [])
        leave[0] = in_ref[...]
        for k, partner in enumerate(partners):
            copy = pltpu.make_async_remote_copy(
                src_ref=leave.at[k],
                dst_ref=land.at[k],
                send_sem=send.at[k],
                recv_sem=recv.at[k],
                device_id=partner,
                device_id_type=ON_MESH,
            )
            copy.start()
            copy.wait()
            both = combine(leave[k], land[k])
            if k + 1 < len(steps):
                leave[k + 1] = both
            else:
                out_ref[...] = both

    n = len(steps)
    return pl.pallas_call(
        kernel,
        out_shape=jax.ShapeDtypeStruct(value.shape, jnp.float32),
        in_specs=[pl.BlockSpec(memory_space=pltpu.VMEM)],
        out_specs=pl.BlockSpec(memory_space=pltpu.VMEM),
        scratch_shapes=[
            pltpu.VMEM((n,) + value.shape, jnp.float32),
            pltpu.VMEM((n,) + value.shape, jnp.float32),
            pltpu.SemaphoreType.DMA((n,)),
            pltpu.SemaphoreType.DMA((n,)),
        ],
        compiler_params=pltpu.CompilerParams(collective_id=collective_id, has_side_effects=True),
    )(value)


def add_logs(left, right):
    return jnp.maximum(left, right) + jnp.log(1.0 + jnp.exp(-jnp.abs(left - right)))


def head_forward(rows_all, head_cols, masked, local_ids, tile, sub):
    tokens, features = rows_all.shape
    width = head_cols.shape[1]

    def kernel(rows_ref, head_ref, masked_ref, ids_ref, p_ref, stats_ref):
        ids = jnp.transpose(jnp.broadcast_to(ids_ref[...], (128, tile)))[:, :1]
        lane = lax.broadcasted_iota(jnp.int32, (sub, 128), 1)
        column = lax.broadcasted_iota(jnp.int32, (sub, width), 1)
        for part in range(tile // sub):
            here = slice(part * sub, (part + 1) * sub)
            logits = jnp.dot(rows_ref[here, :], head_ref[...], preferred_element_type=jnp.float32)
            logits = logits + masked_ref[...]
            top = jnp.max(logits, axis=1, keepdims=True)
            picked = jnp.sum(jnp.where(column == ids[here], logits, 0.0), axis=1, keepdims=True)
            lifted = jnp.exp(logits - top)
            spread = jnp.sum(lifted, axis=1, keepdims=True)
            p_ref[here, :] = lifted.astype(jnp.bfloat16)
            table = jnp.where(lane == 0, top, jnp.where(lane == 1, spread, picked))
            stats_ref[:, here] = jnp.transpose(table)[:8]

    return pl.pallas_call(
        kernel,
        grid=(tokens // tile,),
        out_shape=[
            jax.ShapeDtypeStruct((tokens, width), jnp.bfloat16),
            jax.ShapeDtypeStruct((8, tokens), jnp.float32),
        ],
        in_specs=[
            pl.BlockSpec((tile, features), lambda i: (i, 0)),
            pl.BlockSpec((features, width), lambda i: (0, 0)),
            pl.BlockSpec((1, width), lambda i: (0, 0)),
            pl.BlockSpec((1, tile), lambda i: (0, i)),
        ],
        out_specs=[
            pl.BlockSpec((tile, width), lambda i: (i, 0)),
            pl.BlockSpec((8, tile), lambda i: (0, i)),
        ],
        compiler_params=pltpu.CompilerParams(vmem_limit_bytes=50 << 20),
    )(rows_all, head_cols, masked, local_ids[None])


def head_backward(lifted, rows_all, head_cols, local_ids, factors, tile, sub):
    tokens, width = lifted.shape
    features = rows_all.shape[1]
    steps = tokens // tile

    def kernel(p_ref, rows_ref, head_ref, ids_ref, factor_ref, d_rows_ref, d_head_ref, squares_ref, d_logits, total):
        step = pl.program_id(0)
        ids = jnp.transpose(jnp.broadcast_to(ids_ref[...], (128, tile)))[:, :1]
        scales = jnp.transpose(jnp.concatenate([factor_ref[...]] * 16, axis=0))
        scale, hit = scales[:, :1], scales[:, 1:2]
        column = lax.broadcasted_iota(jnp.int32, (sub, width), 1)
        for part in range(tile // sub):
            here = slice(part * sub, (part + 1) * sub)
            d_logits[here, :] = jnp.where(
                column == ids[here], hit[here], p_ref[here, :].astype(jnp.float32) * scale[here]
            ).astype(jnp.bfloat16)
            d_rows_ref[here, :] = lax.dot_general(
                d_logits[here, :], head_ref[...], (((1,), (1,)), ((), ())), preferred_element_type=jnp.float32
            ).astype(jnp.bfloat16)
        term = lax.dot_general(
            rows_ref[...], d_logits[...], (((0,), (0,)), ((), ())), preferred_element_type=jnp.float32
        )

        @pl.when(step == 0)
        def _():
            total[...] = term

        @pl.when(step > 0)
        def _():
            total[...] += term

        @pl.when(step == steps - 1)
        def _():
            low = total[...].astype(jnp.bfloat16)
            d_head_ref[...] = low
            wide = low.astype(jnp.float32)
            squares_ref[...] = jnp.sum((wide * wide).reshape(features // 8, 8, width), axis=0)

    return pl.pallas_call(
        kernel,
        grid=(steps,),
        out_shape=[
            jax.ShapeDtypeStruct((tokens, features), jnp.bfloat16),
            jax.ShapeDtypeStruct((features, width), jnp.bfloat16),
            jax.ShapeDtypeStruct((8, width), jnp.float32),
        ],
        in_specs=[
            pl.BlockSpec((tile, width), lambda i: (i, 0)),
            pl.BlockSpec((tile, features), lambda i: (i, 0)),
            pl.BlockSpec((features, width), lambda i: (0, 0)),
            pl.BlockSpec((1, tile), lambda i: (0, i)),
            pl.BlockSpec((8, tile), lambda i: (0, i)),
        ],
        out_specs=[
            pl.BlockSpec((tile, features), lambda i: (i, 0)),
            pl.BlockSpec((features, width), lambda i: (0, 0)),
            pl.BlockSpec((8, width), lambda i: (0, 0)),
        ],
        scratch_shapes=[pltpu.VMEM((tile, width), jnp.bfloat16), pltpu.VMEM((features, width), jnp.float32)],
        compiler_params=pltpu.CompilerParams(vmem_limit_bytes=56 << 20),
    )(lifted, rows_all, head_cols, local_ids[None], factors)


def head_backward_scattered(lifted, rows_all, head_cols, local_ids, factors, collective_id):
    tokens, width = lifted.shape
    features = rows_all.shape[1]
    hops, block = 3, tokens // 16
    rows, wing = block // 2, features // 2
    zorder = (3, 0, 2, 1)
    cuts = [slice(k, min(k + 512, width)) for k in range(0, width - 256, 512)]
    cuts[-1] = slice(cuts[-1].start, width)
    parts = (slice(0, rows), slice(rows, block))

    def kernel(p_hbm, rows_hbm, head_ref, ids_ref, factor_ref, out, d_head_ref, squares_ref,
               p_buf, r_buf, d_logits, total, acc, give, crecv, b_all, u_all, d_all, a_all, fin,
               in_sem, core_send, core_recv, send, recv, local):
        dp, seq, z, y, x, c = place()
        core = (dp, seq + 1 - 2 * c)
        xway = (dp, seq + 2 - 4 * x)
        yway = (dp + 1 - 2 * y, seq)
        up, down = (dp + 2, seq), (dp - 2, seq)
        has_up, has_down = z < hops, z > 0
        groups = ((1 - y, 1 - x), (y, 1 - x), (1 - y, x), (y, x))

        def fetch(slot, zz, yy, xx):
            return (
                pltpu.make_async_copy(p_hbm.at[zz, yy, xx], p_buf.at[slot], in_sem.at[slot, 0]),
                pltpu.make_async_copy(rows_hbm.at[zz, yy, xx], r_buf.at[slot], in_sem.at[slot, 1]),
            )

        for copy in fetch(0, zorder[0], *groups[0]):
            copy.start()
        greet([core, xway, yway], [(has_up, up), (has_down, down)])
        sems = Sems(send, recv, local)

        def remote(src, dst, device):
            ss, rs = sems.pair()
            return pltpu.make_async_remote_copy(src_ref=src, dst_ref=dst, send_sem=ss, recv_sem=rs,
                                                device_id=device, device_id_type=ON_MESH)

        def to_core(g, k, zz):
            yy, xx = groups[g]
            return pltpu.make_async_remote_copy(
                src_ref=give.at[k], dst_ref=crecv.at[zz, yy, xx], send_sem=core_send.at[g * 4 + k],
                recv_sem=core_recv.at[g * 4 + k], device_id=core, device_id_type=ON_MESH)

        total[...] = jnp.zeros_like(total)
        column = lax.broadcasted_iota(jnp.int32, (rows, width), 1)

        def zz_of(k):
            return jnp.where(k == 0, 3, jnp.where(k == 1, 0, jnp.where(k == 2, 2, 1)))

        def compute(g, k):
            yy, xx = groups[g]
            zz = zz_of(k)
            slot = lax.rem(k, 2)
            for copy in fetch(slot, zz, yy, xx):
                copy.wait()
            if g < 3:
                more = k < 4
            else:
                more = k < 3
            nyy, nxx = groups[min(g + 1, 3)]
            last = k == 3

            @pl.when(more)
            def _():
                for copy in fetch(1 - slot, jnp.where(last, 3, zz_of(k + 1)), jnp.where(last, nyy, yy), jnp.where(last, nxx, xx)):
                    copy.start()
            first = pl.multiple_of(((zz * 2 + yy) * 2 + xx) * block, block)
            here = pl.ds(first, block)
            ids = jnp.transpose(jnp.broadcast_to(ids_ref[:, here], (128, block)))[:, :1]
            scales = jnp.transpose(jnp.concatenate([factor_ref[:, here]] * 16, axis=0))
            if g > 0:
                to_core(g - 1, k, zz).wait_send()
            for part in parts:
                d_logits[part, :] = jnp.where(
                    column == ids[part], scales[part, 1:2], p_buf[slot, part, :].astype(jnp.float32) * scales[part, :1]
                ).astype(jnp.bfloat16)
                d_rows = lax.dot_general(
                    d_logits[part, :], head_ref[...], (((1,), (1,)), ((), ())), preferred_element_type=jnp.float32)
                left, right = d_rows[:, :wing], d_rows[:, wing:]
                acc[zz, yy, xx, part, :] = jnp.where(c == 0, left, right).astype(jnp.bfloat16)
                give[k, part, :] = jnp.where(c == 0, right, left).astype(jnp.bfloat16)
            to_core(g, k, zz).start()
            for cut in cuts:
                total[:, cut] += lax.dot_general(
                    r_buf[slot], d_logits[:, cut], (((0,), (0,)), ((), ())), preferred_element_type=jnp.float32)

        def add(dst, src):
            dst[...] = (dst[...].astype(jnp.float32) + src[...].astype(jnp.float32)).astype(dst.dtype)

        own_b = (x, y)
        own_a = (y, x)
        b_way, a_way = (xway, yway), (yway, xway)

        def spot(p, zz, a, b):
            yy, xx = (a, b) if p == 0 else (b, a)
            return acc.at[zz, yy, xx, parts[p]]

        b_msgs, z_up, z_down = {}, {}, {}
        for p in range(2):
            for zz in range(hops + 1):
                for near in range(2):
                    a = own_a[p] if near else 1 - own_a[p]
                    b_msgs[p, zz, near] = remote(spot(p, zz, a, 1 - own_b[p]), b_all.at[p, zz, a], b_way[p])
                    mine = spot(p, zz, a, own_b[p])
                    if zz > 0:
                        z_up[p, zz, near] = remote(mine, u_all.at[p, zz - 1, a], up)
                    if zz < hops:
                        z_down[p, zz, near] = remote(mine, d_all.at[p, zz, a], down)

        def core_add(g):
            yy, xx = groups[g]
            for k, zz in enumerate(zorder):
                to_core(g, k, zz).wait_recv()
                for part in parts:
                    add(acc.at[zz, yy, xx, part], crecv.at[zz, yy, xx, part])
                for p, near in (((0, 0), (1, 0)), ((0, 1),), ((1, 1),), ())[g]:
                    b_msgs[p, zz, near].start()

        def b_add(p, near):
            a = own_a[p] if near else 1 - own_a[p]
            for zz in zorder:
                b_msgs[p, zz, near].wait_recv()
                add(spot(p, zz, a, own_b[p]), b_all.at[p, zz, a])

        def z_take(p, zz, near, msgs, land):
            a = own_a[p] if near else 1 - own_a[p]
            msgs[p, zz, near].wait_recv()
            add(spot(p, zz, a, own_b[p]), land.at[p, zz - 1 if msgs is z_up else zz, a])

        def z_hop(p, near, hop):
            @pl.when(z == hop)
            def _():
                for zz in range(hops, hop, -1):
                    if hop > 0:
                        z_take(p, zz, near, z_up, u_all)
                    z_up[p, zz, near].start()

            @pl.when(z == hops - hop)
            def _():
                for zz in range(0, hops - hop):
                    if hop > 0:
                        z_take(p, zz, near, z_down, d_all)
                    z_down[p, zz, near].start()

        def run(g):
            def turn(k, _):
                compute(g, k)
                return 0
            lax.fori_loop(0, 4, turn, 0)

        run(0)
        core_add(0)
        run(1)
        core_add(1)
        b_add(1, 0)
        z_hop(1, 0, 0)
        run(2)
        core_add(2)
        b_add(0, 0)
        z_hop(0, 0, 0)
        z_hop(1, 0, 1)
        run(3)
        core_add(3)
        for p in range(2):
            b_add(p, 1)
            z_hop(p, 1, 0)
        z_hop(0, 0, 1)
        z_hop(1, 0, 2)
        for p in range(2):
            z_hop(p, 1, 1)
        z_hop(0, 0, 2)
        for p in range(2):
            z_hop(p, 1, 2)
        low = total[...].astype(jnp.bfloat16)
        d_head_ref[...] = low
        wide = low.astype(jnp.float32)
        squares_ref[...] = jnp.sum((wide * wide).reshape(features // 8, 8, width), axis=0)
        a_msgs = []
        for p in range(2):
            for zz in range(hops + 1):
                @pl.when(z == zz)
                def _():
                    for near in range(2):
                        if zz > 0:
                            z_take(p, zz, near, z_up, u_all)
                        if zz < hops:
                            z_take(p, zz, near, z_down, d_all)
            msg = remote(spot(p, z, 1 - own_a[p], own_b[p]), a_all.at[p], a_way[p])
            msg.start()
            a_msgs.append(msg)
        for p in range(2):
            a_msgs[p].wait_recv()
            fin[parts[p], :] = spot(p, z, own_a[p], own_b[p])[...].astype(jnp.float32) + a_all[p].astype(jnp.float32)
        side = pl.ds(pl.multiple_of(c * wing, 128), wing)
        other = remote(fin.at[pl.ds(pl.multiple_of((1 - c) * rows, 8), rows), :], out.at[:, side], core)
        keep = pltpu.make_async_copy(fin.at[pl.ds(pl.multiple_of(c * rows, 8), rows), :], out.at[:, side], sems.own())
        other.start()
        keep.start()
        for k in range(4):
            to_core(3, k, zorder[k]).wait_send()
        for msg in list(b_msgs.values()) + a_msgs:
            msg.wait_send()
        for zz in range(hops + 1):
            @pl.when(z < zz)
            def _():
                for p in range(2):
                    for near in range(2):
                        if zz > 0:
                            z_up[p, zz, near].wait_send()

            @pl.when(z > zz)
            def _():
                for p in range(2):
                    for near in range(2):
                        if zz < hops:
                            z_down[p, zz, near].wait_send()
        keep.wait()
        other.wait()

    bf = jnp.bfloat16
    n_send = 2 * 8 + 2 * 2 * 2 * hops + 2 + 1
    whole = pl.BlockSpec(memory_space=pltpu.VMEM)
    return pl.pallas_call(
        kernel,
        out_shape=[
            jax.ShapeDtypeStruct((rows, features), jnp.float32),
            jax.ShapeDtypeStruct((features, width), bf),
            jax.ShapeDtypeStruct((8, width), jnp.float32),
        ],
        in_specs=[pl.BlockSpec(memory_space=pl.ANY)] * 2 + [whole] * 3,
        out_specs=[pl.BlockSpec(memory_space=pl.ANY), whole, whole],
        scratch_shapes=[
            pltpu.VMEM((2, block, width), bf),
            pltpu.VMEM((2, block, features), bf),
            pltpu.VMEM((block, width), bf),
            pltpu.VMEM((features, width), jnp.float32),
            pltpu.VMEM((hops + 1, 2, 2, block, wing), bf),
            pltpu.VMEM((4, block, wing), bf),
            pltpu.VMEM((hops + 1, 2, 2, block, wing), bf),
            pltpu.VMEM((2, hops + 1, 2, rows, wing), bf),
            pltpu.VMEM((2, hops, 2, rows, wing), bf),
            pltpu.VMEM((2, hops, 2, rows, wing), bf),
            pltpu.VMEM((2, rows, wing), bf),
            pltpu.VMEM((block, wing), jnp.float32),
            pltpu.SemaphoreType.DMA((2, 2)),
            pltpu.SemaphoreType.DMA((16,)),
            pltpu.SemaphoreType.DMA((16,)),
            pltpu.SemaphoreType.DMA((n_send,)),
            pltpu.SemaphoreType.DMA((n_send,)),
            pltpu.SemaphoreType.DMA((1,)),
        ],
        compiler_params=pltpu.CompilerParams(collective_id=collective_id, has_side_effects=True, vmem_limit_bytes=60 << 20),
    )(
        lifted.reshape(hops + 1, 2, 2, block, width),
        rows_all.reshape(hops + 1, 2, 2, block, features),
        head_cols,
        local_ids[None],
        factors,
    )


def embed_gradient(columns, token_ids, vocab, block):
    features, tokens = columns.shape
    lanes = 128
    high_rows = -(-vocab // (8 * lanes)) * 8
    group = 2
    steps = tokens // block

    def kernel(columns_ref, ids_ref, out_ref, squares_ref):
        step = pl.program_id(0)
        ids = ids_ref[...]
        high = lax.broadcasted_iota(jnp.int32, (high_rows, block), 0) == lax.shift_right_logical(ids, 7)
        high = jnp.where(high, 1.0, 0.0).astype(jnp.bfloat16)
        low = lax.broadcasted_iota(jnp.int32, (lanes, block), 0) == jnp.bitwise_and(ids, lanes - 1)
        values = columns_ref[...].astype(jnp.float32)

        @pl.when(step == 0)
        def _():
            out_ref[...] = jnp.zeros_like(out_ref)

        for first in range(0, features, group):
            spread = jnp.concatenate(
                [jnp.where(low, values[f : f + 1], 0.0).astype(jnp.bfloat16) for f in range(first, first + group)], axis=0
            )
            term = lax.dot_general(high, spread, (((1,), (1,)), ((), ())), preferred_element_type=jnp.float32)
            for k in range(group):
                out_ref[first + k] += term[:, k * lanes : (k + 1) * lanes]

        @pl.when(step == steps - 1)
        def _():
            def turn(f, total):
                one = out_ref[f]
                return total + jnp.sum((one * one).reshape(high_rows // 8, 8, lanes), axis=0)
            squares_ref[...] = lax.fori_loop(0, features, turn, jnp.zeros((8, lanes), jnp.float32))

    sums, squares = pl.pallas_call(
        kernel,
        grid=(steps,),
        out_shape=[
            jax.ShapeDtypeStruct((features, high_rows, lanes), jnp.float32),
            jax.ShapeDtypeStruct((8, lanes), jnp.float32),
        ],
        in_specs=[pl.BlockSpec((features, block), lambda i: (0, i)), pl.BlockSpec((1, block), lambda i: (0, i))],
        out_specs=[
            pl.BlockSpec((features, high_rows, lanes), lambda i: (0, 0, 0)),
            pl.BlockSpec((8, lanes), lambda i: (0, 0)),
        ],
        compiler_params=pltpu.CompilerParams(vmem_limit_bytes=50 << 20),
    )(columns, token_ids[None])
    return sums[:, : vocab // lanes].reshape(features, vocab), squares


BOTH = ("dp", "seq")
mark_height = 8


def mark_rows(targets, loss_mask):
    own = targets.shape[0] // lax.axis_size("seq")
    first = lax.axis_index("seq") * own
    own_targets = lax.dynamic_slice_in_dim(targets, first, own)
    own_mask = lax.dynamic_slice_in_dim(loss_mask, first, own)
    rows = jnp.stack([own_targets // 256, own_targets % 256, own_mask]).astype(jnp.float32)
    return jnp.pad(rows, ((0, mark_height - 3), (0, 0)))[None]


def marks_of(gathered):
    rows = gathered[0].reshape(-1, mark_height, gathered.shape[2]).astype(jnp.float32)
    numbers = rows[:, :3].transpose(1, 0, 2).reshape(3, -1).astype(jnp.int32)
    return (numbers[0] * 256 + numbers[1], numbers[2])


def on_box():
    return lax.axis_size("dp") == 8 and lax.axis_size("seq") == 4


def gather_rows(tensors, portions, collective_id):
    if on_box():
        return gather_blocks(tensors, portions, collective_id)
    return gather_plain(tensors)


def gather_plain(tensors):
    return [lax.all_gather(t.astype(jnp.bfloat16), BOTH, axis=1, tiled=True) for t in tensors]


def scatter_rows(tensors, portions, collective_id):
    if on_box():
        devices = lax.axis_size("dp") * lax.axis_size("seq")
        rows = [t.shape[1] // devices for t in tensors]
        return scatter_blocks(tensors, portions, rows, collective_id)
    return scatter_plain(tensors)


def scatter_plain(tensors):
    return [
        lax.psum_scatter(t, BOTH, scatter_dimension=1, tiled=True).astype(jnp.float32) for t in tensors
    ]


def scatter_joined(square, expand, shrink):
    width, count = square.shape[2], square.shape[0]
    cut = [expand[:, :, k : k + width] for k in range(0, expand.shape[2], width)]
    shrink_sum, both = scatter_plain([shrink, jnp.concatenate([square] + cut)])
    wide = jnp.concatenate([both[k : k + 1] for k in range(count, both.shape[0])], axis=2)
    return [both[:count], wide, shrink_sum]


def gradient_portions(square, expand, shrink):
    return [
        [(1, 0, 1, 0, 2 * expand), (0, 0, 1, 0, 2 * square)],
        [(2, 0, 1, 0, 2 * shrink), (4, 0, 1, 0, 2 * square)],
        [(0, 1, 4, 0, 2 * square)],
        [(0, 4, 5, 0, 2 * square), (4, 1, 3, 0, 2 * square), (3, 0, 1, 0, 2 * square)],
    ]


def weight_portions(square, expand, shrink, vectors, marks=0):
    split = 2 * square * 2 // 3
    first = [(1, 0, 1, 0, 2 * expand)]
    second = [(2, 0, 1, 0, 2 * shrink)]
    third = [(0, 0, 2, 0, 2 * square), (0, 2, 3, 0, split)]
    fourth = [(0, 3, 5, 0, 2 * square), (0, 2, 3, split, 2 * square)]
    if vectors:
        fourth.append((3, 0, 1, 0, 2 * vectors))
    if marks:
        fourth.append((4, 0, 1, 0, 2 * marks))
    return [first, second, third, fourth]


def row_portions(rows):
    ends = [0, rows * 5 // 8, rows * 10 // 8, rows * 13 // 8, 2 * rows]
    return [[(0, 0, 1, first, last)] for first, last in zip(ends, ends[1:])]


def as_rows(vectors):
    lanes = -(-vectors.shape[0] // 256) * 256
    return jnp.pad(vectors.T, ((0, 0), (0, lanes - vectors.shape[0])))[None]

EXACT_MATMUL = lax.Precision.HIGHEST
BETA_ONE = 0.9
BETA_TWO = 0.999
ADAM_EPS = 1e-08
WEIGHT_DECAY = 0.01
LEARN_RATES = (0.03, 0.03, 0.015, 0.5, 2.0, 0.05)
DECAY_FLAGS = (True, True, True, False, True, True)
param_stride = 11
head_tile = 1024
embed_block = 1024
far_below = -1e30
joined = 2
scan_block = 256


def from_behind(value, axis, steps):
    count = lax.axis_size(axis)
    leading, last = (max(0, -steps), min(count, count - steps))
    return lax.ppermute(value, axis, [(source, source + steps) for source in range(leading, last)])


def carried_in(value, axis, join, neutral, backward):
    count, mine = (lax.axis_size(axis), lax.axis_index(axis))
    pieces = lax.all_gather(jnp.stack(value), axis)
    if backward:
        pieces = pieces[::-1]
        mine = count - 1 - mine
    running = neutral
    for position in range(count - 1):
        longer = join(running, tuple(pieces[position]))
        running = tuple(
            jnp.where(position < mine, new, old) for new, old in zip(longer, running)
        )
    return running


def layer_norm(values, gain, bias):
    centre = values - jnp.mean(values, axis=-1, keepdims=True)
    spread = jnp.mean(centre * centre, axis=-1, keepdims=True)
    return centre * lax.rsqrt(spread + 1e-05) * gain + bias


def matmul(left, right):
    return jnp.dot(left, right, preferred_element_type=jnp.float32)


def matmul_tn(left, right):
    return lax.dot_general(
        left, right, (((0,), (0,)), ((), ())), preferred_element_type=jnp.float32
    )


def matmul_nt(left, right):
    return lax.dot_general(
        left, right, (((1,), (1,)), ((), ())), preferred_element_type=jnp.float32
    )


def blend_all(normed, incoming, shares):
    earlier = jnp.concatenate([incoming, normed[:-1]], axis=0)
    return tuple(
        (
            normed * shares[member] + earlier * (1.0 - shares[member])
            for member in range(shares.shape[0])
        )
    )


def take_previous(normed):
    return from_behind(normed[-1:], "seq", 1)


def give_back(grad_first):
    return from_behind(grad_first, "seq", -1)


def block_ends(arriving_lookups, arriving_contents, logarithmic_fading_speed):
    decay_rate = jnp.exp(logarithmic_fading_speed)
    length = arriving_lookups.shape[0]
    ages = (length - 1.0 - jnp.arange(length, dtype=jnp.float32))[:, None]
    weight = jnp.exp(arriving_lookups - decay_rate * ages)
    return (jnp.sum(weight * arriving_contents, axis=0), jnp.sum(weight, axis=0))


def block_factor(logarithmic_fading_speed, length):
    return jnp.exp(-jnp.exp(logarithmic_fading_speed) * length)


def chain_combine(earlier, later):
    return (
        earlier[0] * later[2] + later[0],
        earlier[1] * later[2] + later[1],
        earlier[2] * later[2],
    )


def token_mixer_block(
    arriving_lookups,
    arriving_contents,
    logarithmic_fading_speed,
    present_reward,
    initial_numerator,
    initial_denominator,
):
    decay_rate = jnp.exp(logarithmic_fading_speed)
    length, channels = arriving_lookups.shape
    block_size = min(scan_block, length)
    block_count = length // block_size
    offsets = jnp.arange(block_size, dtype=jnp.float32)[:, None]
    lower_mask = (offsets > offsets.T).astype(jnp.float32)
    diagonal_amplifier = jnp.exp(present_reward)
    back_decay = jnp.exp(-decay_rate * (offsets - 1.0))
    carry_decay = jnp.exp(-decay_rate * offsets)
    tail_decay = jnp.exp(-decay_rate * (block_size - 1.0))
    full_decay = jnp.exp(-decay_rate * block_size)

    def sub_block(state, step_item):
        numerator, denominator = state
        key_block, value_block = step_item
        lifted = jnp.exp(key_block + decay_rate * offsets)
        prefix_sums = jnp.dot(
            lower_mask,
            jnp.concatenate([lifted * value_block, lifted], axis=1),
            precision=EXACT_MATMUL,
        )
        own_term = diagonal_amplifier * jnp.exp(key_block)
        top_part = (
            back_decay * prefix_sums[:, :channels]
            + carry_decay * numerator
            + own_term * value_block
        )
        low_part = back_decay * prefix_sums[:, channels:] + carry_decay * denominator + own_term
        next_num = tail_decay * jnp.sum(lifted * value_block, axis=0) + full_decay * numerator
        next_den = tail_decay * jnp.sum(lifted, axis=0) + full_decay * denominator
        return ((next_num, next_den), (top_part / low_part, low_part))

    shaped = (
        arriving_lookups.reshape(block_count, block_size, channels),
        arriving_contents.reshape(block_count, block_size, channels),
    )
    (end_num, end_den), (block_outs, denoms) = lax.scan(
        sub_block, (initial_numerator, initial_denominator), shaped
    )
    return (
        (block_outs.reshape(length, channels), end_num, end_den),
        denoms.reshape(length, channels),
    )


def layer_forward(stream, gathered):
    square, expand, shrink, params = gathered
    normed = layer_norm(stream, params[0], params[1])
    incoming_one = take_previous(normed)
    blended = blend_all(normed, incoming_one, params[2:5])
    mixed_key = blended[0].astype(jnp.bfloat16)
    mixed_value = blended[1].astype(jnp.bfloat16)
    mixed_gate = blended[2].astype(jnp.bfloat16)
    arriving_lookups = matmul(mixed_key, square[0])
    arriving_contents = matmul(mixed_value, square[1])
    gates_in = matmul(mixed_gate, square[2])
    length = arriving_lookups.shape[0]
    end_sums = block_ends(arriving_lookups, arriving_contents, params[5])
    zero_state = jnp.zeros_like(end_sums[0])
    one_state = jnp.ones_like(end_sums[0])
    factor = block_factor(params[5], length)
    initial_numerator, initial_denominator, spare_factor = carried_in(
        (end_sums[0], end_sums[1], factor),
        "seq",
        chain_combine,
        (zero_state, zero_state, one_state),
        False,
    )
    (mixed_out, spare_placeholder, spare_placeholder), spare_placeholder = token_mixer_block(
        arriving_lookups,
        arriving_contents,
        params[5],
        params[6],
        initial_numerator,
        initial_denominator,
    )
    gated = (jax.nn.sigmoid(gates_in) * mixed_out).astype(jnp.bfloat16)
    middle = stream + matmul(gated, square[3])
    normed_two = layer_norm(middle, params[7], params[8])
    incoming_two = take_previous(normed_two)
    blended_two = blend_all(normed_two, incoming_two, params[9:11])
    chan_key = blended_two[0].astype(jnp.bfloat16)
    chan_gate = blended_two[1].astype(jnp.bfloat16)
    pre_act = matmul(chan_key, expand)
    activated = jnp.square(jnp.maximum(pre_act, 0.0)).astype(jnp.bfloat16)
    chan_value = matmul(activated, shrink)
    gate_pre = matmul(chan_gate, square[4])
    result = middle + jax.nn.sigmoid(gate_pre) * chan_value
    saved = (
        stream,
        incoming_one,
        mixed_key,
        mixed_value,
        mixed_gate,
        arriving_lookups,
        arriving_contents,
        gates_in,
        initial_numerator,
        initial_denominator,
        gated,
        middle,
        incoming_two,
        chan_key,
        chan_gate,
        pre_act,
        activated,
        chan_value,
        gate_pre,
    )
    return (result, saved)


def norm_back(stream, incoming, params, first_row, share_rows, grads):
    normed, norm_pull = jax.vjp(layer_norm, stream, params[first_row], params[first_row + 1])
    shares = params[share_rows[0] : share_rows[1]]
    spare_placeholder, blend_pull = jax.vjp(blend_all, normed, incoming, shares)
    d_normed, d_incoming, d_shares = blend_pull(grads)
    from_next = give_back(d_incoming)
    d_normed = d_normed.at[-1].add(from_next[0])
    d_stream, d_gain, d_bias = norm_pull(d_normed)
    return (d_stream, jnp.stack([d_gain, d_bias]), d_shares)


def layer_backward(gradient, saved, gathered):
    square, expand, shrink, params = gathered
    (
        stream,
        incoming_one,
        mixed_key,
        mixed_value,
        mixed_gate,
        arriving_lookups,
        arriving_contents,
        gates_in,
        initial_numerator,
        initial_denominator,
        gated,
        middle,
        incoming_two,
        chan_key,
        chan_gate,
        pre_act,
        activated,
        chan_value,
        gate_pre,
    ) = saved
    gate_sig = jax.nn.sigmoid(gate_pre)
    d_value = (gradient * gate_sig).astype(jnp.bfloat16)
    d_gate_pre = (gradient * chan_value * gate_sig * (1.0 - gate_sig)).astype(jnp.bfloat16)
    g_shrink = matmul_tn(activated, d_value)
    d_active = matmul_nt(d_value, shrink)
    d_pre = (d_active * 2.0 * jnp.maximum(pre_act, 0.0)).astype(jnp.bfloat16)
    g_expand = matmul_tn(chan_key, d_pre)
    g_chan_gate = matmul_tn(chan_gate, d_gate_pre)
    d_chan_key = matmul_nt(d_pre, expand)
    d_chan_gate = matmul_nt(d_gate_pre, square[4])
    d_middle, second_norm_gradient, second_share_gradient = norm_back(
        middle, incoming_two, params, 7, (9, 11), (d_chan_key, d_chan_gate)
    )
    d_middle = d_middle + gradient
    d_output = d_middle.astype(jnp.bfloat16)
    g_output = matmul_tn(gated, d_output)
    d_gated = matmul_nt(d_output, square[3])
    (mixed_out, spare_placeholder, spare_placeholder), token_mixer_backward, denoms = jax.vjp(
        token_mixer_block,
        arriving_lookups,
        arriving_contents,
        params[5],
        params[6],
        initial_numerator,
        initial_denominator,
        has_aux=True,
    )
    gate_sig_one = jax.nn.sigmoid(gates_in)
    mixed_gradient = d_gated * gate_sig_one
    d_gates_in = (d_gated * mixed_out * gate_sig_one * (1.0 - gate_sig_one)).astype(jnp.bfloat16)
    length = arriving_lookups.shape[0]
    decay_rate = jnp.exp(params[5])
    carried = (
        jnp.exp(-decay_rate * jnp.arange(length, dtype=jnp.float32)[:, None])
        * mixed_gradient
        / denoms
    )
    zero_state = jnp.zeros_like(decay_rate)
    one_state = jnp.ones_like(decay_rate)
    factor = block_factor(params[5], length)
    following_numerator, following_denominator, spare_factor = carried_in(
        (jnp.sum(carried, axis=0), -jnp.sum(carried * mixed_out, axis=0), factor),
        "seq",
        chain_combine,
        (zero_state, zero_state, one_state),
        True,
    )
    (
        lookup_sensitivity,
        content_sensitivity,
        fading_sensitivity,
        reward_sensitivity,
        spare_placeholder,
        spare_placeholder,
    ) = token_mixer_backward((mixed_gradient, following_numerator, following_denominator))
    lookup_sensitivity = lookup_sensitivity.astype(jnp.bfloat16)
    content_sensitivity = content_sensitivity.astype(jnp.bfloat16)
    g_key = matmul_tn(mixed_key, lookup_sensitivity)
    g_value = matmul_tn(mixed_value, content_sensitivity)
    g_gate = matmul_tn(mixed_gate, d_gates_in)
    d_mixed_key = matmul_nt(lookup_sensitivity, square[0])
    d_mixed_value = matmul_nt(content_sensitivity, square[1])
    d_mixed_gate = matmul_nt(d_gates_in, square[2])
    d_stream, first_norm_gradient, first_share_gradient = norm_back(
        stream, incoming_one, params, 0, (2, 5), (d_mixed_key, d_mixed_value, d_mixed_gate)
    )
    d_stream = d_stream + d_middle
    g_square = jnp.stack([g_key, g_value, g_gate, g_output, g_chan_gate])
    g_params = jnp.concatenate(
        [
            first_norm_gradient,
            first_share_gradient,
            fading_sensitivity[None],
            reward_sensitivity[None],
            second_norm_gradient,
            second_share_gradient,
        ],
        axis=0,
    )
    return (d_stream, (g_square, g_expand, g_shrink, g_params))


def adam_update(weights, gradient, first, second, step_rate, decay_on):
    first_new = BETA_ONE * first + (1.0 - BETA_ONE) * gradient
    second_new = BETA_TWO * second + (1.0 - BETA_TWO) * gradient * gradient
    first_hat = first_new / (1.0 - BETA_ONE**STEP)
    second_hat = second_new / (1.0 - BETA_TWO**STEP)
    moved = first_hat / (jnp.sqrt(second_hat) + ADAM_EPS)
    if decay_on:
        moved = moved + WEIGHT_DECAY * weights
    return (weights - step_rate * moved, first_new, second_new)


def adam_columns(weights, pieces, first, second, scale, slot):
    rows, columns = weights.shape
    width = pieces.shape[2]

    def kernel(w_ref, g_ref, first_ref, second_ref, scale_ref, w_out, first_out, second_out):
        gradient = g_ref[0].astype(jnp.float32) * scale_ref[0]
        w_out[...], first_out[...], second_out[...] = adam_update(
            w_ref[...], gradient, first_ref[...], second_ref[...], LEARN_RATES[slot], DECAY_FLAGS[slot]
        )

    block = pl.BlockSpec((rows, width), lambda i: (0, i))
    return pl.pallas_call(
        kernel,
        grid=(-(-columns // width),),
        out_shape=[jax.ShapeDtypeStruct(weights.shape, jnp.float32)] * 3,
        in_specs=[
            block,
            pl.BlockSpec((1, rows, width), lambda i: (i, 0, 0)),
            block,
            block,
            pl.BlockSpec(memory_space=pltpu.SMEM),
        ],
        out_specs=[block] * 3,
        compiler_params=pltpu.CompilerParams(vmem_limit_bytes=40 << 20),
    )(weights, pieces, first, second, scale[None])


def per_device(
    token_ids,
    targets,
    loss_mask,
    square_weights,
    expand_weights,
    shrink_weights,
    vector_params,
    embed_table,
    head_table,
    square_first,
    expand_first,
    shrink_first,
    vector_first,
    embed_first,
    head_first,
    square_second,
    expand_second,
    shrink_second,
    vector_second,
    embed_second,
    head_second,
):
    layers = square_weights.shape[0]
    global_rows = param_stride * layers
    total_tokens = token_ids.shape[0]

    vector_rows = vector_params.shape[0]
    square_own, expand_own, shrink_own = (
        square_weights.shape[2],
        expand_weights.shape[1],
        shrink_weights.shape[1],
    )

    def fetch_layer(layer_id):
        with_vectors = layer_id == 0
        shards = [
            square_weights[layer_id],
            expand_weights[layer_id][None],
            shrink_weights[layer_id][None],
        ]
        if with_vectors:
            shards.append(as_rows(vector_params))
            shards.append(mark_rows(targets, loss_mask))
        else:
            return gather_plain(shards)
        return gather_rows(
            shards,
            weight_portions(
                square_own,
                expand_own,
                shrink_own,
                with_vectors * square_own,
                with_vectors * mark_height,
            ),
            layer_id,
        )

    fetched = [fetch_layer(layer_id) for layer_id in range(layers)]
    vectors_all = fetched[0][3][0, :, :vector_rows].T.astype(jnp.float32)
    global_params = vectors_all[global_rows:]
    blocks = [
        (
            fetched[layer_id][0],
            fetched[layer_id][1][0],
            fetched[layer_id][2][0],
            vectors_all[layer_id * param_stride : (layer_id + 1) * param_stride],
        )
        for layer_id in range(layers)
    ]

    columns = jnp.take(embed_table.astype(jnp.bfloat16), token_ids, axis=1)
    embedded = lax.all_to_all(
        columns, ("dp", "seq"), split_axis=1, concat_axis=0, tiled=True
    ).T.astype(jnp.float32)
    stream, norm_pull_zero = jax.vjp(layer_norm, embedded, global_params[0], global_params[1])
    saved_layers = []
    for layer_id in range(layers):
        stream, saved = layer_forward(stream, blocks[layer_id])
        saved_layers.append(saved)
    normed, norm_pull_last = jax.vjp(layer_norm, stream, global_params[2], global_params[3])
    dp_count = lax.axis_size("dp")
    features, vocab_own = head_table.shape
    vocab_part = -(-vocab_own // (dp_count * 128)) * 128
    head_cut = jnp.pad(
        head_table.astype(jnp.bfloat16), ((0, 0), (0, dp_count * vocab_part - vocab_own))
    ).reshape(features, dp_count, vocab_part)
    head_cols = lax.all_to_all(
        head_cut.transpose(1, 0, 2), "dp", split_axis=0, concat_axis=0, tiled=True
    ).reshape(dp_count * features, vocab_part)
    valid = jnp.clip(vocab_own - lax.axis_index("dp") * vocab_part, 0, vocab_part)
    masked = jnp.where(jnp.arange(vocab_part) < valid, 0.0, far_below)[None]
    own_rows = normed.shape[0]
    rows_all = gather_rows([normed[None]], row_portions(own_rows), 10)[0][0]
    all_targets, all_mask = marks_of(fetched[0][4])
    first_column = lax.axis_index("seq") * vocab_own + lax.axis_index("dp") * vocab_part
    local_ids = all_targets - first_column
    local_ids = jnp.where(local_ids < valid, local_ids, -1)
    tile = min(head_tile, total_tokens)
    lifted, stats = head_forward(rows_all, head_cols, masked, local_ids, tile, tile // 4)
    own_log = stats[0] + jnp.log(stats[1])
    log_total = exchange_everywhere(own_log.reshape(-1, 128), add_logs, 13).reshape(-1)
    counted = all_mask.astype(jnp.float32)
    picked_part = jnp.sum(counted * stats[2])
    weight_rows = counted / total_tokens
    factors = jnp.pad(
        jnp.stack(
            [
                jnp.exp(stats[0] - log_total) * weight_rows,
                (jnp.exp(stats[2] - log_total) - 1.0) * weight_rows,
            ]
        ),
        ((0, 6), (0, 0)),
    )
    if on_box():
        d_normed, grad_head, head_squares = head_backward_scattered(
            lifted, rows_all, head_cols, local_ids, factors, 11
        )
    else:
        d_rows, grad_head, head_squares = head_backward(
            lifted, rows_all, head_cols, local_ids, factors, tile, tile // 2
        )
        d_normed = scatter_plain([d_rows[None]])[0][0]
    g_head = lax.all_to_all(
        grad_head.reshape(dp_count, features, vocab_part), "dp", split_axis=0, concat_axis=0, tiled=True
    )
    d_stream, d_gain_last, d_bias_last = norm_pull_last(d_normed)
    layer_grads = [None] * layers
    vector_grads = [None] * layers
    later_squares = []
    d_embedded = d_stream
    for layer_id in reversed(range(layers)):
        d_stream, grads = layer_backward(d_stream, saved_layers[layer_id], blocks[layer_id])
        vector_grads[layer_id] = grads[3]
        low_grads = [
            grads[0].astype(jnp.bfloat16),
            grads[1].astype(jnp.bfloat16)[None],
            grads[2].astype(jnp.bfloat16)[None],
        ]
        if layer_id == 0:
            d_embedded, d_gain_zero, d_bias_zero = norm_pull_zero(d_stream)
            all_vectors = jnp.concatenate(
                vector_grads
                + [jnp.stack([d_gain_zero, d_bias_zero, d_gain_last, d_bias_last])],
                axis=0,
            )
            low_grads.append(as_rows(all_vectors).astype(jnp.bfloat16))
        if layer_id > 0:
            layer_grads[layer_id] = scatter_joined(low_grads[0][:joined], *low_grads[1:])
            later_squares.append(low_grads[0][joined:])
    low_grads, g_head = lax.optimization_barrier((low_grads, g_head))
    summed = scatter_rows(
        low_grads + later_squares,
        gradient_portions(square_own, expand_own, shrink_own),
        layers,
    )
    layer_grads[0] = summed[:4]
    for layer_id, square_sum in zip(reversed(range(1, layers)), summed[4:]):
        layer_grads[layer_id][0] = jnp.concatenate([layer_grads[layer_id][0], square_sum])
    back_columns = lax.all_to_all(
        d_embedded.T.astype(jnp.bfloat16), ("dp", "seq"), split_axis=0, concat_axis=1, tiled=True
    )
    g_embed, embed_squares = embed_gradient(
        back_columns, token_ids, embed_table.shape[1], min(embed_block, total_tokens)
    )
    g_square = jnp.stack([layer_grads[layer_id][0] for layer_id in range(layers)])
    g_expand = jnp.concatenate([layer_grads[layer_id][1] for layer_id in range(layers)])
    g_shrink = jnp.concatenate([layer_grads[layer_id][2] for layer_id in range(layers)])
    g_vector = layer_grads[0][3][0, :, :vector_rows].T
    gradients = (g_square, g_expand, g_shrink, g_vector, g_embed, g_head)
    square_part = jnp.sum(embed_squares) + jnp.sum(head_squares)
    for gradient in gradients[:4]:
        square_part = square_part + jnp.sum(gradient * gradient)
    parts = jnp.stack([square_part, picked_part])
    parts = exchange_everywhere(jnp.broadcast_to(jnp.pad(parts, (0, 6))[:, None], (8, 128)), jnp.add, 12)
    square_sum = parts[0, 0]
    loss_sum = jnp.sum(counted * log_total) - parts[1, 0]
    grad_norm = jnp.sqrt(square_sum)
    scale = jnp.minimum(1.0, 0.5 / math.sqrt(total_tokens) / (grad_norm + 1e-06))
    weights = (
        square_weights,
        expand_weights,
        shrink_weights,
        vector_params,
        embed_table,
        head_table,
    )
    firsts = (square_first, expand_first, shrink_first, vector_first, embed_first, head_first)
    seconds = (
        square_second,
        expand_second,
        shrink_second,
        vector_second,
        embed_second,
        head_second,
    )
    updated = [
        adam_update(
            weights[slot],
            gradients[slot] * scale,
            firsts[slot],
            seconds[slot],
            LEARN_RATES[slot],
            DECAY_FLAGS[slot],
        )
        for slot in range(5)
    ]
    updated.append(adam_columns(head_table, g_head, head_first, head_second, scale, 5))
    return (
        loss_sum,
        grad_norm,
        updated[0][0],
        updated[1][0],
        updated[2][0],
        updated[3][0],
        updated[4][0],
        updated[5][0],
        updated[0][1],
        updated[1][1],
        updated[2][1],
        updated[3][1],
        updated[4][1],
        updated[5][1],
        updated[0][2],
        updated[1][2],
        updated[2][2],
        updated[3][2],
        updated[4][2],
        updated[5][2],
    )


def solution(mesh):
    placed = (
        P(),
        P("dp"),
        P("dp"),
        P(None, None, ("dp", "seq"), None),
        P(None, ("dp", "seq"), None),
        P(None, ("dp", "seq"), None),
        P(None, ("dp", "seq")),
        P(("dp", "seq"), None),
        P("dp", "seq"),
        P(None, None, ("dp", "seq"), None),
        P(None, ("dp", "seq"), None),
        P(None, ("dp", "seq"), None),
        P(None, ("dp", "seq")),
        P(("dp", "seq"), None),
        P("dp", "seq"),
        P(None, None, ("dp", "seq"), None),
        P(None, ("dp", "seq"), None),
        P(None, ("dp", "seq"), None),
        P(None, ("dp", "seq")),
        P(("dp", "seq"), None),
        P("dp", "seq"),
    )
    return jax.shard_map(
        per_device,
        mesh=mesh,
        in_specs=placed,
        out_specs=(
            P(),
            P(),
            P(None, None, ("dp", "seq"), None),
            P(None, ("dp", "seq"), None),
            P(None, ("dp", "seq"), None),
            P(None, ("dp", "seq")),
            P(("dp", "seq"), None),
            P("dp", "seq"),
            P(None, None, ("dp", "seq"), None),
            P(None, ("dp", "seq"), None),
            P(None, ("dp", "seq"), None),
            P(None, ("dp", "seq")),
            P(("dp", "seq"), None),
            P("dp", "seq"),
            P(None, None, ("dp", "seq"), None),
            P(None, ("dp", "seq"), None),
            P(None, ("dp", "seq"), None),
            P(None, ("dp", "seq")),
            P(("dp", "seq"), None),
            P("dp", "seq"),
        ),
        check_vma=False,
    )
```
